256 devices in a mesh: ctx: 64 (over z, y, core), head: 4 (over x).
Axes of the slice: x: 4, y: 4, z: 8, core: 2. Of those that a mesh axis runs over, the one named last changes fastest.
Arguments:
- queries: float32 [8192, 2048], P('ctx', 'head'), may hold values from -800 to 800
- key_vectors: float32 [8192, 2048], P('ctx', 'head'), may hold values from -800 to 800
- values: float32 [8192, 2048], P('ctx', 'head'), may hold values from -6 to 6
- write_rates: float32 [16, 8192], P('head', 'ctx'), may hold values from 0 to 0.95
- log_decay: float32 [16, 8192], P('head', 'ctx'), may hold values from -2 to 0
- level_gates: float32 [8, 16, 8192], P(None, 'head', 'ctx'), may hold values from 0.25 to 4
- out_weight: bfloat16 [2048, 2048], P('head'), may hold values from -0.125 to 0.125
- out_cotangent: bfloat16 [8192, 2048], P('ctx', 'head'), may hold values from -6 to 6
- final_cotangent: float32 [16, 128, 128], P('head'), may hold values from -6 to 6
Outputs:
- mixed: bfloat16 [8192, 2048], P('ctx', 'head')
- grad_queries: float32 [8192, 2048], P('ctx', 'head')
- grad_keys: float32 [8192, 2048], P('ctx', 'head')
- grad_values: float32 [8192, 2048], P('ctx', 'head')
- grad_rates: float32 [16, 8192], P('head', 'ctx')
- grad_decay: float32 [16, 8192], P('head', 'ctx')
- grad_gates: float32 [8, 16, 8192], P(None, 'head', 'ctx')
- grad_weight: float32 [2048, 2048], P(('head', 'ctx'))
- final_state: float32 [16, 128, 128], P('head')
The draws below stay inside these ranges and needn't reach their ends.
All inputs are finite; a program needn't handle non-finite values.
Results may differ from the reference program's by a relative error of at most 0.0049.
Values may be sent and summed in bfloat16 or wider, within the bound.
A program may use at most 128 MiB of HBM per device.

```python
import math
import jax
import jax.numpy as jnp
from jax import lax

D = 2048
HEADS = 16
HEAD_DIM = 128
SPAN = 64
TOK_DEV = 128
TOKENS = 8192
LEVELS = 8


def head_kinds(key, slow_share):
    chooser = jax.random.uniform(jax.random.fold_in(key, 77), (HEADS, 1))
    return chooser < slow_share


def scaled_field(key):
    subkeys = jax.random.split(key, 4)
    noise_base = jnp.clip(jax.random.normal(subkeys[0], (TOKENS, D)), -4.0, 4.0)
    row_scale = jnp.exp(jax.random.uniform(subkeys[2], (TOKENS, 1), minval=0.0, maxval=math.log(10.0)))
    col_scale = jnp.exp(jax.random.uniform(subkeys[3], (1, D), minval=0.0, maxval=math.log(10.0)))
    return noise_base * row_scale * col_scale


def draw_queries(key, part):
    key = jax.random.fold_in(key, 1)
    return scaled_field(key)


def draw_key_vectors(key, part):
    key = jax.random.fold_in(key, 2)
    return scaled_field(key)


def draw_write_rates(key, part):
    slow_heads = head_kinds(key, 0.55)
    key = jax.random.fold_in(key, 3)
    subkeys = jax.random.split(key, 3)
    slow_rate = jnp.exp(jax.random.uniform(subkeys[0], (HEADS, 1), minval=math.log(0.2), maxval=0.0)) * HEAD_DIM / TOKENS
    fast_rate = jnp.exp(jax.random.uniform(subkeys[1], (HEADS, 1), minval=math.log(0.05), maxval=math.log(0.9)))
    roughness = jax.random.uniform(subkeys[2], (HEADS, TOKENS), minval=0.5, maxval=1.5)
    return jnp.minimum(jnp.where(slow_heads, slow_rate, fast_rate) * roughness, 0.95)


def draw_log_decay(key, part):
    slow_heads = head_kinds(key, 0.55)
    key = jax.random.fold_in(key, 5)
    subkeys = jax.random.split(key, 6)
    slow_rate = jnp.exp(jax.random.uniform(subkeys[0], (HEADS, 1), minval=math.log(0.05), maxval=math.log(0.5))) / TOKENS
    fast_rate = jnp.exp(jax.random.uniform(subkeys[1], (HEADS, 1), minval=math.log(1.0 / 50.0), maxval=math.log(1.0 / 30.0)))
    rates = jnp.where(slow_heads, slow_rate, fast_rate)
    block_count = TOKENS // TOK_DEV
    device_factor = jnp.exp(jax.random.uniform(subkeys[2], (HEADS, block_count, 1), minval=math.log(0.5), maxval=math.log(2.0)))
    roughness = jax.random.uniform(subkeys[3], (HEADS, block_count, TOK_DEV), minval=0.5, maxval=1.5)
    equilibrium_memory = (rates[:, :, None] * device_factor * roughness).reshape(HEADS, TOKENS)
    element_slots = jax.random.randint(subkeys[4], (HEADS, 2, 1), 0, TOKENS)
    measured_items = jax.random.uniform(subkeys[5], (HEADS, 2, 1), minval=0.22, maxval=0.69)
    element_offsets = jnp.arange(TOKENS)[None, None, :]
    element_groups = jnp.sum(jnp.where(element_offsets == element_slots, measured_items, 0.0), axis=1)
    return -equilibrium_memory - element_groups


def block_levels(own_key, dims, pieces, least, high):
    factor_of = 1.0
    for axis_at, parts in pieces:
        heights = jax.random.uniform(jax.random.fold_in(jax.random.fold_in(own_key, 6), axis_at), (parts,), jnp.float32, least / len(pieces), high / len(pieces))
        factor_of = factor_of * jnp.repeat(jnp.exp(heights), dims[axis_at] // parts).reshape((-1,) + (1,) * (len(dims) - 1 - axis_at))
    return factor_of


def noise(stream_key, extent, scale, limit, cuts=(), kind=jnp.bfloat16):
    values = jax.random.normal(stream_key, extent, jnp.float32) * scale
    if len(cuts) > 0:
        values = block_levels(stream_key, extent, cuts, -0.22, 0.18) * values
    return jnp.clip(values, min=-limit, max=limit).astype(kind)


def setup_inputs(seed: int = 0) -> dict:
    splits = jax.random.split(jax.random.key(seed), 10)
    queries = draw_queries(jax.random.fold_in(splits[9], 71), 0)
    key_vectors = draw_key_vectors(jax.random.fold_in(splits[9], 71), 0)
    values = noise(splits[2], (TOKENS, D), 1.0, 6.0, ((0, 64), (1, 4)), jnp.float32)
    write_rates = draw_write_rates(jax.random.fold_in(splits[9], 71), 0)
    log_decay = draw_log_decay(jax.random.fold_in(splits[9], 71), 0)
    level_gates = jnp.clip(jnp.exp(math.log(4.0) - 2.7725887 * jax.random.uniform(splits[5], (LEVELS, HEADS, TOKENS), jnp.float32) ** block_levels(splits[5], (LEVELS, HEADS, TOKENS), ((1, 4), (2, 64)), -0.2, 0.2)), 0.25, 4.0)
    out_weight = noise(splits[6], (D, D), D ** -0.5, 0.125, ((0, 4),))
    out_cotangent = noise(splits[7], (TOKENS, D), 1.0, 6.0, ((0, 64), (1, 4)))
    final_cotangent = noise(splits[8], (HEADS, HEAD_DIM, HEAD_DIM), 1.0, 6.0, ((0, 4),), jnp.float32)
    return {"queries": queries, "key_vectors": key_vectors, "values": values, "write_rates": write_rates, "log_decay": log_decay, "level_gates": level_gates, "out_weight": out_weight, "out_cotangent": out_cotangent, "final_cotangent": final_cotangent}


finest = lax.Precision.HIGHEST

def unit_rows(vectors):
    return vectors * lax.rsqrt(lax.optimization_barrier(jnp.sum(vectors * vectors, axis=-1, keepdims=True)) + 1e-06)

def span_terms(query_in, key_in, value_in, beta_in, forgetting_rates_given):
    span_len = query_in.shape[-2]
    cumulative = jnp.cumsum(forgetting_rates_given, axis=-1)
    row_ids = jnp.arange(span_len)
    causal = row_ids[:, None] >= row_ids[None, :]
    strict = row_ids[:, None] > row_ids[None, :]
    gap_log = jnp.where(causal, cumulative[..., :, None] - cumulative[..., None, :], 0.0)
    decay_mat = jnp.where(causal, jnp.exp(gap_log), 0.0)
    key_gram = jnp.einsum('...td,...sd->...ts', key_in, key_in, precision=finest)
    lower_part = jnp.where(strict, beta_in[..., :, None] * decay_mat * key_gram, 0.0)
    system = lower_part + jnp.eye(span_len, dtype=jnp.float32)
    gamma_all = jnp.exp(cumulative)
    right_side = jnp.concatenate([beta_in[..., None] * value_in, (beta_in * gamma_all)[..., None] * key_in], axis=-1)
    solved = lax.linalg.triangular_solve(system, right_side, left_side=True, lower=True, unit_diagonal=True)
    plain_vals = solved[..., :HEAD_DIM]
    weights = solved[..., HEAD_DIM:]
    scores = jnp.einsum('...td,...sd->...ts', query_in, key_in, precision=finest) * decay_mat
    reader = gamma_all[..., None] * query_in - jnp.einsum('...ts,...sd->...td', scores, weights, precision=finest)
    own_term = jnp.einsum('...ts,...sd->...td', scores, plain_vals, precision=finest)
    tail_keys = jnp.exp(cumulative[..., -1:] - cumulative)[..., None] * key_in
    identity = jnp.eye(HEAD_DIM, dtype=jnp.float32)
    span_maps = jnp.exp(cumulative[..., -1])[..., None, None] * identity - jnp.einsum('...si,...sj->...ij', tail_keys, weights, precision=finest)
    added = jnp.einsum('...si,...sj->...ij', tail_keys, plain_vals, precision=finest)
    return (own_term, reader, span_maps, added)

def head_forward(query_in, key_in, value_in, beta_in, forgetting_rates_given, gate_rows):
    span_count = query_in.shape[0] // SPAN
    span_shape = (span_count, SPAN, HEAD_DIM)
    own_term, reader, span_maps, added = span_terms(unit_rows(query_in).reshape(span_shape), unit_rows(key_in).reshape(span_shape), value_in.reshape(span_shape), beta_in.reshape(span_count, SPAN), forgetting_rates_given.reshape(span_count, SPAN))
    gate_blocks = gate_rows.reshape(LEVELS, span_count, SPAN)
    level_count = LEVELS - 1
    level_ids = jnp.arange(level_count, dtype=jnp.int32)

    def advance(carry, inputs):
        levels, running = carry
        span_id, span_reader, span_map, span_add, span_gate = inputs
        readout = jnp.einsum('td,lde->lte', span_reader, levels, precision=finest)
        level_out = lax.optimization_barrier(jnp.sum(span_gate[1:, :, None] * readout, axis=0))
        moved = jnp.einsum('ij,ljk->lik', span_map, levels, precision=finest)
        flipped = jnp.bitwise_xor(span_id, span_id + 1)
        top_level = jnp.sum(jnp.right_shift(flipped, level_ids + 1) & 1)
        merged = lax.optimization_barrier(jnp.sum(jnp.where((level_ids <= top_level)[:, None, None], moved, 0.0), axis=0)) + span_add
        levels = jnp.where((level_ids > top_level)[:, None, None], moved, 0.0) + jnp.where((level_ids == top_level)[:, None, None], merged[None], 0.0)
        running = jnp.einsum('ij,jk->ik', span_map, running, precision=finest) + span_add
        return ((levels, running), level_out)
    initial = (jnp.zeros((level_count, HEAD_DIM, HEAD_DIM), jnp.float32), jnp.zeros((HEAD_DIM, HEAD_DIM), jnp.float32))
    inputs = (jnp.arange(span_count, dtype=jnp.int32), reader, span_maps, added, jnp.swapaxes(gate_blocks, 0, 1))
    (_, carried), level_outs = lax.scan(jax.checkpoint(advance), initial, inputs)
    head_out = (gate_blocks[0][..., None] * own_term + level_outs).reshape(query_in.shape[0], HEAD_DIM)
    return (head_out, carried)

def reference(queries, key_vectors, values, write_rates, log_decay, level_gates, out_weight, out_cotangent, final_cotangent):
    tokens = queries.shape[0]

    def per_head(matrix):
        return matrix.reshape(tokens, HEADS, HEAD_DIM).transpose(1, 0, 2)

    def join_heads(matrix):
        return matrix.transpose(1, 0, 2).reshape(tokens, D)
    heads_grad = jnp.dot(out_cotangent.astype(jnp.float32), out_weight.T.astype(jnp.float32), preferred_element_type=jnp.float32)

    def single_head(inputs):
        query_in, key_in, value_in, beta_in, forgetting_rates_given, gate_rows, cotangent, carried_cot = inputs
        (head_out, carried), vector_jacobian = jax.vjp(head_forward, query_in, key_in, value_in, beta_in, forgetting_rates_given, gate_rows)
        return (head_out, carried) + vector_jacobian((cotangent, carried_cot))
    results = lax.map(single_head, (per_head(queries), per_head(key_vectors), per_head(values), write_rates, log_decay, jnp.swapaxes(level_gates, 0, 1), per_head(heads_grad), final_cotangent))
    head_outs, final_state, grad_query, grad_key, grad_value, grad_rate, forgetting_derivative, grad_gate = results
    heads_low = join_heads(head_outs).astype(jnp.bfloat16)
    mixed = jnp.dot(heads_low.astype(jnp.float32), out_weight.astype(jnp.float32), preferred_element_type=jnp.float32).astype(jnp.bfloat16)
    grad_weight = jnp.dot(heads_low.T.astype(jnp.float32), out_cotangent.astype(jnp.float32), preferred_element_type=jnp.float32)
    return (mixed, join_heads(grad_query), join_heads(grad_key), join_heads(grad_value), grad_rate, forgetting_derivative, jnp.swapaxes(grad_gate, 0, 1), grad_weight, final_state)
```

```python
import functools

import jax
import jax.numpy as jnp
from jax import lax
from jax.experimental import pallas as pl
from jax.experimental.pallas import tpu as pltpu
from jax.sharding import PartitionSpec as P

F32 = jnp.float32
BF16 = jnp.bfloat16
C = 128
NZ, NY, NB, NL = 8, 4, 4, 8
MESH = pl.DeviceIdType.MESH


def split(x):
    high = x.astype(BF16)
    return high, (x - high.astype(F32)).astype(BF16)


def dot(a, b, ca=1, cb=0, precision=None):
    return lax.dot_general(
        a, b, (((ca,), (cb,)), ((), ())), preferred_element_type=F32, precision=precision
    )


def mm(a, b, ca=1, cb=0):
    return mm_split(split(a), split(b), ca, cb)


def mm_split(a, b, ca=1, cb=0):
    (ah, al), (bh, bl) = a, b
    return dot(
        jnp.concatenate([ah, ah, al], axis=ca), jnp.concatenate([bh, bl, bh], axis=cb), ca, cb
    )


def iotas():
    return (
        lax.broadcasted_iota(jnp.int32, (C, C), 0),
        lax.broadcasted_iota(jnp.int32, (C, C), 1),
    )


def unit(x):
    scale = lax.rsqrt(jnp.sum(x * x, axis=1, keepdims=True) + 1e-6)
    return x * scale, scale


def unit_back(grad, vec, scale):
    return scale * (grad - vec * jnp.sum(vec * grad, axis=1, keepdims=True))


def token_terms(rows):
    row, col = iotas()
    upper = jnp.where(row <= col, 1.0, 0.0).astype(F32)
    cum = dot(rows, upper, precision=lax.Precision.HIGHEST)
    stacked = jnp.concatenate([rows, cum, jnp.zeros((C - 32, C), F32)], axis=0).T
    beta = stacked[:, 0:1]
    cum_col = stacked[:, 17:18]
    cum_row = cum[1:2, :]
    last = cum[1:2, C - 1 : C]
    decay = jnp.where(row >= col, jnp.exp(jnp.minimum(cum_col - cum_row, 0.0)), 0.0)
    return dict(
        beta=beta,
        gam=jnp.exp(cum_col),
        tail=jnp.exp(last - cum_col),
        glast=jnp.exp(last),
        gates=[stacked[:, 2 + i : 3 + i] for i in range(NL)],
        decay=decay,
    )


def inverses(lows):
    row, col = iotas()
    eye = jnp.where(row == col, 1.0, 0.0).astype(F32)
    invs = [eye - jnp.where((row >> 1) == (col >> 1), low, 0.0) for low in lows]
    for bit in range(1, 7):
        here = ((row >> (bit + 1)) == (col >> (bit + 1))) & ((row >> bit) != (col >> bit))
        parts = [mm(jnp.where(here, low, 0.0), inv) for low, inv in zip(lows, invs)]
        invs = [inv - mm(inv, part) for inv, part in zip(invs, parts)]
    return invs


def gate_matrix(tt):
    row, col = iotas()
    return jnp.where((row >> 6) == (col >> 6), tt["gates"][0], tt["gates"][1])


def lockstep(runs):
    results = [None] * len(runs)
    alive = list(range(len(runs)))
    while alive:
        for i in list(alive):
            try:
                next(runs[i])
            except StopIteration as stop:
                results[i] = stop.value
                alive.remove(i)
    return results


def chunk_forward(keys, queries, values, inv, tt):
    beta, gam, decay = tt["beta"], tt["gam"], tt["decay"]
    row, col = iotas()
    kb = beta * gam * keys
    vb = beta * values
    scores = mm(queries, keys, 1, 1) * decay
    yield
    pair = mm(inv, jnp.concatenate([kb, vb], axis=1))
    yield
    mix = mm(scores, inv)
    yield
    both = mm(tt["tail"] * keys, pair, 0, 0)
    yield
    reader = gam * queries - mm(mix, kb)
    yield
    near = mm(mix * gate_matrix(tt), vb)
    yield
    return dict(
        scores=scores, mix=mix, weights=pair[:, :C], plain=pair[:, C:], reader=reader, near=near,
        map=jnp.where(row == col, tt["glast"], 0.0) - both[:, :C], add=both[:, C:],
    )


def near_back(hg, values, mix, tt):
    row, col = iotas()
    gate = gate_matrix(tt)
    cross = mm(hg, tt["beta"] * values, 1, 1)
    yield
    d_vb = mm(mix * gate, hg, 0, 0)
    yield
    gated = cross * mix
    same = (row >> 6) == (col >> 6)
    d_g0 = jnp.sum(jnp.where(same, gated, 0.0), axis=1, keepdims=True)
    d_g1 = jnp.sum(jnp.where(same, 0.0, gated), axis=1, keepdims=True)
    return dict(d_g0=d_g0, d_g1=d_g1, dvb=d_vb, dmix=cross * gate)


def chunk_back_a(d_mix, d_reader, keys, queries, inv, scores, mix, tt, q_scale):
    gam, decay = tt["gam"], tt["decay"]
    row, col = iotas()
    d_mix = d_mix - mm(d_reader, tt["beta"] * gam * keys, 1, 1)
    yield
    d_kb = -mm(mix, d_reader, 0, 0)
    yield
    d_scores = jnp.where(row >= col, mm(d_mix, inv, 1, 1), 0.0)
    yield
    d_qk = d_scores * decay
    d_query = mm(d_qk, keys) + gam * d_reader
    yield
    d_low = mm(mix, d_scores, 0, 0)
    yield
    d_key = mm(d_qk, queries, 0, 0)
    yield
    cum = gam * jnp.sum(d_reader * queries, axis=1, keepdims=True)
    return dict(
        dkb=d_kb, dlow=d_low, dkey=d_key, gap=d_scores * scores, cum=cum,
        query=unit_back(d_query, queries, q_scale),
    )


def chunk_back_b(d_map, d_add, keys, inv, weights, plain, d_vb, d_kb, tt):
    grads = jnp.concatenate([d_add, -d_map], axis=1)
    d_pw = mm(tt["tail"] * keys, grads)
    yield
    d_kt = mm(jnp.concatenate([plain, weights], axis=1), grads, 1, 1)
    yield
    back = mm(inv, d_pw, 0, 0)
    yield
    d_vb = d_vb + back[:, :C]
    return dict(dvb=d_vb, dkb=d_kb + back[:, C:], dkt=d_kt, back=back, value=tt["beta"] * d_vb)


def chunk_back_c(
    d_map, d_vb, d_kb, d_kt, back, d_low, d_key, gap, cum, gram, keys, values, weights, plain, tt,
    k_scale, gate_grads,
):
    beta, gam, tail, decay = tt["beta"], tt["gam"], tt["tail"], tt["decay"]
    row, col = iotas()
    d_low = d_low + mm(back, jnp.concatenate([plain, weights], axis=1), 1, 1)
    yield
    d_low = jnp.where(row > col, -d_low, 0.0) * decay
    d_gram = beta * d_low
    d_key = d_key + mm(d_gram + d_gram.T, keys) + beta * gam * d_kb + tail * d_kt
    yield
    dk_gram = d_low * gram
    d_gap = gap + beta * dk_gram
    kb_k = jnp.sum(d_kb * keys, axis=1, keepdims=True)
    d_beta = jnp.sum(dk_gram + d_vb * values, axis=1, keepdims=True) + gam * kb_k
    tail_part = tail * jnp.sum(d_kt * keys, axis=1, keepdims=True)
    d_cum = cum + gam * beta * kb_k - tail_part + jnp.sum(d_gap, axis=1, keepdims=True)
    d_last = jnp.sum(tail_part, axis=0, keepdims=True) + tt["glast"] * jnp.sum(
        jnp.sum(jnp.where(row == col, d_map, 0.0), axis=1, keepdims=True), axis=0, keepdims=True
    )
    lane = lax.broadcasted_iota(jnp.int32, (1, C), 1)
    d_cum_row = jnp.where(lane == C - 1, d_last, 0.0) - jnp.sum(d_gap, axis=0, keepdims=True)
    cols = jnp.where(col == 0, d_beta, 0.0) + jnp.where(col == 1, d_cum, 0.0)
    for i in range(NL):
        cols = cols + jnp.where(col == 2 + i, gate_grads[i], 0.0)
    rows = cols.T[:16, :]
    at = lax.broadcasted_iota(jnp.int32, (16, C), 0)
    rows = rows + jnp.where(at == 1, d_cum_row, 0.0)
    lower = jnp.where(row >= col, 1.0, 0.0).astype(F32)
    rows = jnp.where(at == 1, dot(rows, lower, precision=lax.Precision.HIGHEST), rows)
    return unit_back(d_key, keys, k_scale), rows


def chunk_chain(maps, adds):
    one = jnp.concatenate([maps[0], adds[0]], axis=1)
    two = mm(maps[1], one)
    run2 = two[:, C:] + adds[1]
    three = mm(maps[2], jnp.concatenate([two[:, :C], run2], axis=1))
    moved = three[:, C:]
    run3 = moved + adds[2]
    four = mm(maps[3], jnp.concatenate([three[:, :C], run3], axis=1))
    return [two[:, :C], three[:, :C], four[:, :C]], run2, moved, run3, four[:, C:] + adds[3]


def chain_back(d_total, d_run4, maps, add0, pre2, pre3, run2, run3, lift_grads, near):
    pair = jnp.concatenate([d_total, d_run4], axis=1)
    d_map3 = mm(pair, jnp.concatenate([pre3, run3], axis=1), 1, 1)
    d_add3 = d_run4
    down = mm(maps[3], pair, 0, 0)
    d_pre3 = down[:, :C] + lift_grads[2]
    d_run3 = down[:, C:]
    d_add2 = d_run3 + near["add2"]
    pair = jnp.concatenate([d_pre3, d_run3 + near["moved"]], axis=1)
    d_map2 = mm(pair, jnp.concatenate([pre2, run2], axis=1), 1, 1)
    down = mm(maps[2], pair, 0, 0)
    d_pre2 = down[:, :C] + lift_grads[1]
    d_run2 = down[:, C:] + near["run2"]
    pair = jnp.concatenate([d_pre2, d_run2], axis=1)
    d_map1 = mm(pair, jnp.concatenate([maps[0], add0], axis=1), 1, 1)
    down = mm(maps[1], pair, 0, 0)
    d_map0 = down[:, :C] + lift_grads[0]
    d_add0 = down[:, C:] + near["add0"]
    return [d_map0, d_map1, d_map2, d_map3], [d_add0, d_run2, d_add2, d_add3]


def kernel(
    k_ref, q_ref, v_ref, rate_ref, decay_ref, gate_ref, w_ref, cot_ref, fcot_ref,
    mixed_ref, dq_ref, dk_ref, dv_ref, dsmall_ref, gw_ref, fin_ref,
    kin, qin, vin, sin, spack, hgin, cot, hg, hl, hlout, gout, sout, res,
    own, peer, mz, az, zst, dxo, dxp, dsc, dsz, lam,
    gpart, gpeer, ysend, yrecv, zsend, zrecv, mpart, mrecv,
    in_send, in_recv, out_send, out_recv, x_send, x_recv, loc, core_send, core_recv,
    zf_send, zf_recv, rel_send, rel_recv, zb_send, zb_recv, relb_send, relb_recv,
    gy_send, gy_recv, gz_send, gz_recv, f_send, f_recv,
):
    me = lax.axis_index("ctx")
    x = lax.axis_index("head")
    z, y, c = me // 8, (me // 2) % 4, me % 2
    pending = []

    def at(zz, yy, cc):
        return {"ctx": (zz * 4 + yy) * 2 + cc}

    def remote(src, dst, send, recv, target):
        return pltpu.make_async_remote_copy(
            src_ref=src, dst_ref=dst, send_sem=send, recv_sem=recv,
            device_id=target, device_id_type=MESH,
        )

    def put(src, dst, send, recv, target, here=None, when=None):
        copy = remote(src, dst, send, recv, target)
        cond = when
        if here is not None:
            cond = jnp.logical_not(here)

            @pl.when(here)
            def _():
                pltpu.make_async_copy(src, dst, recv).start()

        if cond is None:
            copy.start()
            pending.append(copy.wait_send)
        else:

            @pl.when(cond)
            def _():
                copy.start()

            def finish():
                @pl.when(cond)
                def _():
                    copy.wait_send()

            pending.append(finish)

    def got(dst, sem):
        pltpu.make_async_copy(dst, dst, sem).wait()

    def head_cols(i):
        return pl.ds(pl.multiple_of(i * C, C), C)

    for h in range(NY):
        one = slice(h, h + 1)
        spack[h] = jnp.concatenate(
            [rate_ref[one], decay_ref[one]]
            + [gate_ref[i, one] for i in range(NL)]
            + [jnp.zeros((6, C), F32)],
            axis=0,
        )

    barrier = pltpu.get_barrier_semaphore()
    for dy in range(NY):
        for dc in range(2):
            if dy or dc:
                pl.semaphore_signal(
                    barrier, inc=1, device_id=at(z, (y + dy) % NY, (c + dc) % 2), device_id_type=MESH
                )
    for dz in range(1, NZ):
        pl.semaphore_signal(barrier, inc=1, device_id=at((z + dz) % NZ, y, c), device_id_type=MESH)
    for dx in range(1, 4):
        pl.semaphore_signal(barrier, inc=1, device_id={"head": (x + dx) % 4}, device_id_type=MESH)
    pl.semaphore_wait(barrier, 17)

    slot = (y % 2) * 2 + c
    half = y // 2

    def spread(idx, src_of, dst):
        for d in range(NY):
            h = (y + d) % NY
            put(
                src_of(h), dst.at[slot], in_send.at[idx, d], in_recv.at[idx, slot],
                at(z, h, half), here=(c == half) if d == 0 else None,
            )

    def spread_got(idx, dst):
        for b in range(NB):
            got(dst.at[b], in_recv.at[idx, b])

    def gather_back(idx, src, dst_of):
        for b in range(NB):
            ty, tc = 2 * c + b // 2, b % 2
            put(
                src.at[b], dst_of(y), out_send.at[idx, b], out_recv.at[idx, y],
                at(z, ty, tc), here=(ty == y) & (tc == c),
            )

    def gather_got(idx, dst_of):
        for h in range(NY):
            got(dst_of(h), out_recv.at[idx, h])

    spread(0, lambda h: k_ref.at[:, head_cols(h)], kin)
    spread(1, lambda h: spack.at[h], sin)
    cot_cols = pl.ds(pl.multiple_of(x * 512, 512), 512)
    for d in range(1, 4):
        put(
            cot_ref, cot.at[:, cot_cols], x_send.at[0, d - 1], x_recv.at[0, d - 1],
            {"head": (x + d) % 4},
        )
    local_cot = pltpu.make_async_copy(cot_ref, cot.at[:, cot_cols], loc.at[0])
    local_cot.start()
    spread(2, lambda h: q_ref.at[:, head_cols(h)], qin)
    spread(3, lambda h: v_ref.at[:, head_cols(h)], vin)

    names = [
        "keys", "queries", "inv", "gram", "scores", "mix", "weights", "plain", "reader", "near",
        "map", "add", "lift", "dread", "dvb", "dmix", "dkb", "dlow", "dkey", "gap",
    ]

    def load(name, b):
        return res[names.index(name), b]

    def store(name, b, value):
        res[names.index(name), b] = value

    row, col = iotas()
    blocks = range(NB)

    spread_got(0, kin)
    spread_got(1, sin)
    terms = [token_terms(sin[b]) for b in blocks]
    lows, k_scales = [], []
    for b in blocks:
        keys, scale = unit(kin[b])
        k_scales.append(scale)
        store("keys", b, keys)
        gram = mm(keys, keys, 1, 1)
        store("gram", b, gram)
        lows.append(jnp.where(row > col, terms[b]["beta"] * terms[b]["decay"] * gram, 0.0))
    for b, inv in enumerate(inverses(lows)):
        store("inv", b, inv)

    local_cot.wait()
    for d in range(1, 4):
        src_x = (x + 4 - d) % 4
        got(cot.at[:, pl.ds(pl.multiple_of(src_x * 512, 512), 512)], x_recv.at[0, d - 1])
    hg[...] = dot(cot[...], w_ref[...], 1, 1)
    spread(4, lambda h: hg.at[:, head_cols(h)], hgin)

    spread_got(2, qin)
    spread_got(3, vin)
    q_scales = []
    for b in blocks:
        queries, scale = unit(qin[b])
        q_scales.append(scale)
        store("queries", b, queries)
    outs = lockstep(
        [
            chunk_forward(load("keys", b), load("queries", b), vin[b], load("inv", b), terms[b])
            for b in blocks
        ]
    )
    for b in blocks:
        for name in outs[b]:
            store(name, b, outs[b][name])
    maps = [load("map", b) for b in blocks]
    adds = [load("add", b) for b in blocks]
    pres, run2, moved, run3, run4 = chunk_chain(maps, adds)
    own[0] = pres[2]
    own[1] = run4
    other = at(z, y, 1 - c)
    put(own, peer, core_send.at[0], core_recv.at[0], other)
    store("lift", 0, load("reader", 0))
    for b in (1, 2, 3):
        store("lift", b, mm(load("reader", b), maps[0] if b == 1 else pres[b - 2]))
    for b, state, gate in ((1, adds[0], 2), (2, run2, 3), (3, adds[2], 2), (3, moved, 3)):
        store(
            "near", b,
            load("near", b) + terms[b]["gates"][gate] * mm(load("reader", b), state),
        )

    got(peer, core_recv.at[0])
    first = c == 0
    lo_map = jnp.where(first, own[0], peer[0])
    lo_add = jnp.where(first, own[1], peer[1])
    hi_map = jnp.where(first, peer[0], own[0])
    hi_add = jnp.where(first, peer[1], own[1])
    both = mm(hi_map, jnp.concatenate([lo_map, lo_add], axis=1))
    chip_map, chip_add = both[:, :C], both[:, C:] + hi_add
    high = chip_map.astype(BF16)
    rest = jnp.sum(
        jnp.where(row == col, chip_map - high.astype(F32), 0.0), axis=0, keepdims=True
    )
    mz[z, :C] = high
    mz[z, C:] = jnp.broadcast_to(rest, (16, C)).astype(BF16)
    az[z] = chip_add.astype(BF16)

    def map_parts(j):
        rest = jnp.broadcast_to(mz[j, C:].astype(F32)[:1], (C, C))
        return mz[j, :C], jnp.where(row == col, rest, 0.0).astype(BF16)

    second = c == 1
    for d in range(NZ - 1, 0, -1):
        tz = z + d
        up = tz < NZ
        put(mz.at[z], mz.at[z], zf_send.at[d], zf_recv.at[z], at(tz % NZ, y, c), when=up & first)
        put(az.at[z], az.at[z], zf_send.at[NZ + d], zf_recv.at[z], at(tz % NZ, y, c), when=up & second)
    for d in range(1, NZ):
        tz = z - d
        put(
            mz.at[z], mz.at[z], zf_send.at[2 * NZ + d], zf_recv.at[z], at((tz + NZ) % NZ, y, c),
            when=(tz >= 0) & first,
        )
    spread_got(4, hgin)
    outs = lockstep([near_back(hgin[b], vin[b], load("mix", b), terms[b]) for b in blocks])
    gate_grads = []
    for b in blocks:
        store("dvb", b, outs[b]["dvb"])
        store("dmix", b, outs[b]["dmix"])
        gate_grads.append([outs[b]["d_g0"], outs[b]["d_g1"]] + [jnp.zeros((C, 1), F32)] * 6)
    near_reads = [jnp.zeros((C, C), F32)] * NB
    near_cots = {}
    for b, state, gate, name in (
        (1, adds[0], 2, "add0"), (2, run2, 3, "run2"), (3, adds[2], 2, "add2"), (3, moved, 3, "moved"),
    ):
        weight = terms[b]["gates"][gate]
        part = mm(hgin[b], state, 1, 1)
        reader = load("reader", b)
        gate_grads[b][gate] = jnp.sum(part * reader, axis=1, keepdims=True)
        near_reads[b] = near_reads[b] + weight * part
        near_cots[name] = mm(reader, weight * hgin[b], 0, 0)
    for b in blocks:
        store("dread", b, near_reads[b])

    for j in range(NZ - 1):

        @pl.when((j < z) & first)
        def _():
            got(mz.at[j], zf_recv.at[j])

        @pl.when((j < z) & second)
        def _():
            got(az.at[j], zf_recv.at[j])

        put(mz.at[j], mz.at[j], rel_send.at[j], rel_recv.at[j], other, when=(j < z) & first)
        put(az.at[j], az.at[j], rel_send.at[NZ + j], rel_recv.at[j], other, when=(j < z) & second)

    zst[...] = jnp.zeros_like(zst)
    starts = [(z // (2 << b)) * (2 << b) for b in range(3)]

    def step(j, carry):
        @pl.when(first)
        def _():
            got(az.at[j], rel_recv.at[j])

        @pl.when(second)
        def _():
            got(mz.at[j], rel_recv.at[j])

        new = mm_split(map_parts(j), split(zst[...]))
        add = az[j].astype(F32)
        for b in range(3):
            inside = (j >= starts[b]) & (j < starts[b] + (1 << b))
            zst[:, b * C : (b + 1) * C] = new[:, b * C : (b + 1) * C] + jnp.where(inside, add, 0.0)
        return carry

    lax.fori_loop(0, z, step, 0)
    bits = [(z // (1 << b)) % 2 == 1 for b in range(3)]
    reads = [jnp.where(bits[b], zst[:, b * C : (b + 1) * C], 0.0) for b in range(3)]
    chip_states = jnp.concatenate(reads, axis=1)
    run_chip = reads[0] + reads[1] + reads[2]

    lower = mm(lo_map, chip_states)
    states = jnp.concatenate(
        [jnp.where(first, 0.0, lo_add), jnp.where(first, chip_states, lower)], axis=1
    )
    for b in blocks:
        reads_b = mm(load("lift", b), states)
        total = load("near", b)
        for i in range(4):
            total = total + terms[b]["gates"][4 + i] * reads_b[:, i * C : (i + 1) * C]
        hlout[b] = total.astype(BF16)
    gather_back(0, hlout, lambda h: hl.at[:, head_cols(h)])

    last = z == NZ - 1

    @pl.when(last)
    def _():
        fin_ref[y] = mm(chip_map, run_chip) + chip_add

    for d in range(1, NZ):
        put(
            fin_ref.at[y], fin_ref.at[y], f_send.at[d], f_recv.at[0],
            at(NZ - 1 - d, y, c), when=last,
        )

    d_states = jnp.zeros((C, 4 * C), F32)
    for b in blocks:
        weighted = jnp.concatenate([terms[b]["gates"][4 + i] * hgin[b] for i in range(4)], axis=1)
        d_states = d_states + mm(load("lift", b), weighted, 0, 0)
    dxo[...] = d_states
    put(dxo, dxp, core_send.at[1], core_recv.at[1], other)
    prefixes = [None, maps[0], pres[0], pres[1]]
    state_rows = jnp.concatenate([states[:, i * C : (i + 1) * C] for i in range(4)], axis=0)
    lift_grads = []
    backs = [mm(hgin[b], state_rows, 1, 1) for b in blocks]
    for b in blocks:
        lift = load("lift", b)
        d_lift = jnp.zeros((C, C), F32)
        for i in range(4):
            part = backs[b][:, i * C : (i + 1) * C]
            gate_grads[b][4 + i] = jnp.sum(part * lift, axis=1, keepdims=True)
            d_lift = d_lift + terms[b]["gates"][4 + i] * part
        if b:
            store("dread", b, load("dread", b) + mm(d_lift, prefixes[b], 1, 1))
            lift_grads.append(mm(load("reader", b), d_lift, 0, 0))
        else:
            store("dread", b, d_lift)

    got(dxp, core_recv.at[1])
    lo_dx = jnp.where(first, dxo[...], dxp[...])
    hi_dx = jnp.where(first, dxp[...], dxo[...])
    d_chip = lo_dx[:, C:] + mm(lo_map, hi_dx[:, C:], 0, 0)
    for b in range(3):
        dsc[b] = d_chip[:, b * C : (b + 1) * C].astype(BF16)
    rows_mine = pl.ds(pl.multiple_of(c * 64, 64), 64)
    rows_other = pl.ds(pl.multiple_of((1 - c) * 64, 64), 64)
    for b in (2, 1, 0):
        for d in range((2 << b) - 1, 0, -1):
            tz = z - d
            put(
                dsc.at[b, rows_mine], dsz.at[z, b, rows_mine], zb_send.at[b, d],
                zb_recv.at[z, b], at((tz + NZ) % NZ, y, c), when=bits[b] & (tz >= starts[b]),
            )

    gather_got(0, lambda h: hl.at[:, head_cols(h)])
    mpart[...] = dot(hl[...], w_ref[...])
    for d in range(1, 4):
        tx = (x + d) % 4
        put(
            mpart.at[:, pl.ds(pl.multiple_of(tx * 512, 512), 512)], mrecv.at[d - 1],
            x_send.at[1, d - 1], x_recv.at[1, d - 1], {"head": tx},
        )

    def weight_rows(i, carry):
        cols = hl[:, pl.ds(pl.multiple_of(i * C, C), C)]
        part = dot(cols, cot[...], 0, 0)
        gpart[pl.ds(i * 8, 8)] = part.reshape(8, 2, 8, 2048)
        return carry

    lax.fori_loop(0, 4, weight_rows, 0)
    put(gpart.at[:, 1 - c], gpeer, core_send.at[2], core_recv.at[2], other)

    outs = lockstep(
        [
            chunk_back_a(
                load("dmix", b), load("dread", b), load("keys", b), load("queries", b),
                load("inv", b), load("scores", b), load("mix", b), terms[b], q_scales[b],
            )
            for b in blocks
        ]
    )
    cums = [outs[b]["cum"] for b in blocks]
    for b in blocks:
        gout[0, b] = outs[b]["query"].astype(BF16)
        for name in ("dkb", "dlow", "dkey", "gap"):
            store(name, b, outs[b][name])
    targets = (dq_ref, dk_ref, dv_ref)

    def send_back(i):
        gather_back(1 + i, gout.at[i], lambda h: targets[i].at[:, head_cols(h)])

    send_back(0)

    got(gpeer, core_recv.at[2])

    def chip_rows(i, carry):
        for yy in range(NY):
            parts = [gpart[8 * i + 4 * k + yy, c] + gpeer[8 * i + 4 * k + yy] for k in range(2)]
            ysend[yy, pl.ds(pl.multiple_of(16 * i, 16), 16)] = jnp.concatenate(
                parts, axis=0
            ).astype(BF16)
        return carry

    lax.fori_loop(0, 4, chip_rows, 0)
    for d in range(1, NY):
        ty = (y + d) % NY
        put(ysend.at[ty], yrecv.at[d - 1], gy_send.at[d - 1], gy_recv.at[d - 1], at(z, ty, c))

    for i in range(NZ - 1, 0, -1):
        for b in range(3):
            if not (i >> b) & 1:
                continue
            wanted = (z < i) & (z // (2 << b) == i // (2 << b))

            @pl.when(wanted)
            def _():
                got(dsz.at[i, b, rows_mine], zb_recv.at[i, b])

            put(
                dsz.at[i, b, rows_mine], dsz.at[i, b, rows_mine], relb_send.at[i, b],
                relb_recv.at[i, b], other, when=wanted,
            )

    for i in range(1, NZ):

        @pl.when((i > z) & first)
        def _():
            got(mz.at[i], zf_recv.at[i])

        put(mz.at[i], mz.at[i], rel_send.at[2 * NZ + i], rel_recv.at[i], other, when=(i > z) & first)

        @pl.when((i > z) & second)
        def _():
            got(mz.at[i], rel_recv.at[i])

    lam[...] = jnp.zeros_like(lam)
    lam[:, 3 * C :] = fcot_ref[y]
    for i in range(NZ - 1, 0, -1):

        @pl.when(i > z)
        def _():
            lam[...] = mm_split(map_parts(i), split(lam[...]), 0, 0)

        for b in range(3):
            if not (i >> b) & 1:
                continue

            @pl.when((z < i) & (z // (2 << b) == i // (2 << b)))
            def _():
                got(dsz.at[i, b, rows_other], relb_recv.at[i, b])

            @pl.when((z < i) & (z // (2 << b) == i // (2 << b)))
            def _():
                lam[:, b * C : (b + 1) * C] += dsz[i, b].astype(F32)

    d_chip_map = mm(lam[...], jnp.concatenate([zst[...], run_chip], axis=1), 1, 1)
    d_chip_add = lam[:, 3 * C :]
    for b in range(3):
        d_chip_add = d_chip_add + jnp.where(bits[b], 0.0, lam[:, b * C : (b + 1) * C])
    chip_pair = jnp.concatenate([d_chip_map, d_chip_add], axis=1)
    as_second = mm(chip_pair, jnp.concatenate([lo_map, lo_add], axis=1), 1, 1)
    through = mm(hi_map, chip_pair, 0, 0)
    as_first = through[:, :C] + mm(hi_dx[:, C:], chip_states, 1, 1)
    d_total = jnp.where(first, as_first, as_second)
    d_run4 = jnp.where(first, through[:, C:] + hi_dx[:, :C], d_chip_add)
    d_maps, d_adds = chain_back(
        d_total, d_run4, maps, adds[0], pres[0], pres[1], run2, run3, lift_grads, near_cots
    )

    @pl.when(jnp.logical_not(last))
    def _():
        got(fin_ref.at[y], f_recv.at[0])

    for d in range(1, NY):
        ty = (y + d) % NY
        put(fin_ref.at[y], fin_ref.at[y], f_send.at[NZ + d], f_recv.at[d], at(z, ty, c))

    pairs = lockstep(
        [
            chunk_back_b(
                d_maps[b], d_adds[b], load("keys", b), load("inv", b), load("weights", b),
                load("plain", b), load("dvb", b), load("dkb", b), terms[b],
            )
            for b in blocks
        ]
    )
    for b in blocks:
        gout[2, b] = pairs[b]["value"].astype(BF16)
    send_back(2)

    for d in range(1, NY):
        got(yrecv.at[d - 1], gy_recv.at[d - 1])

    def plane_rows(i, carry):
        at_rows = pl.ds(pl.multiple_of(16 * i, 16), 16)
        total = ysend[y, at_rows].astype(F32)
        for d in range(NY - 1):
            total = total + yrecv[d, at_rows].astype(F32)
        for k in range(2):
            part = total[8 * k : 8 * k + 8]
            zsend[2 * i + k] = jnp.concatenate([part[:, :1024], part[:, 1024:]], axis=0).astype(BF16)
        return carry

    lax.fori_loop(0, 4, plane_rows, 0)
    for d in range(NZ - 1, 0, -1):
        tz = (z + d) % NZ
        put(zsend.at[tz], zrecv.at[d - 1], gz_send.at[d - 1], gz_recv.at[d - 1], at(tz, y, c))

    outs = lockstep(
        [
            chunk_back_c(
                d_maps[b], pairs[b]["dvb"], pairs[b]["dkb"], pairs[b]["dkt"], pairs[b]["back"],
                load("dlow", b), load("dkey", b), load("gap", b), cums[b], load("gram", b),
                load("keys", b), vin[b], load("weights", b), load("plain", b), terms[b],
                k_scales[b], gate_grads[b],
            )
            for b in blocks
        ]
    )
    for b in blocks:
        gout[1, b] = outs[b][0].astype(BF16)
        sout[b] = outs[b][1]
    send_back(1)
    gather_back(4, sout, lambda h: dsmall_ref.at[h])

    total = mpart[:, cot_cols]
    for d in range(1, 4):
        got(mrecv.at[d - 1], x_recv.at[1, d - 1])
    for d in range(3):
        total = total + mrecv[d]
    mixed_ref[...] = total.astype(BF16)

    total = zsend[z].astype(F32)
    for d in range(1, NZ):
        got(zrecv.at[d - 1], gz_recv.at[d - 1])
        total = total + zrecv[d - 1].astype(F32)
    gw_ref[...] = jnp.concatenate([total[:8], total[8:]], axis=1)

    for d in range(1, NY):
        sy = (y + NY - d) % NY
        got(fin_ref.at[sy], f_recv.at[d])
    for i in range(3):
        gather_got(1 + i, lambda h, i=i: targets[i].at[:, head_cols(h)])
    gather_got(4, lambda h: dsmall_ref.at[h])
    for finish in pending:
        finish()


def finish_kernel(*refs):
    ins, small_ref = refs[:6], refs[6]
    outs, (rate_ref, decay_ref, gate_ref) = refs[7:13], refs[13:16]
    for i in range(6):
        outs[i][...] = ins[i][...].astype(outs[i].dtype)
    for h in range(NY):
        one = slice(h, h + 1)
        rate_ref[one] = small_ref[h, 0:1]
        decay_ref[one] = small_ref[h, 1:2]
        for i in range(NL):
            gate_ref[i, one] = small_ref[h, 2 + i : 3 + i]


def on_device(
    queries, key_vectors, values, write_rates, log_decay, level_gates, out_weight,
    out_cotangent, final_cotangent,
):
    vmem = pl.BlockSpec(memory_space=pltpu.VMEM)
    anywhere = pl.BlockSpec(memory_space=pl.ANY)
    sem = pltpu.SemaphoreType.DMA
    quad = pltpu.VMEM((NB, C, C), F32)
    mixed, dq, dk, dv, dsmall, gw, fin = pl.pallas_call(
        kernel,
        out_shape=[
            jax.ShapeDtypeStruct((C, 512), BF16),
            jax.ShapeDtypeStruct((C, 512), BF16),
            jax.ShapeDtypeStruct((C, 512), BF16),
            jax.ShapeDtypeStruct((C, 512), BF16),
            jax.ShapeDtypeStruct((4, 16, C), F32),
            jax.ShapeDtypeStruct((8, 2048), F32),
            jax.ShapeDtypeStruct((4, C, C), F32),
        ],
        in_specs=[anywhere] * 3 + [vmem] * 4 + [anywhere, vmem],
        out_specs=[vmem] + [anywhere] * 4 + [vmem] * 2,
        scratch_shapes=[
            quad, quad, quad, pltpu.VMEM((NB, 16, C), F32), pltpu.VMEM((NY, 16, C), F32), quad,
            pltpu.VMEM((C, 2048), BF16),
            pltpu.VMEM((C, 512), F32),
            pltpu.VMEM((C, 512), BF16),
            pltpu.VMEM((NB, C, C), BF16),
            pltpu.VMEM((3, NB, C, C), BF16),
            pltpu.VMEM((NB, 16, C), F32),
            pltpu.VMEM((20, NB, C, C), F32),
            pltpu.VMEM((2, C, C), F32),
            pltpu.VMEM((2, C, C), F32),
            pltpu.VMEM((NZ, C + 16, C), BF16),
            pltpu.VMEM((NZ, C, C), BF16),
            pltpu.VMEM((C, 3 * C), F32),
            pltpu.VMEM((C, 4 * C), F32),
            pltpu.VMEM((C, 4 * C), F32),
            pltpu.VMEM((3, C, C), BF16),
            pltpu.VMEM((NZ, 3, C, C), BF16),
            pltpu.VMEM((C, 4 * C), F32),
            pltpu.VMEM((32, 2, 8, 2048), F32),
            pltpu.VMEM((32, 8, 2048), F32),
            pltpu.VMEM((NY, 64, 2048), BF16),
            pltpu.VMEM((NY - 1, 64, 2048), BF16),
            pltpu.VMEM((NZ, 16, 1024), BF16),
            pltpu.VMEM((NZ - 1, 16, 1024), BF16),
            pltpu.VMEM((C, 2048), F32),
            pltpu.VMEM((3, C, 512), F32),
            sem((5, 4)), sem((5, 4)), sem((5, 4)), sem((5, 4)),
            sem((2, 3)), sem((2, 3)), sem((1,)), sem((3,)), sem((3,)),
            sem((3 * NZ,)), sem((NZ,)), sem((3 * NZ,)), sem((NZ,)),
            sem((3, NZ)), sem((NZ, 3)), sem((NZ, 3)), sem((NZ, 3)),
            sem((NY - 1,)), sem((NY - 1,)), sem((NZ - 1,)), sem((NZ - 1,)),
            sem((NZ + NY,)), sem((NY,)),
        ],
        compiler_params=pltpu.CompilerParams(
            collective_id=0, has_side_effects=True, vmem_limit_bytes=56 * 1024 * 1024
        ),
    )(
        key_vectors, queries, values, write_rates, log_decay, level_gates, out_weight,
        out_cotangent, final_cotangent,
    )
    whole = (mixed, dq, dk, dv, gw, fin)
    out = pl.pallas_call(
        finish_kernel,
        out_shape=[
            jax.ShapeDtypeStruct(part.shape, F32 if i else BF16) for i, part in enumerate(whole)
        ]
        + [
            jax.ShapeDtypeStruct((4, C), F32),
            jax.ShapeDtypeStruct((4, C), F32),
            jax.ShapeDtypeStruct((NL, 4, C), F32),
        ],
        in_specs=[vmem] * 7,
        out_specs=[vmem] * 9,
    )(*whole, dsmall)
    mixed, dq, dk, dv, gw, fin, d_rates, d_decay, d_gates = out
    return (mixed, dq, dk, dv, d_rates, d_decay, d_gates, gw, fin)


def solution(mesh):
    return jax.shard_map(
        on_device,
        mesh=mesh,
        in_specs=(
            P("ctx", "head"), P("ctx", "head"), P("ctx", "head"), P("head", "ctx"),
            P("head", "ctx"), P(None, "head", "ctx"), P("head", None), P("ctx", "head"),
            P("head", None, None),
        ),
        out_specs=(
            P("ctx", "head"), P("ctx", "head"), P("ctx", "head"), P("ctx", "head"),
            P("head", "ctx"), P("head", "ctx"), P(None, "head", "ctx"),
            P(("head", "ctx"), None), P("head", None, None),
        ),
        check_vma=False,
    )
```

```python
import functools

import jax
import jax.numpy as jnp
from jax import lax
from jax.experimental import pallas as pl
from jax.experimental.pallas import tpu as pltpu
from jax.sharding import PartitionSpec as P

F32 = jnp.float32
BF16 = jnp.bfloat16
C = 128
NZ, NY, NB, NL = 8, 4, 4, 8
MESH = pl.DeviceIdType.MESH


def split(x):
    high = x.astype(BF16)
    return high, (x - high.astype(F32)).astype(BF16)


def dot(a, b, ca=1, cb=0, precision=None):
    return lax.dot_general(
        a, b, (((ca,), (cb,)), ((), ())), preferred_element_type=F32, precision=precision
    )


def mm(a, b, ca=1, cb=0):
    return mm_split(split(a), split(b), ca, cb)


def mm_split(a, b, ca=1, cb=0):
    (ah, al), (bh, bl) = a, b
    return dot(
        jnp.concatenate([ah, ah, al], axis=ca), jnp.concatenate([bh, bl, bh], axis=cb), ca, cb
    )


def iotas():
    return (
        lax.broadcasted_iota(jnp.int32, (C, C), 0),
        lax.broadcasted_iota(jnp.int32, (C, C), 1),
    )


def unit(x):
    scale = lax.rsqrt(jnp.sum(x * x, axis=1, keepdims=True) + 1e-6)
    return x * scale, scale


def unit_back(grad, vec, scale):
    return scale * (grad - vec * jnp.sum(vec * grad, axis=1, keepdims=True))


def token_terms(rows):
    row, col = iotas()
    upper = jnp.where(row <= col, 1.0, 0.0).astype(F32)
    cum = dot(rows, upper, precision=lax.Precision.HIGHEST)
    stacked = jnp.concatenate([rows, cum, jnp.zeros((C - 32, C), F32)], axis=0).T
    beta = stacked[:, 0:1]
    cum_col = stacked[:, 17:18]
    cum_row = cum[1:2, :]
    last = cum[1:2, C - 1 : C]
    decay = jnp.where(row >= col, jnp.exp(jnp.minimum(cum_col - cum_row, 0.0)), 0.0)
    return dict(
        beta=beta,
        gam=jnp.exp(cum_col),
        tail=jnp.exp(last - cum_col),
        glast=jnp.exp(last),
        gates=[stacked[:, 2 + i : 3 + i] for i in range(NL)],
        decay=decay,
    )


def inverses(lows):
    row, col = iotas()
    eye = jnp.where(row == col, 1.0, 0.0).astype(F32)
    invs = [eye - jnp.where((row >> 1) == (col >> 1), low, 0.0) for low in lows]
    for bit in range(1, 7):
        here = ((row >> (bit + 1)) == (col >> (bit + 1))) & ((row >> bit) != (col >> bit))
        parts = [mm(jnp.where(here, low, 0.0), inv) for low, inv in zip(lows, invs)]
        invs = [inv - mm(inv, part) for inv, part in zip(invs, parts)]
    return invs


def gate_matrix(tt):
    row, col = iotas()
    return jnp.where((row >> 6) == (col >> 6), tt["gates"][0], tt["gates"][1])


def lockstep(runs):
    results = [None] * len(runs)
    alive = list(range(len(runs)))
    while alive:
        for i in list(alive):
            try:
                next(runs[i])
            except StopIteration as stop:
                results[i] = stop.value
                alive.remove(i)
    return results


def chunk_forward(keys, queries, values, inv, tt):
    beta, gam, decay = tt["beta"], tt["gam"], tt["decay"]
    row, col = iotas()
    kb = beta * gam * keys
    vb = beta * values
    scores = mm(queries, keys, 1, 1) * decay
    yield
    pair = mm(inv, jnp.concatenate([kb, vb], axis=1))
    yield
    mix = mm(scores, inv)
    yield
    both = mm(tt["tail"] * keys, pair, 0, 0)
    yield
    reader = gam * queries - mm(mix, kb)
    yield
    near = mm(mix * gate_matrix(tt), vb)
    yield
    return dict(
        scores=scores, mix=mix, weights=pair[:, :C], plain=pair[:, C:], reader=reader, near=near,
        map=jnp.where(row == col, tt["glast"], 0.0) - both[:, :C], add=both[:, C:],
    )


def near_back(hg, values, mix, tt):
    row, col = iotas()
    gate = gate_matrix(tt)
    cross = mm(hg, tt["beta"] * values, 1, 1)
    yield
    d_vb = mm(mix * gate, hg, 0, 0)
    yield
    gated = cross * mix
    same = (row >> 6) == (col >> 6)
    d_g0 = jnp.sum(jnp.where(same, gated, 0.0), axis=1, keepdims=True)
    d_g1 = jnp.sum(jnp.where(same, 0.0, gated), axis=1, keepdims=True)
    return dict(d_g0=d_g0, d_g1=d_g1, dvb=d_vb, dmix=cross * gate)


def chunk_back_a(d_mix, d_reader, keys, queries, inv, scores, mix, tt, q_scale):
    gam, decay = tt["gam"], tt["decay"]
    row, col = iotas()
    d_mix = d_mix - mm(d_reader, tt["beta"] * gam * keys, 1, 1)
    yield
    d_kb = -mm(mix, d_reader, 0, 0)
    yield
    d_scores = jnp.where(row >= col, mm(d_mix, inv, 1, 1), 0.0)
    yield
    d_qk = d_scores * decay
    d_query = mm(d_qk, keys) + gam * d_reader
    yield
    d_low = mm(mix, d_scores, 0, 0)
    yield
    d_key = mm(d_qk, queries, 0, 0)
    yield
    cum = gam * jnp.sum(d_reader * queries, axis=1, keepdims=True)
    return dict(
        dkb=d_kb, dlow=d_low, dkey=d_key, gap=d_scores * scores, cum=cum,
        query=unit_back(d_query, queries, q_scale),
    )


def chunk_back_b(d_map, d_add, keys, inv, weights, plain, d_vb, d_kb, tt):
    grads = jnp.concatenate([d_add, -d_map], axis=1)
    d_pw = mm(tt["tail"] * keys, grads)
    yield
    d_kt = mm(jnp.concatenate([plain, weights], axis=1), grads, 1, 1)
    yield
    back = mm(inv, d_pw, 0, 0)
    yield
    d_vb = d_vb + back[:, :C]
    return dict(dvb=d_vb, dkb=d_kb + back[:, C:], dkt=d_kt, back=back, value=tt["beta"] * d_vb)


def chunk_back_c(
    d_map, d_vb, d_kb, d_kt, back, d_low, d_key, gap, cum, gram, keys, values, weights, plain, tt,
    k_scale, gate_grads,
):
    beta, gam, tail, decay = tt["beta"], tt["gam"], tt["tail"], tt["decay"]
    row, col = iotas()
    d_low = d_low + mm(back, jnp.concatenate([plain, weights], axis=1), 1, 1)
    yield
    d_low = jnp.where(row > col, -d_low, 0.0) * decay
    d_gram = beta * d_low
    d_key = d_key + mm(d_gram + d_gram.T, keys) + beta * gam * d_kb + tail * d_kt
    yield
    dk_gram = d_low * gram
    d_gap = gap + beta * dk_gram
    kb_k = jnp.sum(d_kb * keys, axis=1, keepdims=True)
    d_beta = jnp.sum(dk_gram + d_vb * values, axis=1, keepdims=True) + gam * kb_k
    tail_part = tail * jnp.sum(d_kt * keys, axis=1, keepdims=True)
    d_cum = cum + gam * beta * kb_k - tail_part + jnp.sum(d_gap, axis=1, keepdims=True)
    d_last = jnp.sum(tail_part, axis=0, keepdims=True) + tt["glast"] * jnp.sum(
        jnp.sum(jnp.where(row == col, d_map, 0.0), axis=1, keepdims=True), axis=0, keepdims=True
    )
    lane = lax.broadcasted_iota(jnp.int32, (1, C), 1)
    d_cum_row = jnp.where(lane == C - 1, d_last, 0.0) - jnp.sum(d_gap, axis=0, keepdims=True)
    cols = jnp.where(col == 0, d_beta, 0.0) + jnp.where(col == 1, d_cum, 0.0)
    for i in range(NL):
        cols = cols + jnp.where(col == 2 + i, gate_grads[i], 0.0)
    rows = cols.T[:16, :]
    at = lax.broadcasted_iota(jnp.int32, (16, C), 0)
    rows = rows + jnp.where(at == 1, d_cum_row, 0.0)
    lower = jnp.where(row >= col, 1.0, 0.0).astype(F32)
    rows = jnp.where(at == 1, dot(rows, lower, precision=lax.Precision.HIGHEST), rows)
    return unit_back(d_key, keys, k_scale), rows


def chunk_chain(maps, adds):
    one = jnp.concatenate([maps[0], adds[0]], axis=1)
    two = mm(maps[1], one)
    run2 = two[:, C:] + adds[1]
    three = mm(maps[2], jnp.concatenate([two[:, :C], run2], axis=1))
    moved = three[:, C:]
    run3 = moved + adds[2]
    four = mm(maps[3], jnp.concatenate([three[:, :C], run3], axis=1))
    return [two[:, :C], three[:, :C], four[:, :C]], run2, moved, run3, four[:, C:] + adds[3]


def chain_back(d_total, d_run4, maps, add0, pre2, pre3, run2, run3, lift_grads, near):
    pair = jnp.concatenate([d_total, d_run4], axis=1)
    d_map3 = mm(pair, jnp.concatenate([pre3, run3], axis=1), 1, 1)
    d_add3 = d_run4
    down = mm(maps[3], pair, 0, 0)
    d_pre3 = down[:, :C] + lift_grads[2]
    d_run3 = down[:, C:]
    d_add2 = d_run3 + near["add2"]
    pair = jnp.concatenate([d_pre3, d_run3 + near["moved"]], axis=1)
    d_map2 = mm(pair, jnp.concatenate([pre2, run2], axis=1), 1, 1)
    down = mm(maps[2], pair, 0, 0)
    d_pre2 = down[:, :C] + lift_grads[1]
    d_run2 = down[:, C:] + near["run2"]
    pair = jnp.concatenate([d_pre2, d_run2], axis=1)
    d_map1 = mm(pair, jnp.concatenate([maps[0], add0], axis=1), 1, 1)
    down = mm(maps[1], pair, 0, 0)
    d_map0 = down[:, :C] + lift_grads[0]
    d_add0 = down[:, C:] + near["add0"]
    return [d_map0, d_map1, d_map2, d_map3], [d_add0, d_run2, d_add2, d_add3]


def kernel(
    k_ref, q_ref, v_ref, rate_ref, decay_ref, gate_ref, w_ref, cot_ref, fcot_ref,
    mixed_ref, dq_ref, dk_ref, dv_ref, dsmall_ref, gw_ref, fin_ref,
    kin, qin, vin, sin, spack, hgin, cot, hg, hl, hlout, gout, sout, res,
    own, peer, mz, az, zst, dxo, dxp, dsc, dsz, lam,
    cotz, gpart, gpeer, gsum, zsend, zrecv, mown, mpart, mrecv,
    in_send, in_recv, out_send, out_recv, x_send, x_recv, loc, core_send, core_recv,
    zf_send, zf_recv, rel_send, rel_recv, zb_send, zb_recv, relb_send, relb_recv,
    gp_send, gp_recv, gz_send, gz_recv, f_send, f_recv,
):
    me = lax.axis_index("ctx")
    x = lax.axis_index("head")
    z, y, c = me // 8, (me // 2) % 4, me % 2
    pending = []

    def at(zz, yy, cc):
        return {"ctx": (zz * 4 + yy) * 2 + cc}

    def remote(src, dst, send, recv, target):
        return pltpu.make_async_remote_copy(
            src_ref=src, dst_ref=dst, send_sem=send, recv_sem=recv,
            device_id=target, device_id_type=MESH,
        )

    def put(src, dst, send, recv, target, here=None, when=None):
        copy = remote(src, dst, send, recv, target)
        cond = when
        if here is not None:
            cond = jnp.logical_not(here)

            @pl.when(here)
            def _():
                pltpu.make_async_copy(src, dst, recv).start()

        if cond is None:
            copy.start()
            pending.append(copy.wait_send)
        else:

            @pl.when(cond)
            def _():
                copy.start()

            def finish():
                @pl.when(cond)
                def _():
                    copy.wait_send()

            pending.append(finish)

    def got(dst, sem):
        pltpu.make_async_copy(dst, dst, sem).wait()

    def head_cols(i):
        return pl.ds(pl.multiple_of(i * C, C), C)

    for h in range(NY):
        one = slice(h, h + 1)
        spack[h] = jnp.concatenate(
            [rate_ref[one], decay_ref[one]]
            + [gate_ref[i, one] for i in range(NL)]
            + [jnp.zeros((6, C), F32)],
            axis=0,
        )

    barrier = pltpu.get_barrier_semaphore()
    for dy in range(NY):
        for dc in range(2):
            if dy or dc:
                pl.semaphore_signal(
                    barrier, inc=1, device_id=at(z, (y + dy) % NY, (c + dc) % 2), device_id_type=MESH
                )
    for dz in range(1, NZ):
        pl.semaphore_signal(barrier, inc=1, device_id=at((z + dz) % NZ, y, c), device_id_type=MESH)
    for dx in range(1, 4):
        pl.semaphore_signal(barrier, inc=1, device_id={"head": (x + dx) % 4}, device_id_type=MESH)
    rows_from = at((z % 2) * 4 + y, z // 2, c)
    rows_to = at(2 * y + z // 4, z % 4, c)
    rows_stay = rows_to["ctx"] == me

    @pl.when(jnp.logical_not(rows_stay))
    def _():
        pl.semaphore_signal(barrier, inc=1, device_id=rows_from, device_id_type=MESH)

    pl.semaphore_wait(barrier, jnp.where(rows_stay, 17, 18))

    slot = (y % 2) * 2 + c
    half = y // 2

    def spread(idx, src_of, dst):
        for d in range(NY):
            h = (y + d) % NY
            put(
                src_of(h), dst(slot), in_send.at[idx, d], in_recv.at[idx, slot],
                at(z, h, half), here=(c == half) if d == 0 else None,
            )

    def spread_got(idx, dst):
        for b in range(NB):
            got(dst(b), in_recv.at[idx, b])

    cot_cols = pl.ds(pl.multiple_of(x * 512, 512), 512)
    kin_at, qin_at, vin_at = (lambda b: kin.at[b]), (lambda b: qin.at[b]), (lambda b: vin.at[b])
    sin_at, hgin_at = (lambda b: sin.at[b]), (lambda b: hgin.at[b])

    def cotz_at(b):
        return cotz.at[b, :, cot_cols]

    def gather_back(idx, src, dst_of):
        for b in range(NB):
            ty, tc = 2 * c + b // 2, b % 2
            put(
                src.at[b], dst_of(y), out_send.at[idx, b], out_recv.at[idx, y],
                at(z, ty, tc), here=(ty == y) & (tc == c),
            )

    def gather_got(idx, dst_of):
        for h in range(NY):
            got(dst_of(h), out_recv.at[idx, h])

    spread(0, lambda h: k_ref.at[:, head_cols(h)], kin_at)
    spread(1, lambda h: spack.at[h], sin_at)
    for d in range(1, 4):
        put(
            cot_ref, cot.at[:, cot_cols], x_send.at[0, d - 1], x_recv.at[0, d - 1],
            {"head": (x + d) % 4},
        )
    local_cot = pltpu.make_async_copy(cot_ref, cot.at[:, cot_cols], loc.at[0])
    local_cot.start()
    spread(5, lambda h: cot_ref, cotz_at)
    spread(2, lambda h: q_ref.at[:, head_cols(h)], qin_at)
    spread(3, lambda h: v_ref.at[:, head_cols(h)], vin_at)

    names = [
        "keys", "queries", "inv", "gram", "scores", "mix", "weights", "plain", "reader", "near",
        "map", "add", "lift", "dread", "dvb", "dmix", "dkb", "dlow", "dkey", "gap",
    ]

    def load(name, b):
        return res[names.index(name), b]

    def store(name, b, value):
        res[names.index(name), b] = value

    row, col = iotas()
    blocks = range(NB)

    spread_got(0, kin_at)
    spread_got(1, sin_at)
    terms = [token_terms(sin[b]) for b in blocks]
    lows, k_scales = [], []
    for b in blocks:
        keys, scale = unit(kin[b])
        k_scales.append(scale)
        store("keys", b, keys)
        gram = mm(keys, keys, 1, 1)
        store("gram", b, gram)
        lows.append(jnp.where(row > col, terms[b]["beta"] * terms[b]["decay"] * gram, 0.0))
    for b, inv in enumerate(inverses(lows)):
        store("inv", b, inv)

    local_cot.wait()
    for d in range(1, 4):
        src_x = (x + 4 - d) % 4
        got(cot.at[:, pl.ds(pl.multiple_of(src_x * 512, 512), 512)], x_recv.at[0, d - 1])
    hg[...] = dot(cot[...], w_ref[...], 1, 1)
    spread(4, lambda h: hg.at[:, head_cols(h)], hgin_at)

    spread_got(5, cotz_at)
    for d in range(1, 4):
        put(
            cotz.at[:, :, cot_cols], cotz.at[:, :, cot_cols], x_send.at[2, d - 1],
            x_recv.at[2, d - 1], {"head": (x + d) % 4},
        )

    spread_got(2, qin_at)
    spread_got(3, vin_at)
    q_scales = []
    for b in blocks:
        queries, scale = unit(qin[b])
        q_scales.append(scale)
        store("queries", b, queries)
    outs = lockstep(
        [
            chunk_forward(load("keys", b), load("queries", b), vin[b], load("inv", b), terms[b])
            for b in blocks
        ]
    )
    for b in blocks:
        for name in outs[b]:
            store(name, b, outs[b][name])
    maps = [load("map", b) for b in blocks]
    adds = [load("add", b) for b in blocks]
    pres, run2, moved, run3, run4 = chunk_chain(maps, adds)
    own[0] = pres[2]
    own[1] = run4
    other = at(z, y, 1 - c)
    put(own, peer, core_send.at[0], core_recv.at[0], other)
    store("lift", 0, load("reader", 0))
    for b in (1, 2, 3):
        store("lift", b, mm(load("reader", b), maps[0] if b == 1 else pres[b - 2]))
    for b, state, gate in ((1, adds[0], 2), (2, run2, 3), (3, adds[2], 2), (3, moved, 3)):
        store(
            "near", b,
            load("near", b) + terms[b]["gates"][gate] * mm(load("reader", b), state),
        )

    spread_got(4, hgin_at)
    d_states = jnp.zeros((C, 4 * C), F32)
    for b in blocks:
        weighted = jnp.concatenate([terms[b]["gates"][4 + i] * hgin[b] for i in range(4)], axis=1)
        d_states = d_states + mm(load("lift", b), weighted, 0, 0)
    dxo[...] = d_states
    put(dxo, dxp, core_send.at[1], core_recv.at[1], other)

    got(peer, core_recv.at[0])
    first = c == 0
    lo_map = jnp.where(first, own[0], peer[0])
    lo_add = jnp.where(first, own[1], peer[1])
    hi_map = jnp.where(first, peer[0], own[0])
    hi_add = jnp.where(first, peer[1], own[1])
    both = mm(hi_map, jnp.concatenate([lo_map, lo_add], axis=1))
    chip_map, chip_add = both[:, :C], both[:, C:] + hi_add
    high = chip_map.astype(BF16)
    rest = jnp.sum(
        jnp.where(row == col, chip_map - high.astype(F32), 0.0), axis=0, keepdims=True
    )
    mz[z, :C] = high
    mz[z, C:] = jnp.broadcast_to(rest, (16, C)).astype(BF16)
    az[z] = chip_add.astype(BF16)

    def map_parts(j):
        rest = jnp.broadcast_to(mz[j, C:].astype(F32)[:1], (C, C))
        return mz[j, :C], jnp.where(row == col, rest, 0.0).astype(BF16)

    second = c == 1
    for d in range(NZ - 1, 0, -1):
        tz = z + d
        up = tz < NZ
        put(mz.at[z], mz.at[z], zf_send.at[d], zf_recv.at[z], at(tz % NZ, y, c), when=up & first)
        put(az.at[z], az.at[z], zf_send.at[NZ + d], zf_recv.at[z], at(tz % NZ, y, c), when=up & second)
    for d in range(1, NZ):
        tz = z - d
        put(
            mz.at[z], mz.at[z], zf_send.at[2 * NZ + d], zf_recv.at[z], at((tz + NZ) % NZ, y, c),
            when=(tz >= 0) & first,
        )
    bits = [(z // (1 << b)) % 2 == 1 for b in range(3)]
    starts = [(z // (2 << b)) * (2 << b) for b in range(3)]

    got(dxp, core_recv.at[1])
    lo_dx = jnp.where(first, dxo[...], dxp[...])
    hi_dx = jnp.where(first, dxp[...], dxo[...])
    d_chip = lo_dx[:, C:] + mm(lo_map, hi_dx[:, C:], 0, 0)
    for b in range(3):
        dsc[b] = d_chip[:, b * C : (b + 1) * C].astype(BF16)
    rows_mine = pl.ds(pl.multiple_of(c * 64, 64), 64)
    rows_other = pl.ds(pl.multiple_of((1 - c) * 64, 64), 64)
    for b in (2, 1, 0):
        for d in range((2 << b) - 1, 0, -1):
            tz = z - d
            put(
                dsc.at[b, rows_mine], dsz.at[z, b, rows_mine], zb_send.at[b, d],
                zb_recv.at[z, b], at((tz + NZ) % NZ, y, c), when=bits[b] & (tz >= starts[b]),
            )

    outs = lockstep([near_back(hgin[b], vin[b], load("mix", b), terms[b]) for b in blocks])
    gate_grads = []
    for b in blocks:
        store("dvb", b, outs[b]["dvb"])
        store("dmix", b, outs[b]["dmix"])
        gate_grads.append([outs[b]["d_g0"], outs[b]["d_g1"]] + [jnp.zeros((C, 1), F32)] * 6)
    near_reads = [jnp.zeros((C, C), F32)] * NB
    near_cots = {}
    for b, state, gate, name in (
        (1, adds[0], 2, "add0"), (2, run2, 3, "run2"), (3, adds[2], 2, "add2"), (3, moved, 3, "moved"),
    ):
        weight = terms[b]["gates"][gate]
        part = mm(hgin[b], state, 1, 1)
        reader = load("reader", b)
        gate_grads[b][gate] = jnp.sum(part * reader, axis=1, keepdims=True)
        near_reads[b] = near_reads[b] + weight * part
        near_cots[name] = mm(reader, weight * hgin[b], 0, 0)
    for b in blocks:
        store("dread", b, near_reads[b])

    for j in range(NZ - 1):

        @pl.when((j < z) & first)
        def _():
            got(mz.at[j], zf_recv.at[j])

        @pl.when((j < z) & second)
        def _():
            got(az.at[j], zf_recv.at[j])

        put(mz.at[j], mz.at[j], rel_send.at[j], rel_recv.at[j], other, when=(j < z) & first)
        put(az.at[j], az.at[j], rel_send.at[NZ + j], rel_recv.at[j], other, when=(j < z) & second)

    zst[...] = jnp.zeros_like(zst)

    def step(j, carry):
        @pl.when(first)
        def _():
            got(az.at[j], rel_recv.at[j])

        @pl.when(second)
        def _():
            got(mz.at[j], rel_recv.at[j])

        new = mm_split(map_parts(j), split(zst[...]))
        add = az[j].astype(F32)
        for b in range(3):
            inside = (j >= starts[b]) & (j < starts[b] + (1 << b))
            zst[:, b * C : (b + 1) * C] = new[:, b * C : (b + 1) * C] + jnp.where(inside, add, 0.0)
        return carry

    lax.fori_loop(0, z, step, 0)
    for i in range(NZ - 1, 0, -1):
        for b in range(3):
            if not (i >> b) & 1:
                continue
            wanted = (z < i) & (z // (2 << b) == i // (2 << b))

            @pl.when(wanted)
            def _():
                got(dsz.at[i, b, rows_mine], zb_recv.at[i, b])

            put(
                dsz.at[i, b, rows_mine], dsz.at[i, b, rows_mine], relb_send.at[i, b],
                relb_recv.at[i, b], other, when=wanted,
            )

    for i in range(1, NZ):

        @pl.when((i > z) & first)
        def _():
            got(mz.at[i], zf_recv.at[i])

        put(mz.at[i], mz.at[i], rel_send.at[2 * NZ + i], rel_recv.at[i], other, when=(i > z) & first)

        @pl.when((i > z) & second)
        def _():
            got(mz.at[i], rel_recv.at[i])

    lam[...] = jnp.zeros_like(lam)
    lam[:, 3 * C :] = fcot_ref[y]
    for i in range(NZ - 1, 0, -1):

        @pl.when(i > z)
        def _():
            lam[...] = mm_split(map_parts(i), split(lam[...]), 0, 0)

        for b in range(3):
            if not (i >> b) & 1:
                continue

            @pl.when((z < i) & (z // (2 << b) == i // (2 << b)))
            def _():
                got(dsz.at[i, b, rows_other], relb_recv.at[i, b])

            @pl.when((z < i) & (z // (2 << b) == i // (2 << b)))
            def _():
                lam[:, b * C : (b + 1) * C] += dsz[i, b].astype(F32)

    reads = [jnp.where(bits[b], zst[:, b * C : (b + 1) * C], 0.0) for b in range(3)]
    chip_states = jnp.concatenate(reads, axis=1)
    run_chip = reads[0] + reads[1] + reads[2]

    lower = mm(lo_map, chip_states)
    states = jnp.concatenate(
        [jnp.where(first, 0.0, lo_add), jnp.where(first, chip_states, lower)], axis=1
    )
    for b in blocks:
        reads_b = mm(load("lift", b), states)
        total = load("near", b)
        for i in range(4):
            total = total + terms[b]["gates"][4 + i] * reads_b[:, i * C : (i + 1) * C]
        hlout[b] = total.astype(BF16)
    gather_back(0, hlout, lambda h: hl.at[:, head_cols(h)])

    for d in range(1, 4):
        src_x = (x + 4 - d) % 4
        got(
            cotz.at[:, :, pl.ds(pl.multiple_of(src_x * 512, 512), 512)], x_recv.at[2, d - 1]
        )

    def weight_rows(i, carry):
        cols = pl.ds(pl.multiple_of(i * 512, 512), 512)
        part = dot(hlout[...].reshape(512, C), cotz[:, :, cols].reshape(512, 512), 0, 0)
        gpart[:, :, :, cols] = part.reshape(NZ, 2, 8, 512)
        return carry

    lax.fori_loop(0, 4, weight_rows, 0)
    put(gpart.at[:, 1 - c], gpeer, core_send.at[2], core_recv.at[2], other)

    last = z == NZ - 1

    @pl.when(last)
    def _():
        fin_ref[y] = mm(chip_map, run_chip) + chip_add

    for d in range(1, NZ):
        put(
            fin_ref.at[y], fin_ref.at[y], f_send.at[d], f_recv.at[0],
            at(NZ - 1 - d, y, c), when=last,
        )

    prefixes = [None, maps[0], pres[0], pres[1]]
    state_rows = jnp.concatenate([states[:, i * C : (i + 1) * C] for i in range(4)], axis=0)
    lift_grads = []
    backs = [mm(hgin[b], state_rows, 1, 1) for b in blocks]
    for b in blocks:
        lift = load("lift", b)
        d_lift = jnp.zeros((C, C), F32)
        for i in range(4):
            part = backs[b][:, i * C : (i + 1) * C]
            gate_grads[b][4 + i] = jnp.sum(part * lift, axis=1, keepdims=True)
            d_lift = d_lift + terms[b]["gates"][4 + i] * part
        if b:
            store("dread", b, load("dread", b) + mm(d_lift, prefixes[b], 1, 1))
            lift_grads.append(mm(load("reader", b), d_lift, 0, 0))
        else:
            store("dread", b, d_lift)

    gather_got(0, lambda h: hl.at[:, head_cols(h)])
    for d in range(1, 4):
        tx = (x + d) % 4
        mpart[d - 1] = dot(
            hl[...], w_ref[:, pl.ds(pl.multiple_of(tx * 512, 512), 512)]
        ).astype(BF16)
        put(
            mpart.at[d - 1], mrecv.at[d - 1], x_send.at[1, d - 1], x_recv.at[1, d - 1],
            {"head": tx},
        )
    mown[...] = dot(hl[...], w_ref[:, cot_cols])

    got(gpeer, core_recv.at[2])

    def chip_rows(i, carry):
        part = gpart[i, c] + gpeer[i]
        zsend[i] = jnp.concatenate([part[:, :1024], part[:, 1024:]], axis=0).astype(BF16)
        return carry

    lax.fori_loop(0, NZ, chip_rows, 0)
    for d in range(NZ - 1, 0, -1):
        tz = (z + d) % NZ
        put(zsend.at[tz], zrecv.at[d - 1], gz_send.at[d - 1], gz_recv.at[d - 1], at(tz, y, c))

    outs = lockstep(
        [
            chunk_back_a(
                load("dmix", b), load("dread", b), load("keys", b), load("queries", b),
                load("inv", b), load("scores", b), load("mix", b), terms[b], q_scales[b],
            )
            for b in blocks
        ]
    )
    cums = [outs[b]["cum"] for b in blocks]
    for b in blocks:
        gout[0, b] = outs[b]["query"].astype(BF16)
        for name in ("dkb", "dlow", "dkey", "gap"):
            store(name, b, outs[b][name])
    targets = (dq_ref, dk_ref, dv_ref)

    def send_back(i):
        gather_back(1 + i, gout.at[i], lambda h: targets[i].at[:, head_cols(h)])

    send_back(0)

    d_chip_map = mm(lam[...], jnp.concatenate([zst[...], run_chip], axis=1), 1, 1)
    d_chip_add = lam[:, 3 * C :]
    for b in range(3):
        d_chip_add = d_chip_add + jnp.where(bits[b], 0.0, lam[:, b * C : (b + 1) * C])
    chip_pair = jnp.concatenate([d_chip_map, d_chip_add], axis=1)
    as_second = mm(chip_pair, jnp.concatenate([lo_map, lo_add], axis=1), 1, 1)
    through = mm(hi_map, chip_pair, 0, 0)
    as_first = through[:, :C] + mm(hi_dx[:, C:], chip_states, 1, 1)
    d_total = jnp.where(first, as_first, as_second)
    d_run4 = jnp.where(first, through[:, C:] + hi_dx[:, :C], d_chip_add)
    d_maps, d_adds = chain_back(
        d_total, d_run4, maps, adds[0], pres[0], pres[1], run2, run3, lift_grads, near_cots
    )

    @pl.when(jnp.logical_not(last))
    def _():
        got(fin_ref.at[y], f_recv.at[0])

    for d in range(1, NY):
        ty = (y + d) % NY
        put(fin_ref.at[y], fin_ref.at[y], f_send.at[NZ + d], f_recv.at[d], at(z, ty, c))

    pairs = lockstep(
        [
            chunk_back_b(
                d_maps[b], d_adds[b], load("keys", b), load("inv", b), load("weights", b),
                load("plain", b), load("dvb", b), load("dkb", b), terms[b],
            )
            for b in blocks
        ]
    )
    for b in blocks:
        gout[2, b] = pairs[b]["value"].astype(BF16)
    send_back(2)

    total = zsend[z].astype(F32)
    for d in range(1, NZ):
        got(zrecv.at[d - 1], gz_recv.at[d - 1])
        total = total + zrecv[d - 1].astype(F32)
    gsum[...] = jnp.concatenate([total[:8], total[8:]], axis=1)
    put(gsum, gw_ref, gp_send.at[0], gp_recv.at[0], rows_to, here=rows_stay)

    outs = lockstep(
        [
            chunk_back_c(
                d_maps[b], pairs[b]["dvb"], pairs[b]["dkb"], pairs[b]["dkt"], pairs[b]["back"],
                load("dlow", b), load("dkey", b), load("gap", b), cums[b], load("gram", b),
                load("keys", b), vin[b], load("weights", b), load("plain", b), terms[b],
                k_scales[b], gate_grads[b],
            )
            for b in blocks
        ]
    )
    for b in blocks:
        gout[1, b] = outs[b][0].astype(BF16)
        sout[b] = outs[b][1]
    send_back(1)
    gather_back(4, sout, lambda h: dsmall_ref.at[h])

    total = mown[...]
    for d in range(1, 4):
        got(mrecv.at[d - 1], x_recv.at[1, d - 1])
    for d in range(3):
        total = total + mrecv[d].astype(F32)
    mixed_ref[...] = total.astype(BF16)
    got(gw_ref, gp_recv.at[0])

    for d in range(1, NY):
        sy = (y + NY - d) % NY
        got(fin_ref.at[sy], f_recv.at[d])
    for i in range(3):
        gather_got(1 + i, lambda h, i=i: targets[i].at[:, head_cols(h)])
    gather_got(4, lambda h: dsmall_ref.at[h])
    for finish in pending:
        finish()


def finish_kernel(*refs):
    ins, small_ref = refs[:6], refs[6]
    outs, (rate_ref, decay_ref, gate_ref) = refs[7:13], refs[13:16]
    for i in range(6):
        outs[i][...] = ins[i][...].astype(outs[i].dtype)
    for h in range(NY):
        one = slice(h, h + 1)
        rate_ref[one] = small_ref[h, 0:1]
        decay_ref[one] = small_ref[h, 1:2]
        for i in range(NL):
            gate_ref[i, one] = small_ref[h, 2 + i : 3 + i]


def on_device(
    queries, key_vectors, values, write_rates, log_decay, level_gates, out_weight,
    out_cotangent, final_cotangent,
):
    vmem = pl.BlockSpec(memory_space=pltpu.VMEM)
    anywhere = pl.BlockSpec(memory_space=pl.ANY)
    sem = pltpu.SemaphoreType.DMA
    quad = pltpu.VMEM((NB, C, C), F32)
    mixed, dq, dk, dv, dsmall, gw, fin = pl.pallas_call(
        kernel,
        out_shape=[
            jax.ShapeDtypeStruct((C, 512), BF16),
            jax.ShapeDtypeStruct((C, 512), BF16),
            jax.ShapeDtypeStruct((C, 512), BF16),
            jax.ShapeDtypeStruct((C, 512), BF16),
            jax.ShapeDtypeStruct((4, 16, C), F32),
            jax.ShapeDtypeStruct((8, 2048), F32),
            jax.ShapeDtypeStruct((4, C, C), F32),
        ],
        in_specs=[anywhere] * 3 + [vmem] * 4 + [anywhere, vmem],
        out_specs=[vmem] + [anywhere] * 4 + [vmem] * 2,
        scratch_shapes=[
            quad, quad, quad, pltpu.VMEM((NB, 16, C), F32), pltpu.VMEM((NY, 16, C), F32), quad,
            pltpu.VMEM((C, 2048), BF16),
            pltpu.VMEM((C, 512), F32),
            pltpu.VMEM((C, 512), BF16),
            pltpu.VMEM((NB, C, C), BF16),
            pltpu.VMEM((3, NB, C, C), BF16),
            pltpu.VMEM((NB, 16, C), F32),
            pltpu.VMEM((20, NB, C, C), F32),
            pltpu.VMEM((2, C, C), F32),
            pltpu.VMEM((2, C, C), F32),
            pltpu.VMEM((NZ, C + 16, C), BF16),
            pltpu.VMEM((NZ, C, C), BF16),
            pltpu.VMEM((C, 3 * C), F32),
            pltpu.VMEM((C, 4 * C), F32),
            pltpu.VMEM((C, 4 * C), F32),
            pltpu.VMEM((3, C, C), BF16),
            pltpu.VMEM((NZ, 3, C, C), BF16),
            pltpu.VMEM((C, 4 * C), F32),
            pltpu.VMEM((NB, C, 2048), BF16),
            pltpu.VMEM((NZ, 2, 8, 2048), F32),
            pltpu.VMEM((NZ, 8, 2048), F32),
            pltpu.VMEM((8, 2048), F32),
            pltpu.VMEM((NZ, 16, 1024), BF16),
            pltpu.VMEM((NZ - 1, 16, 1024), BF16),
            pltpu.VMEM((C, 512), F32),
            pltpu.VMEM((3, C, 512), BF16),
            pltpu.VMEM((3, C, 512), BF16),
            sem((6, 4)), sem((6, 4)), sem((5, 4)), sem((5, 4)),
            sem((3, 3)), sem((3, 3)), sem((1,)), sem((3,)), sem((3,)),
            sem((3 * NZ,)), sem((NZ,)), sem((3 * NZ,)), sem((NZ,)),
            sem((3, NZ)), sem((NZ, 3)), sem((NZ, 3)), sem((NZ, 3)),
            sem((1,)), sem((1,)), sem((NZ - 1,)), sem((NZ - 1,)),
            sem((NZ + NY,)), sem((NY,)),
        ],
        compiler_params=pltpu.CompilerParams(
            collective_id=0, has_side_effects=True, vmem_limit_bytes=56 * 1024 * 1024
        ),
    )(
        key_vectors, queries, values, write_rates, log_decay, level_gates, out_weight,
        out_cotangent, final_cotangent,
    )
    whole = (mixed, dq, dk, dv, gw, fin)
    out = pl.pallas_call(
        finish_kernel,
        out_shape=[
            jax.ShapeDtypeStruct(part.shape, F32 if i else BF16) for i, part in enumerate(whole)
        ]
        + [
            jax.ShapeDtypeStruct((4, C), F32),
            jax.ShapeDtypeStruct((4, C), F32),
            jax.ShapeDtypeStruct((NL, 4, C), F32),
        ],
        in_specs=[vmem] * 7,
        out_specs=[vmem] * 9,
    )(*whole, dsmall)
    mixed, dq, dk, dv, gw, fin, d_rates, d_decay, d_gates = out
    return (mixed, dq, dk, dv, d_rates, d_decay, d_gates, gw, fin)


def solution(mesh):
    return jax.shard_map(
        on_device,
        mesh=mesh,
        in_specs=(
            P("ctx", "head"), P("ctx", "head"), P("ctx", "head"), P("head", "ctx"),
            P("head", "ctx"), P(None, "head", "ctx"), P("head", None), P("ctx", "head"),
            P("head", None, None),
        ),
        out_specs=(
            P("ctx", "head"), P("ctx", "head"), P("ctx", "head"), P("ctx", "head"),
            P("head", "ctx"), P("head", "ctx"), P(None, "head", "ctx"),
            P(("head", "ctx"), None), P("head", None, None),
        ),
        check_vma=False,
    )
```

```python
import functools

import jax
import jax.numpy as jnp
from jax import lax
from jax.experimental import pallas as pl
from jax.experimental.pallas import tpu as pltpu
from jax.sharding import PartitionSpec as P

F32 = jnp.float32
BF16 = jnp.bfloat16
C = 128
NZ, NY, NB, NL = 8, 4, 4, 8
MESH = pl.DeviceIdType.MESH


def split(x):
    high = x.astype(BF16)
    return high, (x - high.astype(F32)).astype(BF16)


SPLITS = {}


def split_once(x):
    if id(x) not in SPLITS:
        SPLITS[id(x)] = (x, split(x))
    return SPLITS[id(x)][1]


def dot(a, b, ca=1, cb=0, precision=None):
    return lax.dot_general(
        a, b, (((ca,), (cb,)), ((), ())), preferred_element_type=F32, precision=precision
    )


def mm(a, b, ca=1, cb=0):
    return mm_split(split_once(a), split_once(b), ca, cb)


def mm_split(a, b, ca=1, cb=0):
    (ah, al), (bh, bl) = a, b
    return dot(
        jnp.concatenate([ah, ah, al], axis=ca), jnp.concatenate([bh, bl, bh], axis=cb), ca, cb
    )


def iotas():
    return (
        lax.broadcasted_iota(jnp.int32, (C, C), 0),
        lax.broadcasted_iota(jnp.int32, (C, C), 1),
    )


def unit(x):
    scale = lax.rsqrt(jnp.sum(x * x, axis=1, keepdims=True) + 1e-6)
    return x * scale, scale


def unit_back(grad, vec, scale):
    return scale * (grad - vec * jnp.sum(vec * grad, axis=1, keepdims=True))


def token_terms(rows):
    row, col = iotas()
    upper = jnp.where(row <= col, 1.0, 0.0).astype(F32)
    cum = dot(rows, upper, precision=lax.Precision.HIGHEST)
    stacked = jnp.concatenate([rows, cum, jnp.zeros((C - 32, C), F32)], axis=0).T
    beta = stacked[:, 0:1]
    cum_col = stacked[:, 17:18]
    cum_row = cum[1:2, :]
    last = cum[1:2, C - 1 : C]
    decay = jnp.where(row >= col, jnp.exp(jnp.minimum(cum_col - cum_row, 0.0)), 0.0)
    return dict(
        beta=beta,
        gam=jnp.exp(cum_col),
        tail=jnp.exp(last - cum_col),
        glast=jnp.exp(last),
        gates=[stacked[:, 2 + i : 3 + i] for i in range(NL)],
        decay=decay,
    )


def inverses(lows):
    row, col = iotas()
    eye = jnp.where(row == col, 1.0, 0.0).astype(F32)
    invs = [eye - jnp.where((row >> 1) == (col >> 1), low, 0.0) for low in lows]
    for bit in range(1, 7):
        here = ((row >> (bit + 1)) == (col >> (bit + 1))) & ((row >> bit) != (col >> bit))
        parts = [mm(jnp.where(here, low, 0.0), inv) for low, inv in zip(lows, invs)]
        invs = [inv - mm(inv, part) for inv, part in zip(invs, parts)]
    return invs


def gate_matrix(tt):
    row, col = iotas()
    return jnp.where((row >> 6) == (col >> 6), tt["gates"][0], tt["gates"][1])


def lockstep(runs):
    results = [None] * len(runs)
    alive = list(range(len(runs)))
    while alive:
        for i in list(alive):
            try:
                next(runs[i])
            except StopIteration as stop:
                results[i] = stop.value
                alive.remove(i)
    return results


def chunk_forward(keys, queries, values, inv, tt):
    beta, gam, decay = tt["beta"], tt["gam"], tt["decay"]
    row, col = iotas()
    kb = beta * gam * keys
    vb = beta * values
    scores = mm(queries, keys, 1, 1) * decay
    yield
    pair = mm(inv, jnp.concatenate([kb, vb], axis=1))
    yield
    mix = mm(scores, inv)
    yield
    both = mm(tt["tail"] * keys, pair, 0, 0)
    yield
    reader = gam * queries - mm(mix, kb)
    yield
    near = mm(mix * gate_matrix(tt), vb)
    yield
    return dict(
        scores=scores, mix=mix, weights=pair[:, :C], plain=pair[:, C:], reader=reader, near=near,
        map=jnp.where(row == col, tt["glast"], 0.0) - both[:, :C], add=both[:, C:],
    )


def near_back(hg, values, mix, tt):
    row, col = iotas()
    gate = gate_matrix(tt)
    cross = mm(hg, tt["beta"] * values, 1, 1)
    yield
    d_vb = mm(mix * gate, hg, 0, 0)
    yield
    gated = cross * mix
    same = (row >> 6) == (col >> 6)
    d_g0 = jnp.sum(jnp.where(same, gated, 0.0), axis=1, keepdims=True)
    d_g1 = jnp.sum(jnp.where(same, 0.0, gated), axis=1, keepdims=True)
    return dict(d_g0=d_g0, d_g1=d_g1, dvb=d_vb, dmix=cross * gate)


def chunk_back_a(d_mix, d_reader, keys, queries, inv, scores, mix, tt, q_scale):
    gam, decay = tt["gam"], tt["decay"]
    row, col = iotas()
    d_mix = d_mix - mm(d_reader, tt["beta"] * gam * keys, 1, 1)
    yield
    d_kb = -mm(mix, d_reader, 0, 0)
    yield
    d_scores = jnp.where(row >= col, mm(d_mix, inv, 1, 1), 0.0)
    yield
    d_qk = d_scores * decay
    d_query = mm(d_qk, keys) + gam * d_reader
    yield
    d_low = mm(mix, d_scores, 0, 0)
    yield
    d_key = mm(d_qk, queries, 0, 0)
    yield
    cum = gam * jnp.sum(d_reader * queries, axis=1, keepdims=True)
    return dict(
        dkb=d_kb, dlow=d_low, dkey=d_key, gap=d_scores * scores, cum=cum,
        query=unit_back(d_query, queries, q_scale),
    )


def chunk_back_b(d_map, d_add, keys, inv, weights, plain, d_vb, d_kb, tt):
    grads = jnp.concatenate([d_add, -d_map], axis=1)
    d_pw = mm(tt["tail"] * keys, grads)
    yield
    d_kt = mm(jnp.concatenate([plain, weights], axis=1), grads, 1, 1)
    yield
    back = mm(inv, d_pw, 0, 0)
    yield
    d_vb = d_vb + back[:, :C]
    return dict(dvb=d_vb, dkb=d_kb + back[:, C:], dkt=d_kt, back=back, value=tt["beta"] * d_vb)


def chunk_back_c(
    d_map, d_vb, d_kb, d_kt, back, d_low, d_key, gap, cum, gram, keys, values, weights, plain, tt,
    k_scale, gate_grads,
):
    beta, gam, tail, decay = tt["beta"], tt["gam"], tt["tail"], tt["decay"]
    row, col = iotas()
    d_low = d_low + mm(back, jnp.concatenate([plain, weights], axis=1), 1, 1)
    yield
    d_low = jnp.where(row > col, -d_low, 0.0) * decay
    d_gram = beta * d_low
    d_key = d_key + mm(d_gram + d_gram.T, keys) + beta * gam * d_kb + tail * d_kt
    yield
    dk_gram = d_low * gram
    d_gap = gap + beta * dk_gram
    kb_k = jnp.sum(d_kb * keys, axis=1, keepdims=True)
    d_beta = jnp.sum(dk_gram + d_vb * values, axis=1, keepdims=True) + gam * kb_k
    tail_part = tail * jnp.sum(d_kt * keys, axis=1, keepdims=True)
    d_cum = cum + gam * beta * kb_k - tail_part + jnp.sum(d_gap, axis=1, keepdims=True)
    d_last = jnp.sum(tail_part, axis=0, keepdims=True) + tt["glast"] * jnp.sum(
        jnp.sum(jnp.where(row == col, d_map, 0.0), axis=1, keepdims=True), axis=0, keepdims=True
    )
    lane = lax.broadcasted_iota(jnp.int32, (1, C), 1)
    d_cum_row = jnp.where(lane == C - 1, d_last, 0.0) - jnp.sum(d_gap, axis=0, keepdims=True)
    cols = jnp.where(col == 0, d_beta, 0.0) + jnp.where(col == 1, d_cum, 0.0)
    for i in range(NL):
        cols = cols + jnp.where(col == 2 + i, gate_grads[i], 0.0)
    rows = cols.T[:16, :]
    at = lax.broadcasted_iota(jnp.int32, (16, C), 0)
    rows = rows + jnp.where(at == 1, d_cum_row, 0.0)
    lower = jnp.where(row >= col, 1.0, 0.0).astype(F32)
    rows = jnp.where(at == 1, dot(rows, lower, precision=lax.Precision.HIGHEST), rows)
    return unit_back(d_key, keys, k_scale), rows


def chunk_chain(maps, adds):
    one = jnp.concatenate([maps[0], adds[0]], axis=1)
    two = mm(maps[1], one)
    run2 = two[:, C:] + adds[1]
    three = mm(maps[2], jnp.concatenate([two[:, :C], run2], axis=1))
    moved = three[:, C:]
    run3 = moved + adds[2]
    four = mm(maps[3], jnp.concatenate([three[:, :C], run3], axis=1))
    return [two[:, :C], three[:, :C], four[:, :C]], run2, moved, run3, four[:, C:] + adds[3]


def chain_back(d_total, d_run4, maps, add0, pre2, pre3, run2, run3, lift_grads, near):
    pair = jnp.concatenate([d_total, d_run4], axis=1)
    d_map3 = mm(pair, jnp.concatenate([pre3, run3], axis=1), 1, 1)
    d_add3 = d_run4
    down = mm(maps[3], pair, 0, 0)
    d_pre3 = down[:, :C] + lift_grads[2]
    d_run3 = down[:, C:]
    d_add2 = d_run3 + near["add2"]
    pair = jnp.concatenate([d_pre3, d_run3 + near["moved"]], axis=1)
    d_map2 = mm(pair, jnp.concatenate([pre2, run2], axis=1), 1, 1)
    down = mm(maps[2], pair, 0, 0)
    d_pre2 = down[:, :C] + lift_grads[1]
    d_run2 = down[:, C:] + near["run2"]
    pair = jnp.concatenate([d_pre2, d_run2], axis=1)
    d_map1 = mm(pair, jnp.concatenate([maps[0], add0], axis=1), 1, 1)
    down = mm(maps[1], pair, 0, 0)
    d_map0 = down[:, :C] + lift_grads[0]
    d_add0 = down[:, C:] + near["add0"]
    return [d_map0, d_map1, d_map2, d_map3], [d_add0, d_run2, d_add2, d_add3]


def kernel(
    k_ref, q_ref, v_ref, rate_ref, decay_ref, gate_ref, w_ref, cot_ref, fcot_ref,
    mixed_ref, dq_ref, dk_ref, dv_ref, dsmall_ref, gw_ref, fin_ref,
    kin, qin, vin, sin, spack, hgin, cot, hg, hl, hlout, gout, sout, wbuf, fcbuf,
    own, peer, mz, az, zst, dxo, dxp, dsc, dsz, lam,
    cotz, gpart, gpeer, gsum, zsend, zrecv, mown, mpart, mrecv,
    in_send, in_recv, out_send, out_recv, x_send, x_recv, loc, core_send, core_recv,
    zf_send, zf_recv, rel_send, rel_recv, zb_send, zb_recv, relb_send, relb_recv,
    gp_send, gp_recv, gz_send, gz_recv, f_send, f_recv,
):
    SPLITS.clear()
    me = lax.axis_index("ctx")
    x = lax.axis_index("head")
    z, y, c = me // 8, (me // 2) % 4, me % 2
    pending = []

    def flush(count):
        for finish in pending[:count]:
            finish()
        del pending[:count]


    def at(zz, yy, cc):
        return {"ctx": (zz * 4 + yy) * 2 + cc}

    def remote(src, dst, send, recv, target):
        return pltpu.make_async_remote_copy(
            src_ref=src, dst_ref=dst, send_sem=send, recv_sem=recv,
            device_id=target, device_id_type=MESH,
        )

    def put(src, dst, send, recv, target, here=None, when=None):
        copy = remote(src, dst, send, recv, target)
        cond = when
        if here is not None:
            cond = jnp.logical_not(here)

            @pl.when(here)
            def _():
                pltpu.make_async_copy(src, dst, recv).start()

        if cond is None:
            copy.start()
            pending.append(copy.wait_send)
        else:

            @pl.when(cond)
            def _():
                copy.start()

            def finish():
                @pl.when(cond)
                def _():
                    copy.wait_send()

            pending.append(finish)

    def got(dst, sem):
        pltpu.make_async_copy(dst, dst, sem).wait()

    def head_cols(i):
        return pl.ds(pl.multiple_of(i * C, C), C)

    local_w = pltpu.make_async_copy(w_ref, wbuf, loc.at[1])
    local_w.start()
    local_fc = pltpu.make_async_copy(fcot_ref.at[y], fcbuf, loc.at[2])
    local_fc.start()
    for h in range(NY):
        one = slice(h, h + 1)
        spack[h] = jnp.concatenate(
            [rate_ref[one], decay_ref[one]]
            + [gate_ref[i, one] for i in range(NL)]
            + [jnp.zeros((6, C), F32)],
            axis=0,
        )

    barrier = pltpu.get_barrier_semaphore()
    for dy in range(NY):
        for dc in range(2):
            if dy or dc:
                pl.semaphore_signal(
                    barrier, inc=1, device_id=at(z, (y + dy) % NY, (c + dc) % 2), device_id_type=MESH
                )
    for dz in range(1, NZ):
        pl.semaphore_signal(barrier, inc=1, device_id=at((z + dz) % NZ, y, c), device_id_type=MESH)
    for dx in range(1, 4):
        pl.semaphore_signal(barrier, inc=1, device_id={"head": (x + dx) % 4}, device_id_type=MESH)
    rows_from = at((z % 2) * 4 + y, z // 2, c)
    rows_to = at(2 * y + z // 4, z % 4, c)
    rows_stay = rows_to["ctx"] == me

    @pl.when(jnp.logical_not(rows_stay))
    def _():
        pl.semaphore_signal(barrier, inc=1, device_id=rows_from, device_id_type=MESH)

    pl.semaphore_wait(barrier, jnp.where(rows_stay, 17, 18))

    slot = (y % 2) * 2 + c
    half = y // 2

    def spread(idx, src_of, dst):
        for d in range(NY):
            h = (y + d) % NY
            put(
                src_of(h), dst(slot), in_send.at[idx, d], in_recv.at[idx, slot],
                at(z, h, half), here=(c == half) if d == 0 else None,
            )

    def spread_got(idx, dst):
        for b in range(NB):
            got(dst(b), in_recv.at[idx, b])

    cot_cols = pl.ds(pl.multiple_of(x * 512, 512), 512)
    kin_at, qin_at, vin_at = (lambda b: kin.at[b]), (lambda b: qin.at[b]), (lambda b: vin.at[b])
    sin_at, hgin_at = (lambda b: sin.at[b]), (lambda b: hgin.at[b])

    def cotz_at(b):
        return cotz.at[b, x, :, :256]

    def cotz_rest(b):
        return cotz.at[b, :, :, 256:]

    def gather_back(idx, src, dst_of):
        for b in range(NB):
            ty, tc = 2 * c + b // 2, b % 2
            put(
                src.at[b], dst_of(y), out_send.at[idx, b], out_recv.at[idx, y],
                at(z, ty, tc), here=(ty == y) & (tc == c),
            )

    def gather_got(idx, dst_of):
        for h in range(NY):
            got(dst_of(h), out_recv.at[idx, h])

    spread(0, lambda h: k_ref.at[:, head_cols(h)], kin_at)
    spread(1, lambda h: spack.at[h], sin_at)
    for d in range(1, 4):
        put(
            cot_ref, cot.at[x], x_send.at[0, d - 1], x_recv.at[0, d - 1], {"head": (x + d) % 4},
        )
    local_cot = pltpu.make_async_copy(cot_ref, cot.at[x], loc.at[0])
    local_cot.start()

    held = {}

    def load(name, b):
        return held[name, b]

    def store(name, b, value):
        held[name, b] = value

    row, col = iotas()
    blocks = range(NB)

    spread_got(0, kin_at)
    spread_got(1, sin_at)
    spread(2, lambda h: q_ref.at[:, head_cols(h)], qin_at)
    spread(3, lambda h: v_ref.at[:, head_cols(h)], vin_at)
    terms = [token_terms(sin[b]) for b in blocks]
    lows, k_scales = [], []
    for b in blocks:
        keys, scale = unit(kin[b])
        k_scales.append(scale)
        store("keys", b, keys)
        gram = mm(keys, keys, 1, 1)
        store("gram", b, gram)
        lows.append(jnp.where(row > col, terms[b]["beta"] * terms[b]["decay"] * gram, 0.0))
    for b, inv in enumerate(inverses(lows)):
        store("inv", b, inv)

    local_cot.wait()
    for d in range(1, 4):
        got(cot.at[(x + 4 - d) % 4], x_recv.at[0, d - 1])
    local_w.wait()
    total = dot(cot[0], wbuf[:, :512], 1, 1)
    for i in range(1, 4):
        total = total + dot(cot[i], wbuf[:, 512 * i : 512 * i + 512], 1, 1)
    hg[...] = total
    spread(4, lambda h: hg.at[:, head_cols(h)], hgin_at)
    spread(5, lambda h: cot_ref.at[:, :256], cotz_at)

    spread_got(2, qin_at)
    spread_got(3, vin_at)
    q_scales = []
    for b in blocks:
        queries, scale = unit(qin[b])
        q_scales.append(scale)
        store("queries", b, queries)
    outs = lockstep(
        [
            chunk_forward(load("keys", b), load("queries", b), vin[b], load("inv", b), terms[b])
            for b in blocks
        ]
    )
    for b in blocks:
        for name in outs[b]:
            store(name, b, outs[b][name])
    maps = [load("map", b) for b in blocks]
    adds = [load("add", b) for b in blocks]
    pres, run2, moved, run3, run4 = chunk_chain(maps, adds)
    sent_early = len(pending)
    spread_got(5, cotz_at)
    for d in range(1, 4):
        put(
            cotz.at[:, x, :, :256], cotz.at[:, x, :, :256], x_send.at[2, d - 1],
            x_recv.at[2, d - 1], {"head": (x + d) % 4},
        )
    own[0] = pres[2]
    own[1] = run4
    other = at(z, y, 1 - c)
    put(own, peer, core_send.at[0], core_recv.at[0], other)
    store("lift", 0, load("reader", 0))
    for b in (1, 2, 3):
        store("lift", b, mm(load("reader", b), maps[0] if b == 1 else pres[b - 2]))
    for b, state, gate in ((1, adds[0], 2), (2, run2, 3), (3, adds[2], 2), (3, moved, 3)):
        store(
            "near", b,
            load("near", b) + terms[b]["gates"][gate] * mm(load("reader", b), state),
        )

    spread_got(4, hgin_at)
    d_states = jnp.zeros((C, 4 * C), F32)
    for b in blocks:
        weighted = jnp.concatenate([terms[b]["gates"][4 + i] * hgin[b] for i in range(4)], axis=1)
        d_states = d_states + mm(load("lift", b), weighted, 0, 0)
    dxo[...] = d_states
    put(dxo, dxp, core_send.at[1], core_recv.at[1], other)
    spread(6, lambda h: cot.at[:, :, 256:], cotz_rest)

    got(peer, core_recv.at[0])
    first = c == 0
    lo_map = jnp.where(first, own[0], peer[0])
    lo_add = jnp.where(first, own[1], peer[1])
    hi_map = jnp.where(first, peer[0], own[0])
    hi_add = jnp.where(first, peer[1], own[1])
    both = mm(hi_map, jnp.concatenate([lo_map, lo_add], axis=1))
    chip_map, chip_add = both[:, :C], both[:, C:] + hi_add
    high = chip_map.astype(BF16)
    rest = jnp.sum(
        jnp.where(row == col, chip_map - high.astype(F32), 0.0), axis=0, keepdims=True
    )
    mz[z, :C] = high
    mz[z, C:] = jnp.broadcast_to(rest, (16, C)).astype(BF16)
    az[z] = chip_add.astype(BF16)

    def map_parts(j):
        rest = jnp.broadcast_to(mz[j, C:].astype(F32)[:1], (C, C))
        return mz[j, :C], jnp.where(row == col, rest, 0.0).astype(BF16)

    second = c == 1
    for d in range(NZ - 1, 0, -1):
        tz = z + d
        up = tz < NZ
        put(mz.at[z], mz.at[z], zf_send.at[d], zf_recv.at[z], at(tz % NZ, y, c), when=up & first)
        put(az.at[z], az.at[z], zf_send.at[NZ + d], zf_recv.at[z], at(tz % NZ, y, c), when=up & second)
    for d in range(1, NZ):
        tz = z - d
        put(
            mz.at[z], mz.at[z], zf_send.at[2 * NZ + d], zf_recv.at[z], at((tz + NZ) % NZ, y, c),
            when=(tz >= 0) & first,
        )
    bits = [(z // (1 << b)) % 2 == 1 for b in range(3)]
    starts = [(z // (2 << b)) * (2 << b) for b in range(3)]

    got(dxp, core_recv.at[1])
    lo_dx = jnp.where(first, dxo[...], dxp[...])
    hi_dx = jnp.where(first, dxp[...], dxo[...])
    d_chip = lo_dx[:, C:] + mm(lo_map, hi_dx[:, C:], 0, 0)
    for b in range(3):
        dsc[b] = d_chip[:, b * C : (b + 1) * C].astype(BF16)
    rows_mine = pl.ds(pl.multiple_of(c * 64, 64), 64)
    rows_other = pl.ds(pl.multiple_of((1 - c) * 64, 64), 64)
    for b in (2, 1, 0):
        for d in range((2 << b) - 1, 0, -1):
            tz = z - d
            put(
                dsc.at[b, rows_mine], dsz.at[z, b, rows_mine], zb_send.at[b, d],
                zb_recv.at[z, b], at((tz + NZ) % NZ, y, c), when=bits[b] & (tz >= starts[b]),
            )

    outs = lockstep([near_back(hgin[b], vin[b], load("mix", b), terms[b]) for b in blocks])
    gate_grads = []
    for b in blocks:
        store("dvb", b, outs[b]["dvb"])
        store("dmix", b, outs[b]["dmix"])
        gate_grads.append([outs[b]["d_g0"], outs[b]["d_g1"]] + [jnp.zeros((C, 1), F32)] * 6)
    near_reads = [jnp.zeros((C, C), F32)] * NB
    near_cots = {}
    for b, state, gate, name in (
        (1, adds[0], 2, "add0"), (2, run2, 3, "run2"), (3, adds[2], 2, "add2"), (3, moved, 3, "moved"),
    ):
        weight = terms[b]["gates"][gate]
        part = mm(hgin[b], state, 1, 1)
        reader = load("reader", b)
        gate_grads[b][gate] = jnp.sum(part * reader, axis=1, keepdims=True)
        near_reads[b] = near_reads[b] + weight * part
        near_cots[name] = mm(reader, weight * hgin[b], 0, 0)
    for b in blocks:
        store("dread", b, near_reads[b])
    flush(sent_early)

    for j in range(NZ - 1):

        @pl.when((j < z) & first)
        def _():
            got(mz.at[j], zf_recv.at[j])

        @pl.when((j < z) & second)
        def _():
            got(az.at[j], zf_recv.at[j])

        put(mz.at[j], mz.at[j], rel_send.at[j], rel_recv.at[j], other, when=(j < z) & first)
        put(az.at[j], az.at[j], rel_send.at[NZ + j], rel_recv.at[j], other, when=(j < z) & second)

    zst[...] = jnp.zeros_like(zst)

    def step(j, carry):
        @pl.when(first)
        def _():
            got(az.at[j], rel_recv.at[j])

        @pl.when(second)
        def _():
            got(mz.at[j], rel_recv.at[j])

        new = mm_split(map_parts(j), split(zst[...]))
        add = az[j].astype(F32)
        for b in range(3):
            inside = (j >= starts[b]) & (j < starts[b] + (1 << b))
            zst[:, b * C : (b + 1) * C] = new[:, b * C : (b + 1) * C] + jnp.where(inside, add, 0.0)
        return carry

    lax.fori_loop(0, z, step, 0)
    for i in range(NZ - 1, 0, -1):
        for b in range(3):
            if not (i >> b) & 1:
                continue
            wanted = (z < i) & (z // (2 << b) == i // (2 << b))

            @pl.when(wanted)
            def _():
                got(dsz.at[i, b, rows_mine], zb_recv.at[i, b])

            put(
                dsz.at[i, b, rows_mine], dsz.at[i, b, rows_mine], relb_send.at[i, b],
                relb_recv.at[i, b], other, when=wanted,
            )

    for i in range(1, NZ):

        @pl.when((i > z) & first)
        def _():
            got(mz.at[i], zf_recv.at[i])

        put(mz.at[i], mz.at[i], rel_send.at[2 * NZ + i], rel_recv.at[i], other, when=(i > z) & first)

        @pl.when((i > z) & second)
        def _():
            got(mz.at[i], rel_recv.at[i])

    lam[...] = jnp.zeros_like(lam)
    local_fc.wait()
    lam[:, 3 * C :] = fcbuf[...]
    for i in range(NZ - 1, 0, -1):

        @pl.when(i > z)
        def _():
            lam[...] = mm_split(map_parts(i), split(lam[...]), 0, 0)

        for b in range(3):
            if not (i >> b) & 1:
                continue

            @pl.when((z < i) & (z // (2 << b) == i // (2 << b)))
            def _():
                got(dsz.at[i, b, rows_other], relb_recv.at[i, b])

            @pl.when((z < i) & (z // (2 << b) == i // (2 << b)))
            def _():
                lam[:, b * C : (b + 1) * C] += dsz[i, b].astype(F32)

    reads = [jnp.where(bits[b], zst[:, b * C : (b + 1) * C], 0.0) for b in range(3)]
    chip_states = jnp.concatenate(reads, axis=1)
    run_chip = reads[0] + reads[1] + reads[2]

    sent_early = len(pending)

    lower = mm(lo_map, chip_states)
    states = jnp.concatenate(
        [jnp.where(first, 0.0, lo_add), jnp.where(first, chip_states, lower)], axis=1
    )
    for b in blocks:
        reads_b = mm(load("lift", b), states)
        total = load("near", b)
        for i in range(4):
            total = total + terms[b]["gates"][4 + i] * reads_b[:, i * C : (i + 1) * C]
        hlout[b] = total.astype(BF16)
    gather_back(0, hlout, lambda h: hl.at[:, head_cols(h)])

    last = z == NZ - 1

    @pl.when(last)
    def _():
        fin_ref[y] = mm_split(split(chip_map), split(run_chip)) + chip_add

    for d in range(1, NZ):
        put(
            fin_ref.at[y], fin_ref.at[y], f_send.at[d], f_recv.at[0],
            at(NZ - 1 - d, y, c), when=last,
        )

    prefixes = [None, maps[0], pres[0], pres[1]]
    state_rows = jnp.concatenate([states[:, i * C : (i + 1) * C] for i in range(4)], axis=0)
    lift_grads = []
    backs = [mm(hgin[b], state_rows, 1, 1) for b in blocks]
    for b in blocks:
        lift = load("lift", b)
        d_lift = jnp.zeros((C, C), F32)
        for i in range(4):
            part = backs[b][:, i * C : (i + 1) * C]
            gate_grads[b][4 + i] = jnp.sum(part * lift, axis=1, keepdims=True)
            d_lift = d_lift + terms[b]["gates"][4 + i] * part
        if b:
            store("dread", b, load("dread", b) + mm(d_lift, prefixes[b], 1, 1))
            lift_grads.append(mm(load("reader", b), d_lift, 0, 0))
        else:
            store("dread", b, d_lift)

    spread_got(6, cotz_rest)
    for d in range(1, 4):
        got(cotz.at[:, (x + 4 - d) % 4, :, :256], x_recv.at[2, d - 1])

    def weight_rows(i, carry):
        cols = pl.ds(pl.multiple_of(i * 512, 512), 512)
        part = dot(hlout[...].reshape(512, C), cotz[:, i].reshape(512, 512), 0, 0)
        gpart[:, :, :, cols] = part.reshape(NZ, 2, 8, 512)
        return carry

    lax.fori_loop(0, 4, weight_rows, 0)
    put(gpart.at[:, 1 - c], gpeer, core_send.at[2], core_recv.at[2], other)

    gather_got(0, lambda h: hl.at[:, head_cols(h)])
    for d in range(1, 4):
        tx = (x + d) % 4
        mpart[d - 1] = dot(
            hl[...], wbuf[:, pl.ds(pl.multiple_of(tx * 512, 512), 512)]
        ).astype(BF16)
        put(
            mpart.at[d - 1], mrecv.at[d - 1], x_send.at[1, d - 1], x_recv.at[1, d - 1],
            {"head": tx},
        )
    mown[...] = dot(hl[...], wbuf[:, cot_cols])

    got(gpeer, core_recv.at[2])

    def chip_rows(i, carry):
        part = gpart[i, c] + gpeer[i]
        zsend[i] = jnp.concatenate([part[:, :1024], part[:, 1024:]], axis=0).astype(BF16)
        return carry

    lax.fori_loop(0, NZ, chip_rows, 0)
    for d in range(NZ - 1, 0, -1):
        tz = (z + d) % NZ
        put(zsend.at[tz], zrecv.at[d - 1], gz_send.at[d - 1], gz_recv.at[d - 1], at(tz, y, c))

    outs = lockstep(
        [
            chunk_back_a(
                load("dmix", b), load("dread", b), load("keys", b), load("queries", b),
                load("inv", b), load("scores", b), load("mix", b), terms[b], q_scales[b],
            )
            for b in blocks
        ]
    )
    cums = [outs[b]["cum"] for b in blocks]
    for b in blocks:
        gout[0, b] = outs[b]["query"].astype(BF16)
        for name in ("dkb", "dlow", "dkey", "gap"):
            store(name, b, outs[b][name])
    targets = (dq_ref, dk_ref, dv_ref)

    def send_back(i):
        gather_back(1 + i, gout.at[i], lambda h: targets[i].at[:, head_cols(h)])

    send_back(0)

    d_chip_map = mm(lam[...], jnp.concatenate([zst[...], run_chip], axis=1), 1, 1)
    d_chip_add = lam[:, 3 * C :]
    for b in range(3):
        d_chip_add = d_chip_add + jnp.where(bits[b], 0.0, lam[:, b * C : (b + 1) * C])
    chip_pair = jnp.concatenate([d_chip_map, d_chip_add], axis=1)
    as_second = mm(chip_pair, jnp.concatenate([lo_map, lo_add], axis=1), 1, 1)
    through = mm(hi_map, chip_pair, 0, 0)
    as_first = through[:, :C] + mm(hi_dx[:, C:], chip_states, 1, 1)
    d_total = jnp.where(first, as_first, as_second)
    d_run4 = jnp.where(first, through[:, C:] + hi_dx[:, :C], d_chip_add)
    d_maps, d_adds = chain_back(
        d_total, d_run4, maps, adds[0], pres[0], pres[1], run2, run3, lift_grads, near_cots
    )

    @pl.when(jnp.logical_not(last))
    def _():
        got(fin_ref.at[y], f_recv.at[0])

    for d in range(1, NY):
        ty = (y + d) % NY
        put(fin_ref.at[y], fin_ref.at[y], f_send.at[NZ + d], f_recv.at[d], at(z, ty, c))

    flush(sent_early)
    pairs = lockstep(
        [
            chunk_back_b(
                d_maps[b], d_adds[b], load("keys", b), load("inv", b), load("weights", b),
                load("plain", b), load("dvb", b), load("dkb", b), terms[b],
            )
            for b in blocks
        ]
    )
    for b in blocks:
        gout[2, b] = pairs[b]["value"].astype(BF16)
    send_back(2)

    total = zsend[z].astype(F32)
    for d in range(1, NZ):
        got(zrecv.at[d - 1], gz_recv.at[d - 1])
        total = total + zrecv[d - 1].astype(F32)
    gsum[...] = jnp.concatenate([total[:8], total[8:]], axis=1)
    put(gsum, gw_ref, gp_send.at[0], gp_recv.at[0], rows_to, here=rows_stay)

    outs = lockstep(
        [
            chunk_back_c(
                d_maps[b], pairs[b]["dvb"], pairs[b]["dkb"], pairs[b]["dkt"], pairs[b]["back"],
                load("dlow", b), load("dkey", b), load("gap", b), cums[b], load("gram", b),
                load("keys", b), vin[b], load("weights", b), load("plain", b), terms[b],
                k_scales[b], gate_grads[b],
            )
            for b in blocks
        ]
    )
    for b in blocks:
        gout[1, b] = outs[b][0].astype(BF16)
        sout[b] = outs[b][1]
    send_back(1)
    gather_back(4, sout, lambda h: dsmall_ref.at[h])

    total = mown[...]
    for d in range(1, 4):
        got(mrecv.at[d - 1], x_recv.at[1, d - 1])
    for d in range(3):
        total = total + mrecv[d].astype(F32)
    mixed_ref[...] = total.astype(BF16)
    got(gw_ref, gp_recv.at[0])

    for d in range(1, NY):
        sy = (y + NY - d) % NY
        got(fin_ref.at[sy], f_recv.at[d])
    for i in range(3):
        gather_got(1 + i, lambda h, i=i: targets[i].at[:, head_cols(h)])
    gather_got(4, lambda h: dsmall_ref.at[h])
    flush(len(pending))


def finish_kernel(*refs):
    ins, small_ref = refs[:6], refs[6]
    outs, (rate_ref, decay_ref, gate_ref) = refs[7:13], refs[13:16]
    for i in range(6):
        outs[i][...] = ins[i][...].astype(outs[i].dtype)
    for h in range(NY):
        one = slice(h, h + 1)
        rate_ref[one] = small_ref[h, 0:1]
        decay_ref[one] = small_ref[h, 1:2]
        for i in range(NL):
            gate_ref[i, one] = small_ref[h, 2 + i : 3 + i]


def on_device(
    queries, key_vectors, values, write_rates, log_decay, level_gates, out_weight,
    out_cotangent, final_cotangent,
):
    vmem = pl.BlockSpec(memory_space=pltpu.VMEM)
    anywhere = pl.BlockSpec(memory_space=pl.ANY)
    sem = pltpu.SemaphoreType.DMA
    quad = pltpu.VMEM((NB, C, C), F32)
    mixed, dq, dk, dv, dsmall, gw, fin = pl.pallas_call(
        kernel,
        out_shape=[
            jax.ShapeDtypeStruct((C, 512), BF16),
            jax.ShapeDtypeStruct((C, 512), BF16),
            jax.ShapeDtypeStruct((C, 512), BF16),
            jax.ShapeDtypeStruct((C, 512), BF16),
            jax.ShapeDtypeStruct((4, 16, C), F32),
            jax.ShapeDtypeStruct((8, 2048), F32),
            jax.ShapeDtypeStruct((4, C, C), F32),
        ],
        in_specs=[anywhere] * 3 + [vmem] * 3 + [anywhere] * 3,
        out_specs=[vmem] + [anywhere] * 4 + [vmem] * 2,
        scratch_shapes=[
            quad, quad, quad, pltpu.VMEM((NB, 16, C), F32), pltpu.VMEM((NY, 16, C), F32), quad,
            pltpu.VMEM((4, C, 512), BF16),
            pltpu.VMEM((C, 512), F32),
            pltpu.VMEM((C, 512), BF16),
            pltpu.VMEM((NB, C, C), BF16),
            pltpu.VMEM((3, NB, C, C), BF16),
            pltpu.VMEM((NB, 16, C), F32),
            pltpu.VMEM((512, 2048), BF16),
            pltpu.VMEM((C, C), F32),
            pltpu.VMEM((2, C, C), F32),
            pltpu.VMEM((2, C, C), F32),
            pltpu.VMEM((NZ, C + 16, C), BF16),
            pltpu.VMEM((NZ, C, C), BF16),
            pltpu.VMEM((C, 3 * C), F32),
            pltpu.VMEM((C, 4 * C), F32),
            pltpu.VMEM((C, 4 * C), F32),
            pltpu.VMEM((3, C, C), BF16),
            pltpu.VMEM((NZ, 3, C, C), BF16),
            pltpu.VMEM((C, 4 * C), F32),
            pltpu.VMEM((NB, 4, C, 512), BF16),
            pltpu.VMEM((NZ, 2, 8, 2048), F32),
            pltpu.VMEM((NZ, 8, 2048), F32),
            pltpu.VMEM((8, 2048), F32),
            pltpu.VMEM((NZ, 16, 1024), BF16),
            pltpu.VMEM((NZ - 1, 16, 1024), BF16),
            pltpu.VMEM((C, 512), F32),
            pltpu.VMEM((3, C, 512), BF16),
            pltpu.VMEM((3, C, 512), BF16),
            sem((7, 4)), sem((7, 4)), sem((5, 4)), sem((5, 4)),
            sem((3, 3)), sem((3, 3)), sem((3,)), sem((3,)), sem((3,)),
            sem((3 * NZ,)), sem((NZ,)), sem((3 * NZ,)), sem((NZ,)),
            sem((3, NZ)), sem((NZ, 3)), sem((NZ, 3)), sem((NZ, 3)),
            sem((1,)), sem((1,)), sem((NZ - 1,)), sem((NZ - 1,)),
            sem((NZ + NY,)), sem((NY,)),
        ],
        compiler_params=pltpu.CompilerParams(
            collective_id=0, has_side_effects=True, vmem_limit_bytes=56 * 1024 * 1024
        ),
    )(
        key_vectors, queries, values, write_rates, log_decay, level_gates, out_weight,
        out_cotangent, final_cotangent,
    )
    whole = (mixed, dq, dk, dv, gw, fin)
    out = pl.pallas_call(
        finish_kernel,
        out_shape=[
            jax.ShapeDtypeStruct(part.shape, F32 if i else BF16) for i, part in enumerate(whole)
        ]
        + [
            jax.ShapeDtypeStruct((4, C), F32),
            jax.ShapeDtypeStruct((4, C), F32),
            jax.ShapeDtypeStruct((NL, 4, C), F32),
        ],
        in_specs=[vmem] * 7,
        out_specs=[vmem] * 9,
    )(*whole, dsmall)
    mixed, dq, dk, dv, gw, fin, d_rates, d_decay, d_gates = out
    return (mixed, dq, dk, dv, d_rates, d_decay, d_gates, gw, fin)


def solution(mesh):
    return jax.shard_map(
        on_device,
        mesh=mesh,
        in_specs=(
            P("ctx", "head"), P("ctx", "head"), P("ctx", "head"), P("head", "ctx"),
            P("head", "ctx"), P(None, "head", "ctx"), P("head", None), P("ctx", "head"),
            P("head", None, None),
        ),
        out_specs=(
            P("ctx", "head"), P("ctx", "head"), P("ctx", "head"), P("ctx", "head"),
            P("head", "ctx"), P("head", "ctx"), P(None, "head", "ctx"),
            P(("head", "ctx"), None), P("head", None, None),
        ),
        check_vma=False,
    )
```

```python
import functools

import jax
import jax.numpy as jnp
from jax import lax
from jax.experimental import pallas as pl
from jax.experimental.pallas import tpu as pltpu
from jax.sharding import PartitionSpec as P

F32 = jnp.float32
BF16 = jnp.bfloat16
C = 128
NZ, NY, NB, NL = 8, 4, 4, 8
MESH = pl.DeviceIdType.MESH


def split(x):
    high = x.astype(BF16)
    return high, (x - high.astype(F32)).astype(BF16)


SPLITS = {}


def split_once(x):
    if id(x) not in SPLITS:
        SPLITS[id(x)] = (x, split(x))
    return SPLITS[id(x)][1]


def dot(a, b, ca=1, cb=0, precision=None):
    return lax.dot_general(
        a, b, (((ca,), (cb,)), ((), ())), preferred_element_type=F32, precision=precision
    )


def mm(a, b, ca=1, cb=0):
    return mm_split(split_once(a), split_once(b), ca, cb)


def mm_split(a, b, ca=1, cb=0):
    (ah, al), (bh, bl) = a, b
    return dot(
        jnp.concatenate([ah, ah, al], axis=ca), jnp.concatenate([bh, bl, bh], axis=cb), ca, cb
    )


def iotas():
    return (
        lax.broadcasted_iota(jnp.int32, (C, C), 0),
        lax.broadcasted_iota(jnp.int32, (C, C), 1),
    )


def unit(x):
    scale = lax.rsqrt(jnp.sum(x * x, axis=1, keepdims=True) + 1e-6)
    return x * scale, scale


def unit_back(grad, vec, scale):
    return scale * (grad - vec * jnp.sum(vec * grad, axis=1, keepdims=True))


def token_terms(rows):
    row, col = iotas()
    upper = jnp.where(row <= col, 1.0, 0.0).astype(F32)
    cum = dot(rows, upper, precision=lax.Precision.HIGHEST)
    stacked = jnp.concatenate([rows, cum, jnp.zeros((C - 32, C), F32)], axis=0).T
    beta = stacked[:, 0:1]
    cum_col = stacked[:, 17:18]
    cum_row = cum[1:2, :]
    last = cum[1:2, C - 1 : C]
    decay = jnp.where(row >= col, jnp.exp(jnp.minimum(cum_col - cum_row, 0.0)), 0.0)
    return dict(
        beta=beta,
        gam=jnp.exp(cum_col),
        tail=jnp.exp(last - cum_col),
        glast=jnp.exp(last),
        gates=[stacked[:, 2 + i : 3 + i] for i in range(NL)],
        decay=decay,
    )


def inverses(lows):
    row, col = iotas()
    eye = jnp.where(row == col, 1.0, 0.0).astype(F32)
    invs = [eye - jnp.where((row >> 1) == (col >> 1), low, 0.0) for low in lows]
    for bit in range(1, 7):
        here = ((row >> (bit + 1)) == (col >> (bit + 1))) & ((row >> bit) != (col >> bit))
        parts = [mm(jnp.where(here, low, 0.0), inv) for low, inv in zip(lows, invs)]
        invs = [inv - mm(inv, part) for inv, part in zip(invs, parts)]
    return invs


def gate_matrix(tt):
    row, col = iotas()
    return jnp.where((row >> 6) == (col >> 6), tt["gates"][0], tt["gates"][1])


def lockstep(runs):
    results = [None] * len(runs)
    alive = list(range(len(runs)))
    while alive:
        for i in list(alive):
            try:
                next(runs[i])
            except StopIteration as stop:
                results[i] = stop.value
                alive.remove(i)
    return results


def chunk_states(keys, values, inv, tt):
    row, col = iotas()
    beta = tt["beta"]
    pair = mm(inv, jnp.concatenate([beta * tt["gam"] * keys, beta * values], axis=1))
    yield
    both = mm(tt["tail"] * keys, pair, 0, 0)
    yield
    return dict(
        weights=pair[:, :C], plain=pair[:, C:], add=both[:, C:],
        map=jnp.where(row == col, tt["glast"], 0.0) - both[:, :C],
    )


def chunk_reads(keys, queries, values, inv, tt):
    scores = mm(queries, keys, 1, 1) * tt["decay"]
    yield
    mix = mm(scores, inv)
    yield
    reader = tt["gam"] * queries - mm(mix, tt["beta"] * tt["gam"] * keys)
    yield
    near = mm(mix * gate_matrix(tt), tt["beta"] * values)
    yield
    return dict(scores=scores, mix=mix, reader=reader, near=near)


def near_back(hg, values, mix, tt):
    row, col = iotas()
    gate = gate_matrix(tt)
    cross = mm(hg, tt["beta"] * values, 1, 1)
    yield
    d_vb = mm(mix * gate, hg, 0, 0)
    yield
    gated = cross * mix
    same = (row >> 6) == (col >> 6)
    d_g0 = jnp.sum(jnp.where(same, gated, 0.0), axis=1, keepdims=True)
    d_g1 = jnp.sum(jnp.where(same, 0.0, gated), axis=1, keepdims=True)
    return dict(d_g0=d_g0, d_g1=d_g1, dvb=d_vb, dmix=cross * gate)


def chunk_back_a(d_mix, d_reader, keys, queries, inv, scores, mix, tt, q_scale):
    gam, decay = tt["gam"], tt["decay"]
    row, col = iotas()
    d_mix = d_mix - mm(d_reader, tt["beta"] * gam * keys, 1, 1)
    yield
    d_kb = -mm(mix, d_reader, 0, 0)
    yield
    d_scores = jnp.where(row >= col, mm(d_mix, inv, 1, 1), 0.0)
    yield
    d_qk = d_scores * decay
    d_query = mm(d_qk, keys) + gam * d_reader
    yield
    d_low = mm(mix, d_scores, 0, 0)
    yield
    d_key = mm(d_qk, queries, 0, 0)
    yield
    cum = gam * jnp.sum(d_reader * queries, axis=1, keepdims=True)
    return dict(
        dkb=d_kb, dlow=d_low, dkey=d_key, gap=d_scores * scores, cum=cum,
        query=unit_back(d_query, queries, q_scale),
    )


def chunk_back_b(d_map, d_add, keys, inv, weights, plain, d_vb, d_kb, tt):
    grads = jnp.concatenate([d_add, -d_map], axis=1)
    d_pw = mm(tt["tail"] * keys, grads)
    yield
    d_kt = mm(jnp.concatenate([plain, weights], axis=1), grads, 1, 1)
    yield
    back = mm(inv, d_pw, 0, 0)
    yield
    d_vb = d_vb + back[:, :C]
    return dict(dvb=d_vb, dkb=d_kb + back[:, C:], dkt=d_kt, back=back, value=tt["beta"] * d_vb)


def chunk_back_c(
    d_map, d_vb, d_kb, d_kt, back, d_low, d_key, gap, cum, gram, keys, values, weights, plain, tt,
    k_scale, gate_grads,
):
    beta, gam, tail, decay = tt["beta"], tt["gam"], tt["tail"], tt["decay"]
    row, col = iotas()
    d_low = d_low + mm(back, jnp.concatenate([plain, weights], axis=1), 1, 1)
    yield
    d_low = jnp.where(row > col, -d_low, 0.0) * decay
    d_gram = beta * d_low
    d_key = d_key + mm(d_gram + d_gram.T, keys) + beta * gam * d_kb + tail * d_kt
    yield
    dk_gram = d_low * gram
    d_gap = gap + beta * dk_gram
    kb_k = jnp.sum(d_kb * keys, axis=1, keepdims=True)
    d_beta = jnp.sum(dk_gram + d_vb * values, axis=1, keepdims=True) + gam * kb_k
    tail_part = tail * jnp.sum(d_kt * keys, axis=1, keepdims=True)
    d_cum = cum + gam * beta * kb_k - tail_part + jnp.sum(d_gap, axis=1, keepdims=True)
    d_last = jnp.sum(tail_part, axis=0, keepdims=True) + tt["glast"] * jnp.sum(
        jnp.sum(jnp.where(row == col, d_map, 0.0), axis=1, keepdims=True), axis=0, keepdims=True
    )
    lane = lax.broadcasted_iota(jnp.int32, (1, C), 1)
    d_cum_row = jnp.where(lane == C - 1, d_last, 0.0) - jnp.sum(d_gap, axis=0, keepdims=True)
    cols = jnp.where(col == 0, d_beta, 0.0) + jnp.where(col == 1, d_cum, 0.0)
    for i in range(NL):
        cols = cols + jnp.where(col == 2 + i, gate_grads[i], 0.0)
    rows = cols.T[:16, :]
    at = lax.broadcasted_iota(jnp.int32, (16, C), 0)
    rows = rows + jnp.where(at == 1, d_cum_row, 0.0)
    lower = jnp.where(row >= col, 1.0, 0.0).astype(F32)
    rows = jnp.where(at == 1, dot(rows, lower, precision=lax.Precision.HIGHEST), rows)
    return unit_back(d_key, keys, k_scale), rows


def chunk_chain(maps, adds):
    one = jnp.concatenate([maps[0], adds[0]], axis=1)
    two = mm(maps[1], one)
    run2 = two[:, C:] + adds[1]
    three = mm(maps[2], jnp.concatenate([two[:, :C], run2], axis=1))
    moved = three[:, C:]
    run3 = moved + adds[2]
    four = mm(maps[3], jnp.concatenate([three[:, :C], run3], axis=1))
    return [two[:, :C], three[:, :C], four[:, :C]], run2, moved, run3, four[:, C:] + adds[3]


def chain_back(d_total, d_run4, maps, add0, pre2, pre3, run2, run3, lift_grads, near):
    pair = jnp.concatenate([d_total, d_run4], axis=1)
    d_map3 = mm(pair, jnp.concatenate([pre3, run3], axis=1), 1, 1)
    d_add3 = d_run4
    down = mm(maps[3], pair, 0, 0)
    d_pre3 = down[:, :C] + lift_grads[2]
    d_run3 = down[:, C:]
    d_add2 = d_run3 + near["add2"]
    pair = jnp.concatenate([d_pre3, d_run3 + near["moved"]], axis=1)
    d_map2 = mm(pair, jnp.concatenate([pre2, run2], axis=1), 1, 1)
    down = mm(maps[2], pair, 0, 0)
    d_pre2 = down[:, :C] + lift_grads[1]
    d_run2 = down[:, C:] + near["run2"]
    pair = jnp.concatenate([d_pre2, d_run2], axis=1)
    d_map1 = mm(pair, jnp.concatenate([maps[0], add0], axis=1), 1, 1)
    down = mm(maps[1], pair, 0, 0)
    d_map0 = down[:, :C] + lift_grads[0]
    d_add0 = down[:, C:] + near["add0"]
    return [d_map0, d_map1, d_map2, d_map3], [d_add0, d_run2, d_add2, d_add3]


def kernel(
    k_ref, q_ref, v_ref, rate_ref, decay_ref, gate_ref, w_ref, cot_ref, fcot_ref,
    mixed_ref, dq_ref, dk_ref, dv_ref, dsmall_ref, gw_ref, fin_ref,
    kin, qin, vin, sin, spack, hgin, cot, hg, hl, hlout, gout, sout, wbuf, fcbuf,
    own, peer, mz, az, zst, dxo, dxp, dsc, dsz, lam,
    cotz, gpart, gpeer, gsum, zsend, zrecv, mown, mpart, mrecv,
    in_send, in_recv, out_send, out_recv, x_send, x_recv, loc, core_send, core_recv,
    zf_send, zf_recv, rel_send, rel_recv, zb_send, zb_recv, relb_send, relb_recv,
    gp_send, gp_recv, gz_send, gz_recv, f_send, f_recv,
):
    SPLITS.clear()
    me = lax.axis_index("ctx")
    x = lax.axis_index("head")
    z, y, c = me // 8, (me // 2) % 4, me % 2
    pending = []

    def flush(count):
        for finish in pending[:count]:
            finish()
        del pending[:count]


    def at(zz, yy, cc):
        return {"ctx": (zz * 4 + yy) * 2 + cc}

    def remote(src, dst, send, recv, target):
        return pltpu.make_async_remote_copy(
            src_ref=src, dst_ref=dst, send_sem=send, recv_sem=recv,
            device_id=target, device_id_type=MESH,
        )

    def put(src, dst, send, recv, target, here=None, when=None):
        copy = remote(src, dst, send, recv, target)
        cond = when
        if here is not None:
            cond = jnp.logical_not(here)

            @pl.when(here)
            def _():
                pltpu.make_async_copy(src, dst, recv).start()

        if cond is None:
            copy.start()
            pending.append(copy.wait_send)
        else:

            @pl.when(cond)
            def _():
                copy.start()

            def finish():
                @pl.when(cond)
                def _():
                    copy.wait_send()

            pending.append(finish)

    def got(dst, sem):
        pltpu.make_async_copy(dst, dst, sem).wait()

    def head_cols(i):
        return pl.ds(pl.multiple_of(i * C, C), C)

    local_w = pltpu.make_async_copy(w_ref, wbuf, loc.at[1])
    local_w.start()
    local_fc = pltpu.make_async_copy(fcot_ref.at[y], fcbuf, loc.at[2])
    local_fc.start()
    for h in range(NY):
        one = slice(h, h + 1)
        spack[h] = jnp.concatenate(
            [rate_ref[one], decay_ref[one]]
            + [gate_ref[i, one] for i in range(NL)]
            + [jnp.zeros((6, C), F32)],
            axis=0,
        )

    barrier = pltpu.get_barrier_semaphore()
    for dy in range(NY):
        for dc in range(2):
            if dy or dc:
                pl.semaphore_signal(
                    barrier, inc=1, device_id=at(z, (y + dy) % NY, (c + dc) % 2), device_id_type=MESH
                )
    for dz in range(1, NZ):
        pl.semaphore_signal(barrier, inc=1, device_id=at((z + dz) % NZ, y, c), device_id_type=MESH)
    for dx in range(1, 4):
        pl.semaphore_signal(barrier, inc=1, device_id={"head": (x + dx) % 4}, device_id_type=MESH)
    rows_from = at((z % 2) * 4 + y, z // 2, c)
    rows_to = at(2 * y + z // 4, z % 4, c)
    rows_stay = rows_to["ctx"] == me

    @pl.when(jnp.logical_not(rows_stay))
    def _():
        pl.semaphore_signal(barrier, inc=1, device_id=rows_from, device_id_type=MESH)

    pl.semaphore_wait(barrier, jnp.where(rows_stay, 17, 18))

    slot = (y % 2) * 2 + c
    half = y // 2

    def spread(idx, src_of, dst):
        for d in range(NY):
            h = (y + d) % NY
            put(
                src_of(h), dst(slot), in_send.at[idx, d], in_recv.at[idx, slot],
                at(z, h, half), here=(c == half) if d == 0 else None,
            )

    def spread_got(idx, dst):
        for b in range(NB):
            got(dst(b), in_recv.at[idx, b])

    cot_cols = pl.ds(pl.multiple_of(x * 512, 512), 512)
    kin_at, qin_at, vin_at = (lambda b: kin.at[b]), (lambda b: qin.at[b]), (lambda b: vin.at[b])
    sin_at, hgin_at = (lambda b: sin.at[b]), (lambda b: hgin.at[b])

    def cotz_at(b):
        return cotz.at[b, x, :, :256]

    def cotz_rest(b):
        return cotz.at[b, :, :, 256:]

    def gather_back(idx, src, dst_of):
        for b in range(NB):
            ty, tc = 2 * c + b // 2, b % 2
            put(
                src.at[b], dst_of(y), out_send.at[idx, b], out_recv.at[idx, y],
                at(z, ty, tc), here=(ty == y) & (tc == c),
            )

    def gather_got(idx, dst_of):
        for h in range(NY):
            got(dst_of(h), out_recv.at[idx, h])

    spread(1, lambda h: spack.at[h], sin_at)
    spread(0, lambda h: k_ref.at[:, head_cols(h)], kin_at)
    for d in range(1, 4):
        put(
            cot_ref, cot.at[x], x_send.at[0, d - 1], x_recv.at[0, d - 1], {"head": (x + d) % 4},
        )
    local_cot = pltpu.make_async_copy(cot_ref, cot.at[x], loc.at[0])
    local_cot.start()

    held = {}

    def load(name, b):
        return held[name, b]

    def store(name, b, value):
        held[name, b] = value

    row, col = iotas()
    blocks = range(NB)

    spread_got(1, sin_at)
    terms = [token_terms(sin[b]) for b in blocks]
    spread_got(0, kin_at)
    spread(3, lambda h: v_ref.at[:, head_cols(h)], vin_at)
    spread(2, lambda h: q_ref.at[:, head_cols(h)], qin_at)
    lows, k_scales = [], []
    for b in blocks:
        keys, scale = unit(kin[b])
        k_scales.append(scale)
        store("keys", b, keys)
        gram = mm(keys, keys, 1, 1)
        store("gram", b, gram)
        lows.append(jnp.where(row > col, terms[b]["beta"] * terms[b]["decay"] * gram, 0.0))
    for b, inv in enumerate(inverses(lows)):
        store("inv", b, inv)

    spread_got(3, vin_at)
    outs = lockstep([chunk_states(load("keys", b), vin[b], load("inv", b), terms[b]) for b in blocks])
    for b in blocks:
        for name in outs[b]:
            store(name, b, outs[b][name])
    maps = [load("map", b) for b in blocks]
    adds = [load("add", b) for b in blocks]
    pres, run2, moved, run3, run4 = chunk_chain(maps, adds)
    own[0] = pres[2]
    own[1] = run4
    other = at(z, y, 1 - c)
    put(own, peer, core_send.at[0], core_recv.at[0], other)

    local_cot.wait()
    for d in range(1, 4):
        got(cot.at[(x + 4 - d) % 4], x_recv.at[0, d - 1])
    local_w.wait()
    total = dot(cot[0], wbuf[:, :512], 1, 1)
    for i in range(1, 4):
        total = total + dot(cot[i], wbuf[:, 512 * i : 512 * i + 512], 1, 1)
    hg[...] = total
    spread(4, lambda h: hg.at[:, head_cols(h)], hgin_at)
    spread(5, lambda h: cot_ref.at[:, :256], cotz_at)

    got(peer, core_recv.at[0])
    first = c == 0
    lo_map = jnp.where(first, own[0], peer[0])
    lo_add = jnp.where(first, own[1], peer[1])
    hi_map = jnp.where(first, peer[0], own[0])
    hi_add = jnp.where(first, peer[1], own[1])
    both = mm(hi_map, jnp.concatenate([lo_map, lo_add], axis=1))
    chip_map, chip_add = both[:, :C], both[:, C:] + hi_add
    high = chip_map.astype(BF16)
    rest = jnp.sum(
        jnp.where(row == col, chip_map - high.astype(F32), 0.0), axis=0, keepdims=True
    )
    mz[z, :C] = high
    mz[z, C:] = jnp.broadcast_to(rest, (16, C)).astype(BF16)
    az[z] = chip_add.T.astype(BF16)
    second = c == 1
    for d in range(NZ - 1, 0, -1):
        tz = z + d
        up = tz < NZ
        put(mz.at[z], mz.at[z], zf_send.at[d], zf_recv.at[z], at(tz % NZ, y, c), when=up & first)
        put(az.at[z], az.at[z], zf_send.at[NZ + d], zf_recv.at[z], at(tz % NZ, y, c), when=up & second)
    for d in range(1, NZ):
        tz = z - d
        put(
            mz.at[z], mz.at[z], zf_send.at[2 * NZ + d], zf_recv.at[z], at((tz + NZ) % NZ, y, c),
            when=(tz >= 0) & first,
        )

    spread_got(2, qin_at)
    q_scales = []
    for b in blocks:
        queries, scale = unit(qin[b])
        q_scales.append(scale)
        store("queries", b, queries)
    outs = lockstep(
        [
            chunk_reads(load("keys", b), load("queries", b), vin[b], load("inv", b), terms[b])
            for b in blocks
        ]
    )
    for b in blocks:
        for name in outs[b]:
            store(name, b, outs[b][name])
    store("lift", 0, load("reader", 0))
    for b in (1, 2, 3):
        store("lift", b, mm(load("reader", b), maps[0] if b == 1 else pres[b - 2]))

    spread_got(4, hgin_at)
    d_states = jnp.zeros((4 * C, C), F32)
    for b in blocks:
        turned = hgin[b].T
        weighted = jnp.concatenate(
            [turned * sin[b, 6 + i : 7 + i] for i in range(4)], axis=0
        )
        d_states = d_states + mm(weighted, load("lift", b))
    dxo[...] = d_states
    put(dxo, dxp, core_send.at[1], core_recv.at[1], other)
    sent_early = len(pending)
    spread_got(5, cotz_at)
    for d in range(1, 4):
        put(
            cotz.at[:, x, :, :256], cotz.at[:, x, :, :256], x_send.at[2, d - 1],
            x_recv.at[2, d - 1], {"head": (x + d) % 4},
        )
    spread(6, lambda h: cot.at[:, :, 256:], cotz_rest)

    for b, state, gate in ((1, adds[0], 2), (2, run2, 3), (3, adds[2], 2), (3, moved, 3)):
        store(
            "near", b,
            load("near", b) + terms[b]["gates"][gate] * mm(load("reader", b), state),
        )

    bits = [(z // (1 << b)) % 2 == 1 for b in range(3)]
    starts = [(z // (2 << b)) * (2 << b) for b in range(3)]
    got(dxp, core_recv.at[1])
    lo_dx = jnp.where(first, dxo[...], dxp[...])
    hi_dx = jnp.where(first, dxp[...], dxo[...])
    d_chip = lo_dx[C:] + mm(hi_dx[C:], lo_map)
    for b in range(3):
        dsc[b] = d_chip[b * C : (b + 1) * C].astype(BF16)
    rows_mine = pl.ds(pl.multiple_of(c * 64, 64), 64)
    rows_other = pl.ds(pl.multiple_of((1 - c) * 64, 64), 64)
    for b in (2, 1, 0):
        for d in range((2 << b) - 1, 0, -1):
            tz = z - d
            put(
                dsc.at[b, rows_mine], dsz.at[z, b, rows_mine], zb_send.at[b, d],
                zb_recv.at[z, b], at((tz + NZ) % NZ, y, c), when=bits[b] & (tz >= starts[b]),
            )

    outs = lockstep([near_back(hgin[b], vin[b], load("mix", b), terms[b]) for b in blocks])
    gate_grads = []
    for b in blocks:
        store("dvb", b, outs[b]["dvb"])
        store("dmix", b, outs[b]["dmix"])
        gate_grads.append([outs[b]["d_g0"], outs[b]["d_g1"]] + [jnp.zeros((C, 1), F32)] * 6)
    near_reads = [jnp.zeros((C, C), F32)] * NB
    near_cots = {}
    for b, state, gate, name in (
        (1, adds[0], 2, "add0"), (2, run2, 3, "run2"), (3, adds[2], 2, "add2"), (3, moved, 3, "moved"),
    ):
        weight = terms[b]["gates"][gate]
        part = mm(hgin[b], state, 1, 1)
        reader = load("reader", b)
        gate_grads[b][gate] = jnp.sum(part * reader, axis=1, keepdims=True)
        near_reads[b] = near_reads[b] + weight * part
        near_cots[name] = mm(reader, weight * hgin[b], 0, 0)
    for b in blocks:
        store("dread", b, near_reads[b])
    flush(sent_early)

    for j in range(NZ - 1):

        @pl.when((j < z) & first)
        def _():
            got(mz.at[j], zf_recv.at[j])

        @pl.when((j < z) & second)
        def _():
            got(az.at[j], zf_recv.at[j])

        put(mz.at[j], mz.at[j], rel_send.at[j], rel_recv.at[j], other, when=(j < z) & first)
        put(az.at[j], az.at[j], rel_send.at[NZ + j], rel_recv.at[j], other, when=(j < z) & second)

    zst[...] = jnp.zeros_like(zst)

    def step(j, carry):
        @pl.when(first)
        def _():
            got(az.at[j], rel_recv.at[j])

        @pl.when(second)
        def _():
            got(mz.at[j], rel_recv.at[j])

        now = zst[...]
        high = mz[j, :C]
        new = dot(
            jnp.concatenate(split(now), axis=1), jnp.concatenate([high, high], axis=1), 1, 1
        ) + now * mz[j, C:].astype(F32)[:1]
        add = az[j].astype(F32)
        for b in range(3):
            inside = (j >= starts[b]) & (j < starts[b] + (1 << b))
            zst[b * C : (b + 1) * C] = new[b * C : (b + 1) * C] + jnp.where(inside, add, 0.0)
        return carry

    lax.fori_loop(0, z, step, 0)
    reads = [jnp.where(bits[b], zst[b * C : (b + 1) * C], 0.0) for b in range(3)]
    chip_states = jnp.concatenate(reads, axis=0)
    run_chip = reads[0] + reads[1] + reads[2]

    lower = mm(chip_states, lo_map, 1, 1)
    states = jnp.concatenate(
        [jnp.where(first, 0.0, lo_add.T), jnp.where(first, chip_states, lower)], axis=0
    )
    for b in blocks:
        reads_b = mm(load("lift", b), states, 1, 1)
        total = load("near", b)
        for i in range(4):
            total = total + terms[b]["gates"][4 + i] * reads_b[:, i * C : (i + 1) * C]
        hlout[b] = total.astype(BF16)
    gather_back(0, hlout, lambda h: hl.at[:, head_cols(h)])

    last = z == NZ - 1

    @pl.when(last)
    def _():
        fin_ref[y] = mm_split(split(run_chip), split(chip_map), 1, 1).T + chip_add

    for d in range(1, NZ):
        put(
            fin_ref.at[y], fin_ref.at[y], f_send.at[d], f_recv.at[0],
            at(NZ - 1 - d, y, c), when=last,
        )

    prefixes = [None, maps[0], pres[0], pres[1]]
    state_cols = jnp.concatenate([states[i * C : (i + 1) * C] for i in range(4)], axis=1)
    lift_grads = []
    backs = [mm(hgin[b], state_cols) for b in blocks]
    for b in blocks:
        lift = load("lift", b)
        d_lift = jnp.zeros((C, C), F32)
        for i in range(4):
            part = backs[b][:, i * C : (i + 1) * C]
            gate_grads[b][4 + i] = jnp.sum(part * lift, axis=1, keepdims=True)
            d_lift = d_lift + terms[b]["gates"][4 + i] * part
        if b:
            store("dread", b, load("dread", b) + mm(d_lift, prefixes[b], 1, 1))
            lift_grads.append(mm(load("reader", b), d_lift, 0, 0))
        else:
            store("dread", b, d_lift)

    for i in range(NZ - 1, 0, -1):
        for b in range(3):
            if not (i >> b) & 1:
                continue
            wanted = (z < i) & (z // (2 << b) == i // (2 << b))

            @pl.when(wanted)
            def _():
                got(dsz.at[i, b, rows_mine], zb_recv.at[i, b])

            put(
                dsz.at[i, b, rows_mine], dsz.at[i, b, rows_mine], relb_send.at[i, b],
                relb_recv.at[i, b], other, when=wanted,
            )

    for i in range(1, NZ):

        @pl.when((i > z) & first)
        def _():
            got(mz.at[i], zf_recv.at[i])

        put(mz.at[i], mz.at[i], rel_send.at[2 * NZ + i], rel_recv.at[i], other, when=(i > z) & first)

        @pl.when((i > z) & second)
        def _():
            got(mz.at[i], rel_recv.at[i])

    sent_early = len(pending)

    spread_got(6, cotz_rest)
    for d in range(1, 4):
        got(cotz.at[:, (x + 4 - d) % 4, :, :256], x_recv.at[2, d - 1])

    def weight_rows(i, carry):
        cols = pl.ds(pl.multiple_of(i * 512, 512), 512)
        part = dot(hlout[...].reshape(512, C), cotz[:, i].reshape(512, 512), 0, 0)
        gpart[:, :, :, cols] = part.reshape(NZ, 2, 8, 512)
        return carry

    lax.fori_loop(0, 4, weight_rows, 0)
    put(gpart.at[:, 1 - c], gpeer, core_send.at[2], core_recv.at[2], other)

    gather_got(0, lambda h: hl.at[:, head_cols(h)])
    for d in range(1, 4):
        tx = (x + d) % 4
        mpart[d - 1] = dot(
            hl[...], wbuf[:, pl.ds(pl.multiple_of(tx * 512, 512), 512)]
        ).astype(BF16)
        put(
            mpart.at[d - 1], mrecv.at[d - 1], x_send.at[1, d - 1], x_recv.at[1, d - 1],
            {"head": tx},
        )
    mown[...] = dot(hl[...], wbuf[:, cot_cols])

    got(gpeer, core_recv.at[2])

    def chip_rows(i, carry):
        part = gpart[i, c] + gpeer[i]
        zsend[i] = jnp.concatenate([part[:, :1024], part[:, 1024:]], axis=0).astype(BF16)
        return carry

    lax.fori_loop(0, NZ, chip_rows, 0)
    for d in range(NZ - 1, 0, -1):
        tz = (z + d) % NZ
        put(zsend.at[tz], zrecv.at[d - 1], gz_send.at[d - 1], gz_recv.at[d - 1], at(tz, y, c))

    outs = lockstep(
        [
            chunk_back_a(
                load("dmix", b), load("dread", b), load("keys", b), load("queries", b),
                load("inv", b), load("scores", b), load("mix", b), terms[b], q_scales[b],
            )
            for b in blocks
        ]
    )
    cums = [outs[b]["cum"] for b in blocks]
    for b in blocks:
        gout[0, b] = outs[b]["query"].astype(BF16)
        for name in ("dkb", "dlow", "dkey", "gap"):
            store(name, b, outs[b][name])
    targets = (dq_ref, dk_ref, dv_ref)

    def send_back(i):
        gather_back(1 + i, gout.at[i], lambda h: targets[i].at[:, head_cols(h)])

    send_back(0)

    lam[...] = jnp.zeros_like(lam)
    local_fc.wait()
    lam[3 * C :] = fcbuf[...].T
    for i in range(NZ - 1, 0, -1):

        @pl.when(i > z)
        def _():
            now = lam[...]
            high = mz[i, :C]
            lam[...] = dot(
                jnp.concatenate(split(now), axis=1), jnp.concatenate([high, high], axis=0)
            ) + now * mz[i, C:].astype(F32)[:1]

        for b in range(3):
            if not (i >> b) & 1:
                continue

            @pl.when((z < i) & (z // (2 << b) == i // (2 << b)))
            def _():
                got(dsz.at[i, b, rows_other], relb_recv.at[i, b])
                lam[b * C : (b + 1) * C] += dsz[i, b].astype(F32)

    d_chip_map = mm(lam[...], jnp.concatenate([zst[...], run_chip], axis=0), 0, 0)
    d_chip_add = lam[3 * C :]
    for b in range(3):
        d_chip_add = d_chip_add + jnp.where(bits[b], 0.0, lam[b * C : (b + 1) * C])
    d_chip_add = d_chip_add.T
    chip_pair = jnp.concatenate([d_chip_map, d_chip_add], axis=1)
    as_second = mm(chip_pair, jnp.concatenate([lo_map, lo_add], axis=1), 1, 1)
    through = mm(hi_map, chip_pair, 0, 0)
    as_first = through[:, :C] + mm(hi_dx[C:], chip_states, 0, 0)
    d_total = jnp.where(first, as_first, as_second)
    d_run4 = jnp.where(first, through[:, C:] + hi_dx[:C].T, d_chip_add)
    d_maps, d_adds = chain_back(
        d_total, d_run4, maps, adds[0], pres[0], pres[1], run2, run3, lift_grads, near_cots
    )

    @pl.when(jnp.logical_not(last))
    def _():
        got(fin_ref.at[y], f_recv.at[0])

    for d in range(1, NY):
        ty = (y + d) % NY
        put(fin_ref.at[y], fin_ref.at[y], f_send.at[NZ + d], f_recv.at[d], at(z, ty, c))

    flush(sent_early)
    pairs = lockstep(
        [
            chunk_back_b(
                d_maps[b], d_adds[b], load("keys", b), load("inv", b), load("weights", b),
                load("plain", b), load("dvb", b), load("dkb", b), terms[b],
            )
            for b in blocks
        ]
    )
    for b in blocks:
        gout[2, b] = pairs[b]["value"].astype(BF16)
    send_back(2)

    total = zsend[z].astype(F32)
    for d in range(1, NZ):
        got(zrecv.at[d - 1], gz_recv.at[d - 1])
        total = total + zrecv[d - 1].astype(F32)
    gsum[...] = jnp.concatenate([total[:8], total[8:]], axis=1)
    put(gsum, gw_ref, gp_send.at[0], gp_recv.at[0], rows_to, here=rows_stay)

    outs = lockstep(
        [
            chunk_back_c(
                d_maps[b], pairs[b]["dvb"], pairs[b]["dkb"], pairs[b]["dkt"], pairs[b]["back"],
                load("dlow", b), load("dkey", b), load("gap", b), cums[b], load("gram", b),
                load("keys", b), vin[b], load("weights", b), load("plain", b), terms[b],
                k_scales[b], gate_grads[b],
            )
            for b in blocks
        ]
    )
    for b in blocks:
        gout[1, b] = outs[b][0].astype(BF16)
        sout[b] = outs[b][1]
    send_back(1)
    gather_back(4, sout, lambda h: dsmall_ref.at[h])

    total = mown[...]
    for d in range(1, 4):
        got(mrecv.at[d - 1], x_recv.at[1, d - 1])
    for d in range(3):
        total = total + mrecv[d].astype(F32)
    mixed_ref[...] = total.astype(BF16)
    got(gw_ref, gp_recv.at[0])

    for d in range(1, NY):
        sy = (y + NY - d) % NY
        got(fin_ref.at[sy], f_recv.at[d])
    for i in range(3):
        gather_got(1 + i, lambda h, i=i: targets[i].at[:, head_cols(h)])
    gather_got(4, lambda h: dsmall_ref.at[h])
    flush(len(pending))


def finish_kernel(*refs):
    ins, small_ref = refs[:6], refs[6]
    outs, (rate_ref, decay_ref, gate_ref) = refs[7:13], refs[13:16]
    for i in range(6):
        outs[i][...] = ins[i][...].astype(outs[i].dtype)
    for h in range(NY):
        one = slice(h, h + 1)
        rate_ref[one] = small_ref[h, 0:1]
        decay_ref[one] = small_ref[h, 1:2]
        for i in range(NL):
            gate_ref[i, one] = small_ref[h, 2 + i : 3 + i]


def on_device(
    queries, key_vectors, values, write_rates, log_decay, level_gates, out_weight,
    out_cotangent, final_cotangent,
):
    vmem = pl.BlockSpec(memory_space=pltpu.VMEM)
    anywhere = pl.BlockSpec(memory_space=pl.ANY)
    sem = pltpu.SemaphoreType.DMA
    quad = pltpu.VMEM((NB, C, C), F32)
    mixed, dq, dk, dv, dsmall, gw, fin = pl.pallas_call(
        kernel,
        out_shape=[
            jax.ShapeDtypeStruct((C, 512), BF16),
            jax.ShapeDtypeStruct((C, 512), BF16),
            jax.ShapeDtypeStruct((C, 512), BF16),
            jax.ShapeDtypeStruct((C, 512), BF16),
            jax.ShapeDtypeStruct((4, 16, C), F32),
            jax.ShapeDtypeStruct((8, 2048), F32),
            jax.ShapeDtypeStruct((4, C, C), F32),
        ],
        in_specs=[anywhere] * 3 + [vmem] * 3 + [anywhere] * 3,
        out_specs=[vmem] + [anywhere] * 4 + [vmem] * 2,
        scratch_shapes=[
            quad, quad, quad, pltpu.VMEM((NB, 16, C), F32), pltpu.VMEM((NY, 16, C), F32), quad,
            pltpu.VMEM((4, C, 512), BF16),
            pltpu.VMEM((C, 512), F32),
            pltpu.VMEM((C, 512), BF16),
            pltpu.VMEM((NB, C, C), BF16),
            pltpu.VMEM((3, NB, C, C), BF16),
            pltpu.VMEM((NB, 16, C), F32),
            pltpu.VMEM((512, 2048), BF16),
            pltpu.VMEM((C, C), F32),
            pltpu.VMEM((2, C, C), F32),
            pltpu.VMEM((2, C, C), F32),
            pltpu.VMEM((NZ, C + 16, C), BF16),
            pltpu.VMEM((NZ, C, C), BF16),
            pltpu.VMEM((3 * C, C), F32),
            pltpu.VMEM((4 * C, C), F32),
            pltpu.VMEM((4 * C, C), F32),
            pltpu.VMEM((3, C, C), BF16),
            pltpu.VMEM((NZ, 3, C, C), BF16),
            pltpu.VMEM((4 * C, C), F32),
            pltpu.VMEM((NB, 4, C, 512), BF16),
            pltpu.VMEM((NZ, 2, 8, 2048), F32),
            pltpu.VMEM((NZ, 8, 2048), F32),
            pltpu.VMEM((8, 2048), F32),
            pltpu.VMEM((NZ, 16, 1024), BF16),
            pltpu.VMEM((NZ - 1, 16, 1024), BF16),
            pltpu.VMEM((C, 512), F32),
            pltpu.VMEM((3, C, 512), BF16),
            pltpu.VMEM((3, C, 512), BF16),
            sem((7, 4)), sem((7, 4)), sem((5, 4)), sem((5, 4)),
            sem((3, 3)), sem((3, 3)), sem((3,)), sem((3,)), sem((3,)),
            sem((3 * NZ,)), sem((NZ,)), sem((3 * NZ,)), sem((NZ,)),
            sem((3, NZ)), sem((NZ, 3)), sem((NZ, 3)), sem((NZ, 3)),
            sem((1,)), sem((1,)), sem((NZ - 1,)), sem((NZ - 1,)),
            sem((NZ + NY,)), sem((NY,)),
        ],
        compiler_params=pltpu.CompilerParams(
            collective_id=0, has_side_effects=True, vmem_limit_bytes=56 * 1024 * 1024
        ),
    )(
        key_vectors, queries, values, write_rates, log_decay, level_gates, out_weight,
        out_cotangent, final_cotangent,
    )
    whole = (mixed, dq, dk, dv, gw, fin)
    out = pl.pallas_call(
        finish_kernel,
        out_shape=[
            jax.ShapeDtypeStruct(part.shape, F32 if i else BF16) for i, part in enumerate(whole)
        ]
        + [
            jax.ShapeDtypeStruct((4, C), F32),
            jax.ShapeDtypeStruct((4, C), F32),
            jax.ShapeDtypeStruct((NL, 4, C), F32),
        ],
        in_specs=[vmem] * 7,
        out_specs=[vmem] * 9,
    )(*whole, dsmall)
    mixed, dq, dk, dv, gw, fin, d_rates, d_decay, d_gates = out
    return (mixed, dq, dk, dv, d_rates, d_decay, d_gates, gw, fin)


def solution(mesh):
    return jax.shard_map(
        on_device,
        mesh=mesh,
        in_specs=(
            P("ctx", "head"), P("ctx", "head"), P("ctx", "head"), P("head", "ctx"),
            P("head", "ctx"), P(None, "head", "ctx"), P("head", None), P("ctx", "head"),
            P("head", None, None),
        ),
        out_specs=(
            P("ctx", "head"), P("ctx", "head"), P("ctx", "head"), P("ctx", "head"),
            P("head", "ctx"), P("head", "ctx"), P(None, "head", "ctx"),
            P(("head", "ctx"), None), P("head", None, None),
        ),
        check_vma=False,
    )
```

```python
import functools

import jax
import jax.numpy as jnp
from jax import lax
from jax.experimental import pallas as pl
from jax.experimental.pallas import tpu as pltpu
from jax.sharding import PartitionSpec as P

F32 = jnp.float32
BF16 = jnp.bfloat16
C = 128
NZ, NY, NB, NL = 8, 4, 4, 8
MESH = pl.DeviceIdType.MESH


def split(x):
    high = x.astype(BF16)
    return high, (x - high.astype(F32)).astype(BF16)


SPLITS = {}


def split_once(x):
    if id(x) not in SPLITS:
        SPLITS[id(x)] = (x, split(x))
    return SPLITS[id(x)][1]


def dot(a, b, ca=1, cb=0, precision=None):
    return lax.dot_general(
        a, b, (((ca,), (cb,)), ((), ())), preferred_element_type=F32, precision=precision
    )


def mm(a, b, ca=1, cb=0):
    return mm_split(split_once(a), split_once(b), ca, cb)


def mm_split(a, b, ca=1, cb=0):
    (ah, al), (bh, bl) = a, b
    if bh.shape == (C, C):
        other = 1 - cb
        both = dot(
            jnp.concatenate([ah, al], axis=ca),
            jnp.concatenate(
                [
                    jnp.concatenate([bh, bl], axis=other),
                    jnp.concatenate([bl, bh], axis=other),
                ],
                axis=cb,
            ),
            ca, cb,
        )
        return both[:, :C] + both[:, C:]
    return dot(
        jnp.concatenate([ah, ah, al], axis=ca), jnp.concatenate([bh, bl, bh], axis=cb), ca, cb
    )


def iotas():
    return (
        lax.broadcasted_iota(jnp.int32, (C, C), 0),
        lax.broadcasted_iota(jnp.int32, (C, C), 1),
    )


def unit(x):
    scale = lax.rsqrt(jnp.sum(x * x, axis=1, keepdims=True) + 1e-6)
    return x * scale, scale


def unit_back(grad, vec, scale):
    return scale * (grad - vec * jnp.sum(vec * grad, axis=1, keepdims=True))


def token_terms(rows):
    row, col = iotas()
    upper = jnp.where(row <= col, 1.0, 0.0).astype(F32)
    cum = dot(rows, upper, precision=lax.Precision.HIGHEST)
    stacked = jnp.concatenate([rows, cum, jnp.zeros((C - 32, C), F32)], axis=0).T
    beta = stacked[:, 0:1]
    cum_col = stacked[:, 17:18]
    cum_row = cum[1:2, :]
    last = cum[1:2, C - 1 : C]
    decay = jnp.where(row >= col, jnp.exp(jnp.minimum(cum_col - cum_row, 0.0)), 0.0)
    return dict(
        beta=beta,
        gam=jnp.exp(cum_col),
        tail=jnp.exp(last - cum_col),
        glast=jnp.exp(last),
        shared={},
        gates=[stacked[:, 2 + i : 3 + i] for i in range(NL)],
        decay=decay,
    )


def inverses(lows):
    row, col = iotas()
    eye = jnp.where(row == col, 1.0, 0.0).astype(F32)
    ones = [jnp.where((row >> 3) == (col >> 3), -low, 0.0) for low in lows]
    twos = [mm(n, n) for n in ones]
    fours = [mm(n, n) for n in twos]
    invs = [eye + n + m + mm(n, m) for n, m in zip(ones, twos)]
    invs = [inv + mm(inv, m) for inv, m in zip(invs, fours)]
    for bit in (3, 5):
        here = ((row >> (bit + 2)) == (col >> (bit + 2))) & ((row >> bit) != (col >> bit))
        rests = [-mm(jnp.where(here, low, 0.0), inv) for low, inv in zip(lows, invs)]
        squares = [mm(rest, rest) for rest in rests]
        invs = [inv + mm(inv, rest) for inv, rest in zip(invs, rests)]
        invs = [inv + mm(inv, square) for inv, square in zip(invs, squares)]
    return invs


def gate_matrix(tt):
    row, col = iotas()
    return jnp.where((row >> 6) == (col >> 6), tt["gates"][0], tt["gates"][1])


def lockstep(runs):
    results = [None] * len(runs)
    alive = list(range(len(runs)))
    while alive:
        for i in list(alive):
            try:
                next(runs[i])
            except StopIteration as stop:
                results[i] = stop.value
                alive.remove(i)
    return results


def scaled(tt, name, keys=None, values=None):
    shared = tt["shared"]
    if name not in shared:
        if name == "kb":
            shared[name] = tt["beta"] * tt["gam"] * keys
        elif name == "vb":
            shared[name] = tt["beta"] * values
        elif name == "kt":
            shared[name] = tt["tail"] * keys
        else:
            shared[name] = gate_matrix(tt)
    return shared[name]


def chunk_states(keys, values, inv, tt):
    row, col = iotas()
    pair = mm(
        inv,
        jnp.concatenate([scaled(tt, "kb", keys), scaled(tt, "vb", values=values)], axis=1),
    )
    yield
    both = mm(scaled(tt, "kt", keys), pair, 0, 0)
    yield
    return dict(
        weights=pair[:, :C], plain=pair[:, C:], add=both[:, C:],
        map=jnp.where(row == col, tt["glast"], 0.0) - both[:, :C],
    )


def chunk_reads(keys, queries, values, inv, tt):
    scores = mm(queries, keys, 1, 1) * tt["decay"]
    yield
    mix = mm(scores, inv)
    yield
    reader = tt["gam"] * queries - mm(mix, scaled(tt, "kb"))
    yield
    gated = scaled(tt, "gate") * mix
    tt["shared"]["gated"] = gated
    near = mm(gated, scaled(tt, "vb"))
    yield
    return dict(scores=scores, mix=mix, reader=reader, near=near)


def near_back(hg, values, mix, tt):
    row, col = iotas()
    gate = scaled(tt, "gate")
    cross = mm(hg, scaled(tt, "vb"), 1, 1)
    yield
    d_vb = mm(scaled(tt, "gated"), hg, 0, 0)
    yield
    gated = cross * mix
    same = (row >> 6) == (col >> 6)
    d_g0 = jnp.sum(jnp.where(same, gated, 0.0), axis=1, keepdims=True)
    d_g1 = jnp.sum(jnp.where(same, 0.0, gated), axis=1, keepdims=True)
    return dict(d_g0=d_g0, d_g1=d_g1, dvb=d_vb, dmix=cross * gate)


def chunk_back_a(d_mix, d_reader, keys, queries, inv, scores, mix, tt, q_scale):
    gam, decay = tt["gam"], tt["decay"]
    row, col = iotas()
    d_mix = d_mix - mm(d_reader, scaled(tt, "kb"), 1, 1)
    yield
    d_kb = -mm(mix, d_reader, 0, 0)
    yield
    d_scores = jnp.where(row >= col, mm(d_mix, inv, 1, 1), 0.0)
    yield
    d_qk = d_scores * decay
    d_query = mm(d_qk, keys) + gam * d_reader
    yield
    d_low = mm(mix, d_scores, 0, 0)
    yield
    d_key = mm(d_qk, queries, 0, 0)
    yield
    cum = gam * jnp.sum(d_reader * queries, axis=1, keepdims=True)
    return dict(
        dkb=d_kb, dlow=d_low, dkey=d_key, gap=d_scores * scores, cum=cum,
        query=unit_back(d_query, queries, q_scale),
    )


def chunk_back_b(d_map, d_add, keys, inv, weights, plain, d_vb, d_kb, tt):
    grads = jnp.concatenate([d_add, -d_map], axis=1)
    d_pw = mm(scaled(tt, "kt"), grads)
    yield
    d_kt = mm(jnp.concatenate([plain, weights], axis=1), grads, 1, 1)
    yield
    back = mm(inv, d_pw, 0, 0)
    yield
    d_vb = d_vb + back[:, :C]
    return dict(dvb=d_vb, dkb=d_kb + back[:, C:], dkt=d_kt, back=back, value=tt["beta"] * d_vb)


def chunk_back_c(
    d_map, d_vb, d_kb, d_kt, back, d_low, d_key, gap, cum, gram, keys, values, weights, plain, tt,
    k_scale, gate_grads,
):
    beta, gam, tail, decay = tt["beta"], tt["gam"], tt["tail"], tt["decay"]
    row, col = iotas()
    d_low = d_low + mm(back, jnp.concatenate([plain, weights], axis=1), 1, 1)
    yield
    d_low = jnp.where(row > col, -d_low, 0.0) * decay
    d_gram = beta * d_low
    d_key = d_key + mm(d_gram + d_gram.T, keys) + beta * gam * d_kb + tail * d_kt
    yield
    dk_gram = d_low * gram
    d_gap = gap + beta * dk_gram
    kb_k = jnp.sum(d_kb * keys, axis=1, keepdims=True)
    d_beta = jnp.sum(dk_gram + d_vb * values, axis=1, keepdims=True) + gam * kb_k
    tail_part = tail * jnp.sum(d_kt * keys, axis=1, keepdims=True)
    d_cum = cum + gam * beta * kb_k - tail_part + jnp.sum(d_gap, axis=1, keepdims=True)
    d_last = jnp.sum(tail_part, axis=0, keepdims=True) + tt["glast"] * jnp.sum(
        jnp.sum(jnp.where(row == col, d_map, 0.0), axis=1, keepdims=True), axis=0, keepdims=True
    )
    lane = lax.broadcasted_iota(jnp.int32, (1, C), 1)
    d_cum_row = jnp.where(lane == C - 1, d_last, 0.0) - jnp.sum(d_gap, axis=0, keepdims=True)
    cols = jnp.where(col == 0, d_beta, 0.0) + jnp.where(col == 1, d_cum, 0.0)
    for i in range(NL):
        cols = cols + jnp.where(col == 2 + i, gate_grads[i], 0.0)
    rows = cols.T[:16, :]
    at = lax.broadcasted_iota(jnp.int32, (16, C), 0)
    rows = rows + jnp.where(at == 1, d_cum_row, 0.0)
    lower = jnp.where(row >= col, 1.0, 0.0).astype(F32)
    rows = jnp.where(at == 1, dot(rows, lower, precision=lax.Precision.HIGHEST), rows)
    return unit_back(d_key, keys, k_scale), rows


def chunk_chain(maps, adds):
    one = jnp.concatenate([maps[0], adds[0]], axis=1)
    two = mm(maps[1], one)
    run2 = two[:, C:] + adds[1]
    three = mm(maps[2], jnp.concatenate([two[:, :C], run2], axis=1))
    moved = three[:, C:]
    run3 = moved + adds[2]
    four = mm(maps[3], jnp.concatenate([three[:, :C], run3], axis=1))
    return [two[:, :C], three[:, :C], four[:, :C]], run2, moved, run3, four[:, C:] + adds[3]


def chain_back(d_total, d_run4, maps, add0, pre2, pre3, run2, run3, lift_grads, near):
    pair = jnp.concatenate([d_total, d_run4], axis=1)
    d_map3 = mm(pair, jnp.concatenate([pre3, run3], axis=1), 1, 1)
    d_add3 = d_run4
    down = mm(maps[3], pair, 0, 0)
    d_pre3 = down[:, :C] + lift_grads[2]
    d_run3 = down[:, C:]
    d_add2 = d_run3 + near["add2"]
    pair = jnp.concatenate([d_pre3, d_run3 + near["moved"]], axis=1)
    d_map2 = mm(pair, jnp.concatenate([pre2, run2], axis=1), 1, 1)
    down = mm(maps[2], pair, 0, 0)
    d_pre2 = down[:, :C] + lift_grads[1]
    d_run2 = down[:, C:] + near["run2"]
    pair = jnp.concatenate([d_pre2, d_run2], axis=1)
    d_map1 = mm(pair, jnp.concatenate([maps[0], add0], axis=1), 1, 1)
    down = mm(maps[1], pair, 0, 0)
    d_map0 = down[:, :C] + lift_grads[0]
    d_add0 = down[:, C:] + near["add0"]
    return [d_map0, d_map1, d_map2, d_map3], [d_add0, d_run2, d_add2, d_add3]


def kernel(
    k_ref, q_ref, v_ref, rate_ref, decay_ref, gate_ref, w_ref, cot_ref, fcot_ref,
    mixed_ref, dq_ref, dk_ref, dv_ref, dsmall_ref, gw_ref, fin_ref,
    kin, qin, vin, sin, spack, hgin, cot, hg, hl, hlout, gout, sout, wbuf, fcbuf,
    own, peer, mz, az, zst, dxo, dxp, dsc, dsz, lam,
    cotz, gpart, gpeer, gsum, zsend, zrecv, mown, mpart, mrecv,
    in_send, in_recv, out_send, out_recv, x_send, x_recv, loc, core_send, core_recv,
    zf_send, zf_recv, rel_send, rel_recv, zb_send, zb_recv, relb_send, relb_recv,
    gp_send, gp_recv, gz_send, gz_recv, f_send, f_recv,
):
    SPLITS.clear()
    me = lax.axis_index("ctx")
    x = lax.axis_index("head")
    z, y, c = me // 8, (me // 2) % 4, me % 2
    pending = []

    def flush(count):
        for finish in pending[:count]:
            finish()
        del pending[:count]


    def at(zz, yy, cc):
        return {"ctx": (zz * 4 + yy) * 2 + cc}

    def remote(src, dst, send, recv, target):
        return pltpu.make_async_remote_copy(
            src_ref=src, dst_ref=dst, send_sem=send, recv_sem=recv,
            device_id=target, device_id_type=MESH,
        )

    def put(src, dst, send, recv, target, here=None, when=None):
        copy = remote(src, dst, send, recv, target)
        cond = when
        if here is not None:
            cond = jnp.logical_not(here)

            @pl.when(here)
            def _():
                pltpu.make_async_copy(src, dst, recv).start()

        if cond is None:
            copy.start()
            pending.append(copy.wait_send)
        else:

            @pl.when(cond)
            def _():
                copy.start()

            def finish():
                @pl.when(cond)
                def _():
                    copy.wait_send()

            pending.append(finish)

    def got(dst, sem):
        pltpu.make_async_copy(dst, dst, sem).wait()

    def head_cols(i):
        return pl.ds(pl.multiple_of(i * C, C), C)

    local_w = pltpu.make_async_copy(w_ref, wbuf, loc.at[1])
    local_w.start()
    local_fc = pltpu.make_async_copy(fcot_ref.at[y], fcbuf, loc.at[2])
    local_fc.start()
    for h in range(NY):
        one = slice(h, h + 1)
        spack[h] = jnp.concatenate(
            [rate_ref[one], decay_ref[one]]
            + [gate_ref[i, one] for i in range(NL)]
            + [jnp.zeros((6, C), F32)],
            axis=0,
        )

    barrier = pltpu.get_barrier_semaphore()
    for dy in range(NY):
        for dc in range(2):
            if dy or dc:
                pl.semaphore_signal(
                    barrier, inc=1, device_id=at(z, (y + dy) % NY, (c + dc) % 2), device_id_type=MESH
                )
    for dz in range(1, NZ):
        pl.semaphore_signal(barrier, inc=1, device_id=at((z + dz) % NZ, y, c), device_id_type=MESH)
    for dx in range(1, 4):
        pl.semaphore_signal(barrier, inc=1, device_id={"head": (x + dx) % 4}, device_id_type=MESH)
    rows_from = at((z % 2) * 4 + y, z // 2, c)
    rows_to = at(2 * y + z // 4, z % 4, c)
    rows_stay = rows_to["ctx"] == me

    @pl.when(jnp.logical_not(rows_stay))
    def _():
        pl.semaphore_signal(barrier, inc=1, device_id=rows_from, device_id_type=MESH)

    pl.semaphore_wait(barrier, jnp.where(rows_stay, 17, 18))

    slot = (y % 2) * 2 + c
    half = y // 2

    def spread(idx, src_of, dst):
        for d in range(NY):
            h = (y + d) % NY
            put(
                src_of(h), dst(slot), in_send.at[idx, d], in_recv.at[idx, slot],
                at(z, h, half), here=(c == half) if d == 0 else None,
            )

    def spread_got(idx, dst):
        for b in range(NB):
            got(dst(b), in_recv.at[idx, b])

    cot_cols = pl.ds(pl.multiple_of(x * 512, 512), 512)
    kin_at, qin_at, vin_at = (lambda b: kin.at[b]), (lambda b: qin.at[b]), (lambda b: vin.at[b])
    sin_at, hgin_at = (lambda b: sin.at[b]), (lambda b: hgin.at[b])

    def cotz_at(b):
        return cotz.at[b, x, :, :256]

    def cotz_rest(b):
        return cotz.at[b, :, :, 256:]

    def gather_back(idx, src, dst_of):
        for b in range(NB):
            ty, tc = 2 * c + b // 2, b % 2
            put(
                src.at[b], dst_of(y), out_send.at[idx, b], out_recv.at[idx, y],
                at(z, ty, tc), here=(ty == y) & (tc == c),
            )

    def gather_got(idx, dst_of):
        for h in range(NY):
            got(dst_of(h), out_recv.at[idx, h])

    spread(1, lambda h: spack.at[h], sin_at)
    spread(0, lambda h: k_ref.at[:, head_cols(h)], kin_at)
    for d in range(1, 4):
        put(
            cot_ref, cot.at[x], x_send.at[0, d - 1], x_recv.at[0, d - 1], {"head": (x + d) % 4},
        )
    local_cot = pltpu.make_async_copy(cot_ref, cot.at[x], loc.at[0])
    local_cot.start()

    held = {}

    def load(name, b):
        return held[name, b]

    def store(name, b, value):
        held[name, b] = value

    row, col = iotas()
    blocks = range(NB)

    spread_got(1, sin_at)
    terms = [token_terms(sin[b]) for b in blocks]
    spread_got(0, kin_at)
    spread(3, lambda h: v_ref.at[:, head_cols(h)], vin_at)
    spread(2, lambda h: q_ref.at[:, head_cols(h)], qin_at)
    lows, k_scales = [], []
    for b in blocks:
        keys, scale = unit(kin[b])
        k_scales.append(scale)
        store("keys", b, keys)
        gram = mm(keys, keys, 1, 1)
        store("gram", b, gram)
        lows.append(jnp.where(row > col, terms[b]["beta"] * terms[b]["decay"] * gram, 0.0))
    for b, inv in enumerate(inverses(lows)):
        store("inv", b, inv)

    spread_got(3, vin_at)
    outs = lockstep([chunk_states(load("keys", b), vin[b], load("inv", b), terms[b]) for b in blocks])
    for b in blocks:
        for name in outs[b]:
            store(name, b, outs[b][name])
    maps = [load("map", b) for b in blocks]
    adds = [load("add", b) for b in blocks]
    pres, run2, moved, run3, run4 = chunk_chain(maps, adds)
    own[0] = pres[2]
    own[1] = run4
    other = at(z, y, 1 - c)
    put(own, peer, core_send.at[0], core_recv.at[0], other)

    local_cot.wait()
    for d in range(1, 4):
        got(cot.at[(x + 4 - d) % 4], x_recv.at[0, d - 1])
    local_w.wait()
    total = dot(cot[0], wbuf[:, :512], 1, 1)
    for i in range(1, 4):
        total = total + dot(cot[i], wbuf[:, 512 * i : 512 * i + 512], 1, 1)
    hg[...] = total
    spread(4, lambda h: hg.at[:, head_cols(h)], hgin_at)
    spread(5, lambda h: cot_ref.at[:, :256], cotz_at)

    got(peer, core_recv.at[0])
    first = c == 0
    lo_map = jnp.where(first, own[0], peer[0])
    lo_add = jnp.where(first, own[1], peer[1])
    hi_map = jnp.where(first, peer[0], own[0])
    hi_add = jnp.where(first, peer[1], own[1])
    both = mm(hi_map, jnp.concatenate([lo_map, lo_add], axis=1))
    chip_map, chip_add = both[:, :C], both[:, C:] + hi_add
    high = chip_map.astype(BF16)
    rest = jnp.sum(
        jnp.where(row == col, chip_map - high.astype(F32), 0.0), axis=0, keepdims=True
    )
    mz[z, :C] = high
    mz[z, C:] = jnp.broadcast_to(rest, (16, C)).astype(BF16)
    az[z] = chip_add.T.astype(BF16)
    second = c == 1
    for d in range(NZ - 1, 0, -1):
        tz = z + d
        up = tz < NZ
        put(mz.at[z], mz.at[z], zf_send.at[d], zf_recv.at[z], at(tz % NZ, y, c), when=up & first)
        put(az.at[z], az.at[z], zf_send.at[NZ + d], zf_recv.at[z], at(tz % NZ, y, c), when=up & second)
    for d in range(1, NZ):
        tz = z - d
        put(
            mz.at[z], mz.at[z], zf_send.at[2 * NZ + d], zf_recv.at[z], at((tz + NZ) % NZ, y, c),
            when=(tz >= 0) & first,
        )

    spread_got(2, qin_at)
    q_scales = []
    for b in blocks:
        queries, scale = unit(qin[b])
        q_scales.append(scale)
        store("queries", b, queries)
    outs = lockstep(
        [
            chunk_reads(load("keys", b), load("queries", b), vin[b], load("inv", b), terms[b])
            for b in blocks
        ]
    )
    for b in blocks:
        for name in outs[b]:
            store(name, b, outs[b][name])
    store("lift", 0, load("reader", 0))
    for b in (1, 2, 3):
        store("lift", b, mm(load("reader", b), maps[0] if b == 1 else pres[b - 2]))

    spread_got(4, hgin_at)
    d_states = jnp.zeros((4 * C, C), F32)
    for b in blocks:
        turned = hgin[b].T
        weighted = jnp.concatenate(
            [turned * sin[b, 6 + i : 7 + i] for i in range(4)], axis=0
        )
        d_states = d_states + mm(weighted, load("lift", b))
    dxo[...] = d_states
    put(dxo, dxp, core_send.at[1], core_recv.at[1], other)
    sent_early = len(pending)
    spread_got(5, cotz_at)
    for d in range(1, 4):
        put(
            cotz.at[:, x, :, :256], cotz.at[:, x, :, :256], x_send.at[2, d - 1],
            x_recv.at[2, d - 1], {"head": (x + d) % 4},
        )
    spread(6, lambda h: cot.at[:, :, 256:], cotz_rest)

    for b, state, gate in ((1, adds[0], 2), (2, run2, 3), (3, adds[2], 2), (3, moved, 3)):
        store(
            "near", b,
            load("near", b) + terms[b]["gates"][gate] * mm(load("reader", b), state),
        )

    bits = [(z // (1 << b)) % 2 == 1 for b in range(3)]
    starts = [(z // (2 << b)) * (2 << b) for b in range(3)]
    got(dxp, core_recv.at[1])
    lo_dx = jnp.where(first, dxo[...], dxp[...])
    hi_dx = jnp.where(first, dxp[...], dxo[...])
    d_chip = lo_dx[C:] + mm(hi_dx[C:], lo_map)
    for b in range(3):
        dsc[b] = d_chip[b * C : (b + 1) * C].astype(BF16)
    rows_mine = pl.ds(pl.multiple_of(c * 64, 64), 64)
    rows_other = pl.ds(pl.multiple_of((1 - c) * 64, 64), 64)
    for b in (2, 1, 0):
        for d in range((2 << b) - 1, 0, -1):
            tz = z - d
            put(
                dsc.at[b, rows_mine], dsz.at[z, b, rows_mine], zb_send.at[b, d],
                zb_recv.at[z, b], at((tz + NZ) % NZ, y, c), when=bits[b] & (tz >= starts[b]),
            )

    outs = lockstep([near_back(hgin[b], vin[b], load("mix", b), terms[b]) for b in blocks])
    gate_grads = []
    for b in blocks:
        store("dvb", b, outs[b]["dvb"])
        store("dmix", b, outs[b]["dmix"])
        gate_grads.append([outs[b]["d_g0"], outs[b]["d_g1"]] + [jnp.zeros((C, 1), F32)] * 6)
    near_reads = [jnp.zeros((C, C), F32)] * NB
    near_cots = {}
    for b, state, gate, name in (
        (1, adds[0], 2, "add0"), (2, run2, 3, "run2"), (3, adds[2], 2, "add2"), (3, moved, 3, "moved"),
    ):
        weight = terms[b]["gates"][gate]
        part = mm(hgin[b], state, 1, 1)
        reader = load("reader", b)
        gate_grads[b][gate] = jnp.sum(part * reader, axis=1, keepdims=True)
        near_reads[b] = near_reads[b] + weight * part
        near_cots[name] = mm(reader, weight * hgin[b], 0, 0)
    for b in blocks:
        store("dread", b, near_reads[b])
    flush(sent_early)

    for j in range(NZ - 1):

        @pl.when((j < z) & first)
        def _():
            got(mz.at[j], zf_recv.at[j])

        @pl.when((j < z) & second)
        def _():
            got(az.at[j], zf_recv.at[j])

        put(mz.at[j], mz.at[j], rel_send.at[j], rel_recv.at[j], other, when=(j < z) & first)
        put(az.at[j], az.at[j], rel_send.at[NZ + j], rel_recv.at[j], other, when=(j < z) & second)

    zst[...] = jnp.zeros_like(zst)

    def step(j, carry):
        @pl.when(first)
        def _():
            got(az.at[j], rel_recv.at[j])

        @pl.when(second)
        def _():
            got(mz.at[j], rel_recv.at[j])

        now = zst[...]
        high = mz[j, :C]
        new = dot(
            jnp.concatenate(split(now), axis=1), jnp.concatenate([high, high], axis=1), 1, 1
        ) + now * mz[j, C:].astype(F32)[:1]
        add = az[j].astype(F32)
        for b in range(3):
            inside = (j >= starts[b]) & (j < starts[b] + (1 << b))
            zst[b * C : (b + 1) * C] = new[b * C : (b + 1) * C] + jnp.where(inside, add, 0.0)
        return carry

    lax.fori_loop(0, z, step, 0)
    reads = [jnp.where(bits[b], zst[b * C : (b + 1) * C], 0.0) for b in range(3)]
    chip_states = jnp.concatenate(reads, axis=0)
    run_chip = reads[0] + reads[1] + reads[2]

    lower = mm(chip_states, lo_map, 1, 1)
    states = jnp.concatenate(
        [jnp.where(first, 0.0, lo_add.T), jnp.where(first, chip_states, lower)], axis=0
    )
    for b in blocks:
        reads_b = mm(load("lift", b), states, 1, 1)
        total = load("near", b)
        for i in range(4):
            total = total + terms[b]["gates"][4 + i] * reads_b[:, i * C : (i + 1) * C]
        hlout[b] = total.astype(BF16)
    gather_back(0, hlout, lambda h: hl.at[:, head_cols(h)])

    last = z == NZ - 1

    @pl.when(last)
    def _():
        fin_ref[y] = mm_split(split(run_chip), split(chip_map), 1, 1).T + chip_add

    for d in range(1, NZ):
        put(
            fin_ref.at[y], fin_ref.at[y], f_send.at[d], f_recv.at[0],
            at(NZ - 1 - d, y, c), when=last,
        )

    prefixes = [None, maps[0], pres[0], pres[1]]
    state_cols = jnp.concatenate([states[i * C : (i + 1) * C] for i in range(4)], axis=1)
    lift_grads = []
    backs = [mm(hgin[b], state_cols) for b in blocks]
    for b in blocks:
        lift = load("lift", b)
        d_lift = jnp.zeros((C, C), F32)
        for i in range(4):
            part = backs[b][:, i * C : (i + 1) * C]
            gate_grads[b][4 + i] = jnp.sum(part * lift, axis=1, keepdims=True)
            d_lift = d_lift + terms[b]["gates"][4 + i] * part
        if b:
            store("dread", b, load("dread", b) + mm(d_lift, prefixes[b], 1, 1))
            lift_grads.append(mm(load("reader", b), d_lift, 0, 0))
        else:
            store("dread", b, d_lift)

    for i in range(NZ - 1, 0, -1):
        for b in range(3):
            if not (i >> b) & 1:
                continue
            wanted = (z < i) & (z // (2 << b) == i // (2 << b))

            @pl.when(wanted)
            def _():
                got(dsz.at[i, b, rows_mine], zb_recv.at[i, b])

            put(
                dsz.at[i, b, rows_mine], dsz.at[i, b, rows_mine], relb_send.at[i, b],
                relb_recv.at[i, b], other, when=wanted,
            )

    for i in range(1, NZ):

        @pl.when((i > z) & first)
        def _():
            got(mz.at[i], zf_recv.at[i])

        put(mz.at[i], mz.at[i], rel_send.at[2 * NZ + i], rel_recv.at[i], other, when=(i > z) & first)

        @pl.when((i > z) & second)
        def _():
            got(mz.at[i], rel_recv.at[i])

    sent_early = len(pending)

    spread_got(6, cotz_rest)
    for d in range(1, 4):
        got(cotz.at[:, (x + 4 - d) % 4, :, :256], x_recv.at[2, d - 1])

    def weight_rows(i, carry):
        cols = pl.ds(pl.multiple_of(i * 512, 512), 512)
        part = dot(hlout[...].reshape(512, C), cotz[:, i].reshape(512, 512), 0, 0)
        gpart[:, :, :, cols] = part.reshape(NZ, 2, 8, 512)
        return carry

    lax.fori_loop(0, 4, weight_rows, 0)
    put(gpart.at[:, 1 - c], gpeer, core_send.at[2], core_recv.at[2], other)

    gather_got(0, lambda h: hl.at[:, head_cols(h)])
    for d in range(1, 4):
        tx = (x + d) % 4
        mpart[d - 1] = dot(
            hl[...], wbuf[:, pl.ds(pl.multiple_of(tx * 512, 512), 512)]
        ).astype(BF16)
        put(
            mpart.at[d - 1], mrecv.at[d - 1], x_send.at[1, d - 1], x_recv.at[1, d - 1],
            {"head": tx},
        )
    mown[...] = dot(hl[...], wbuf[:, cot_cols])

    got(gpeer, core_recv.at[2])

    def chip_rows(i, carry):
        part = gpart[i, c] + gpeer[i]
        zsend[i] = jnp.concatenate([part[:, :1024], part[:, 1024:]], axis=0).astype(BF16)
        return carry

    lax.fori_loop(0, NZ, chip_rows, 0)
    for d in range(NZ - 1, 0, -1):
        tz = (z + d) % NZ
        put(zsend.at[tz], zrecv.at[d - 1], gz_send.at[d - 1], gz_recv.at[d - 1], at(tz, y, c))

    outs = lockstep(
        [
            chunk_back_a(
                load("dmix", b), load("dread", b), load("keys", b), load("queries", b),
                load("inv", b), load("scores", b), load("mix", b), terms[b], q_scales[b],
            )
            for b in blocks
        ]
    )
    cums = [outs[b]["cum"] for b in blocks]
    for b in blocks:
        gout[0, b] = outs[b]["query"].astype(BF16)
        for name in ("dkb", "dlow", "dkey", "gap"):
            store(name, b, outs[b][name])
    targets = (dq_ref, dk_ref, dv_ref)

    def send_back(i):
        gather_back(1 + i, gout.at[i], lambda h: targets[i].at[:, head_cols(h)])

    send_back(0)

    lam[...] = jnp.zeros_like(lam)
    local_fc.wait()
    lam[3 * C :] = fcbuf[...].T
    for i in range(NZ - 1, 0, -1):

        @pl.when(i > z)
        def _():
            now = lam[...]
            high = mz[i, :C]
            lam[...] = dot(
                jnp.concatenate(split(now), axis=1), jnp.concatenate([high, high], axis=0)
            ) + now * mz[i, C:].astype(F32)[:1]

        for b in range(3):
            if not (i >> b) & 1:
                continue

            @pl.when((z < i) & (z // (2 << b) == i // (2 << b)))
            def _():
                got(dsz.at[i, b, rows_other], relb_recv.at[i, b])
                lam[b * C : (b + 1) * C] += dsz[i, b].astype(F32)

    d_chip_map = mm(lam[...], jnp.concatenate([zst[...], run_chip], axis=0), 0, 0)
    d_chip_add = lam[3 * C :]
    for b in range(3):
        d_chip_add = d_chip_add + jnp.where(bits[b], 0.0, lam[b * C : (b + 1) * C])
    d_chip_add = d_chip_add.T
    chip_pair = jnp.concatenate([d_chip_map, d_chip_add], axis=1)
    as_second = mm(chip_pair, jnp.concatenate([lo_map, lo_add], axis=1), 1, 1)
    through = mm(hi_map, chip_pair, 0, 0)
    as_first = through[:, :C] + mm(hi_dx[C:], chip_states, 0, 0)
    d_total = jnp.where(first, as_first, as_second)
    d_run4 = jnp.where(first, through[:, C:] + hi_dx[:C].T, d_chip_add)
    d_maps, d_adds = chain_back(
        d_total, d_run4, maps, adds[0], pres[0], pres[1], run2, run3, lift_grads, near_cots
    )

    @pl.when(jnp.logical_not(last))
    def _():
        got(fin_ref.at[y], f_recv.at[0])

    for d in range(1, NY):
        ty = (y + d) % NY
        put(fin_ref.at[y], fin_ref.at[y], f_send.at[NZ + d], f_recv.at[d], at(z, ty, c))

    flush(sent_early)
    pairs = lockstep(
        [
            chunk_back_b(
                d_maps[b], d_adds[b], load("keys", b), load("inv", b), load("weights", b),
                load("plain", b), load("dvb", b), load("dkb", b), terms[b],
            )
            for b in blocks
        ]
    )
    for b in blocks:
        gout[2, b] = pairs[b]["value"].astype(BF16)
    send_back(2)

    total = zsend[z].astype(F32)
    for d in range(1, NZ):
        got(zrecv.at[d - 1], gz_recv.at[d - 1])
        total = total + zrecv[d - 1].astype(F32)
    gsum[...] = jnp.concatenate([total[:8], total[8:]], axis=1)
    put(gsum, gw_ref, gp_send.at[0], gp_recv.at[0], rows_to, here=rows_stay)

    outs = lockstep(
        [
            chunk_back_c(
                d_maps[b], pairs[b]["dvb"], pairs[b]["dkb"], pairs[b]["dkt"], pairs[b]["back"],
                load("dlow", b), load("dkey", b), load("gap", b), cums[b], load("gram", b),
                load("keys", b), vin[b], load("weights", b), load("plain", b), terms[b],
                k_scales[b], gate_grads[b],
            )
            for b in blocks
        ]
    )
    for b in blocks:
        gout[1, b] = outs[b][0].astype(BF16)
        sout[b] = outs[b][1]
    send_back(1)
    gather_back(4, sout, lambda h: dsmall_ref.at[h])

    total = mown[...]
    for d in range(1, 4):
        got(mrecv.at[d - 1], x_recv.at[1, d - 1])
    for d in range(3):
        total = total + mrecv[d].astype(F32)
    mixed_ref[...] = total.astype(BF16)
    got(gw_ref, gp_recv.at[0])

    for d in range(1, NY):
        sy = (y + NY - d) % NY
        got(fin_ref.at[sy], f_recv.at[d])
    for i in range(3):
        gather_got(1 + i, lambda h, i=i: targets[i].at[:, head_cols(h)])
    gather_got(4, lambda h: dsmall_ref.at[h])
    flush(len(pending))


def finish_kernel(*refs):
    ins, small_ref = refs[:6], refs[6]
    outs, (rate_ref, decay_ref, gate_ref) = refs[7:13], refs[13:16]
    for i in range(6):
        outs[i][...] = ins[i][...].astype(outs[i].dtype)
    for h in range(NY):
        one = slice(h, h + 1)
        rate_ref[one] = small_ref[h, 0:1]
        decay_ref[one] = small_ref[h, 1:2]
        for i in range(NL):
            gate_ref[i, one] = small_ref[h, 2 + i : 3 + i]


def on_device(
    queries, key_vectors, values, write_rates, log_decay, level_gates, out_weight,
    out_cotangent, final_cotangent,
):
    vmem = pl.BlockSpec(memory_space=pltpu.VMEM)
    anywhere = pl.BlockSpec(memory_space=pl.ANY)
    sem = pltpu.SemaphoreType.DMA
    quad = pltpu.VMEM((NB, C, C), F32)
    mixed, dq, dk, dv, dsmall, gw, fin = pl.pallas_call(
        kernel,
        out_shape=[
            jax.ShapeDtypeStruct((C, 512), BF16),
            jax.ShapeDtypeStruct((C, 512), BF16),
            jax.ShapeDtypeStruct((C, 512), BF16),
            jax.ShapeDtypeStruct((C, 512), BF16),
            jax.ShapeDtypeStruct((4, 16, C), F32),
            jax.ShapeDtypeStruct((8, 2048), F32),
            jax.ShapeDtypeStruct((4, C, C), F32),
        ],
        in_specs=[anywhere] * 3 + [vmem] * 3 + [anywhere] * 3,
        out_specs=[vmem] + [anywhere] * 4 + [vmem] * 2,
        scratch_shapes=[
            quad, quad, quad, pltpu.VMEM((NB, 16, C), F32), pltpu.VMEM((NY, 16, C), F32), quad,
            pltpu.VMEM((4, C, 512), BF16),
            pltpu.VMEM((C, 512), F32),
            pltpu.VMEM((C, 512), BF16),
            pltpu.VMEM((NB, C, C), BF16),
            pltpu.VMEM((3, NB, C, C), BF16),
            pltpu.VMEM((NB, 16, C), F32),
            pltpu.VMEM((512, 2048), BF16),
            pltpu.VMEM((C, C), F32),
            pltpu.VMEM((2, C, C), F32),
            pltpu.VMEM((2, C, C), F32),
            pltpu.VMEM((NZ, C + 16, C), BF16),
            pltpu.VMEM((NZ, C, C), BF16),
            pltpu.VMEM((3 * C, C), F32),
            pltpu.VMEM((4 * C, C), F32),
            pltpu.VMEM((4 * C, C), F32),
            pltpu.VMEM((3, C, C), BF16),
            pltpu.VMEM((NZ, 3, C, C), BF16),
            pltpu.VMEM((4 * C, C), F32),
            pltpu.VMEM((NB, 4, C, 512), BF16),
            pltpu.VMEM((NZ, 2, 8, 2048), F32),
            pltpu.VMEM((NZ, 8, 2048), F32),
            pltpu.VMEM((8, 2048), F32),
            pltpu.VMEM((NZ, 16, 1024), BF16),
            pltpu.VMEM((NZ - 1, 16, 1024), BF16),
            pltpu.VMEM((C, 512), F32),
            pltpu.VMEM((3, C, 512), BF16),
            pltpu.VMEM((3, C, 512), BF16),
            sem((7, 4)), sem((7, 4)), sem((5, 4)), sem((5, 4)),
            sem((3, 3)), sem((3, 3)), sem((3,)), sem((3,)), sem((3,)),
            sem((3 * NZ,)), sem((NZ,)), sem((3 * NZ,)), sem((NZ,)),
            sem((3, NZ)), sem((NZ, 3)), sem((NZ, 3)), sem((NZ, 3)),
            sem((1,)), sem((1,)), sem((NZ - 1,)), sem((NZ - 1,)),
            sem((NZ + NY,)), sem((NY,)),
        ],
        compiler_params=pltpu.CompilerParams(
            collective_id=0, has_side_effects=True, vmem_limit_bytes=56 * 1024 * 1024
        ),
    )(
        key_vectors, queries, values, write_rates, log_decay, level_gates, out_weight,
        out_cotangent, final_cotangent,
    )
    whole = (mixed, dq, dk, dv, gw, fin)
    out = pl.pallas_call(
        finish_kernel,
        out_shape=[
            jax.ShapeDtypeStruct(part.shape, F32 if i else BF16) for i, part in enumerate(whole)
        ]
        + [
            jax.ShapeDtypeStruct((4, C), F32),
            jax.ShapeDtypeStruct((4, C), F32),
            jax.ShapeDtypeStruct((NL, 4, C), F32),
        ],
        in_specs=[vmem] * 7,
        out_specs=[vmem] * 9,
    )(*whole, dsmall)
    mixed, dq, dk, dv, gw, fin, d_rates, d_decay, d_gates = out
    return (mixed, dq, dk, dv, d_rates, d_decay, d_gates, gw, fin)


def solution(mesh):
    return jax.shard_map(
        on_device,
        mesh=mesh,
        in_specs=(
            P("ctx", "head"), P("ctx", "head"), P("ctx", "head"), P("head", "ctx"),
            P("head", "ctx"), P(None, "head", "ctx"), P("head", None), P("ctx", "head"),
            P("head", None, None),
        ),
        out_specs=(
            P("ctx", "head"), P("ctx", "head"), P("ctx", "head"), P("ctx", "head"),
            P("head", "ctx"), P("head", "ctx"), P(None, "head", "ctx"),
            P(("head", "ctx"), None), P("head", None, None),
        ),
        check_vma=False,
    )
```

```python
import functools

import jax
import jax.numpy as jnp
from jax import lax
from jax.experimental import pallas as pl
from jax.experimental.pallas import tpu as pltpu
from jax.sharding import PartitionSpec as P

F32 = jnp.float32
BF16 = jnp.bfloat16
C = 128
NZ, NY, NB, NL = 8, 4, 4, 8
MESH = pl.DeviceIdType.MESH


def split(x):
    high = x.astype(BF16)
    return high, (x - high.astype(F32)).astype(BF16)


SPLITS = {}


def split_once(x):
    if id(x) not in SPLITS:
        SPLITS[id(x)] = (x, split(x))
    return SPLITS[id(x)][1]


def dot(a, b, ca=1, cb=0, precision=None):
    return lax.dot_general(
        a, b, (((ca,), (cb,)), ((), ())), preferred_element_type=F32, precision=precision
    )


def mm(a, b, ca=1, cb=0):
    return mm_split(split_once(a), split_once(b), ca, cb)


def mm_split(a, b, ca=1, cb=0):
    (ah, al), (bh, bl) = a, b
    if bh.shape == (C, C):
        other = 1 - cb
        both = dot(
            jnp.concatenate([ah, al], axis=ca),
            jnp.concatenate(
                [
                    jnp.concatenate([bh, bl], axis=other),
                    jnp.concatenate([bl, bh], axis=other),
                ],
                axis=cb,
            ),
            ca, cb,
        )
        return both[:, :C] + both[:, C:]
    return dot(
        jnp.concatenate([ah, ah, al], axis=ca), jnp.concatenate([bh, bl, bh], axis=cb), ca, cb
    )


def iotas():
    return (
        lax.broadcasted_iota(jnp.int32, (C, C), 0),
        lax.broadcasted_iota(jnp.int32, (C, C), 1),
    )


def unit(x):
    scale = lax.rsqrt(jnp.sum(x * x, axis=1, keepdims=True) + 1e-6)
    return x * scale, scale


def unit_back(grad, vec, scale):
    return scale * (grad - vec * jnp.sum(vec * grad, axis=1, keepdims=True))


def token_terms(rows):
    row, col = iotas()
    upper = jnp.where(row <= col, 1.0, 0.0).astype(F32)
    cum = dot(rows, upper, precision=lax.Precision.HIGHEST)
    stacked = jnp.concatenate([rows, cum, jnp.zeros((C - 32, C), F32)], axis=0).T
    beta = stacked[:, 0:1]
    cum_col = stacked[:, 17:18]
    cum_row = cum[1:2, :]
    last = cum[1:2, C - 1 : C]
    decay = jnp.where(row >= col, jnp.exp(jnp.minimum(cum_col - cum_row, 0.0)), 0.0)
    return dict(
        beta=beta,
        gam=jnp.exp(cum_col),
        tail=jnp.exp(last - cum_col),
        glast=jnp.exp(last),
        shared={},
        gates=[stacked[:, 2 + i : 3 + i] for i in range(NL)],
        decay=decay,
    )


def inverses(lows):
    row, col = iotas()
    eye = jnp.where(row == col, 1.0, 0.0).astype(F32)
    ones = [jnp.where((row >> 3) == (col >> 3), -low, 0.0) for low in lows]
    twos = [mm(n, n) for n in ones]
    fours = [mm(n, n) for n in twos]
    invs = [eye + n + m + mm(n, m) for n, m in zip(ones, twos)]
    invs = [inv + mm(inv, m) for inv, m in zip(invs, fours)]
    for bit in (3, 5):
        here = ((row >> (bit + 2)) == (col >> (bit + 2))) & ((row >> bit) != (col >> bit))
        rests = [-mm(jnp.where(here, low, 0.0), inv) for low, inv in zip(lows, invs)]
        squares = [mm(rest, rest) for rest in rests]
        invs = [inv + mm(inv, rest) for inv, rest in zip(invs, rests)]
        invs = [inv + mm(inv, square) for inv, square in zip(invs, squares)]
    return invs


def gate_matrix(tt):
    row, col = iotas()
    return jnp.where((row >> 6) == (col >> 6), tt["gates"][0], tt["gates"][1])


def lockstep(runs):
    results = [None] * len(runs)
    alive = list(range(len(runs)))
    while alive:
        for i in list(alive):
            try:
                next(runs[i])
            except StopIteration as stop:
                results[i] = stop.value
                alive.remove(i)
    return results


def scaled(tt, name, keys=None, values=None):
    shared = tt["shared"]
    if name not in shared:
        if name == "kb":
            shared[name] = tt["beta"] * tt["gam"] * keys
        elif name == "vb":
            shared[name] = tt["beta"] * values
        elif name == "kt":
            shared[name] = tt["tail"] * keys
        else:
            shared[name] = gate_matrix(tt)
    return shared[name]


def chunk_states(keys, values, inv, tt):
    row, col = iotas()
    pair = mm(
        inv,
        jnp.concatenate([scaled(tt, "kb", keys), scaled(tt, "vb", values=values)], axis=1),
    )
    yield
    both = mm(scaled(tt, "kt", keys), pair, 0, 0)
    yield
    return dict(
        weights=pair[:, :C], plain=pair[:, C:], add=both[:, C:],
        map=jnp.where(row == col, tt["glast"], 0.0) - both[:, :C],
    )


def chunk_reads(keys, queries, values, inv, tt):
    scores = mm(queries, keys, 1, 1) * tt["decay"]
    yield
    mix = mm(scores, inv)
    yield
    reader = tt["gam"] * queries - mm(mix, scaled(tt, "kb"))
    yield
    gated = scaled(tt, "gate") * mix
    tt["shared"]["gated"] = gated
    near = mm(gated, scaled(tt, "vb"))
    yield
    return dict(scores=scores, mix=mix, reader=reader, near=near)


def near_back(hg, values, mix, tt):
    row, col = iotas()
    gate = scaled(tt, "gate")
    cross = mm(hg, scaled(tt, "vb"), 1, 1)
    yield
    d_vb = mm(scaled(tt, "gated"), hg, 0, 0)
    yield
    gated = cross * mix
    same = (row >> 6) == (col >> 6)
    d_g0 = jnp.sum(jnp.where(same, gated, 0.0), axis=1, keepdims=True)
    d_g1 = jnp.sum(jnp.where(same, 0.0, gated), axis=1, keepdims=True)
    return dict(d_g0=d_g0, d_g1=d_g1, dvb=d_vb, dmix=cross * gate)


def chunk_back_a(d_mix, d_reader, keys, queries, inv, scores, mix, tt, q_scale):
    gam, decay = tt["gam"], tt["decay"]
    row, col = iotas()
    d_mix = d_mix - mm(d_reader, scaled(tt, "kb"), 1, 1)
    yield
    d_kb = -mm(mix, d_reader, 0, 0)
    yield
    d_scores = jnp.where(row >= col, mm(d_mix, inv, 1, 1), 0.0)
    yield
    d_qk = d_scores * decay
    d_query = mm(d_qk, keys) + gam * d_reader
    yield
    d_low = mm(mix, d_scores, 0, 0)
    yield
    d_key = mm(d_qk, queries, 0, 0)
    yield
    cum = gam * jnp.sum(d_reader * queries, axis=1, keepdims=True)
    return dict(
        dkb=d_kb, dlow=d_low, dkey=d_key, gap=d_scores * scores, cum=cum,
        query=unit_back(d_query, queries, q_scale),
    )


def chunk_back_b(d_map, d_add, keys, inv, weights, plain, d_vb, d_kb, tt):
    grads = jnp.concatenate([d_add, -d_map], axis=1)
    d_pw = mm(scaled(tt, "kt"), grads)
    yield
    d_kt = mm(jnp.concatenate([plain, weights], axis=1), grads, 1, 1)
    yield
    back = mm(inv, d_pw, 0, 0)
    yield
    d_vb = d_vb + back[:, :C]
    return dict(dvb=d_vb, dkb=d_kb + back[:, C:], dkt=d_kt, back=back, value=tt["beta"] * d_vb)


def chunk_back_c(
    d_map, d_vb, d_kb, d_kt, back, d_low, d_key, gap, cum, gram, keys, values, weights, plain, tt,
    k_scale, gate_grads,
):
    beta, gam, tail, decay = tt["beta"], tt["gam"], tt["tail"], tt["decay"]
    row, col = iotas()
    d_low = d_low + mm(back, jnp.concatenate([plain, weights], axis=1), 1, 1)
    yield
    d_low = jnp.where(row > col, -d_low, 0.0) * decay
    d_gram = beta * d_low
    d_key = d_key + mm(d_gram + d_gram.T, keys) + beta * gam * d_kb + tail * d_kt
    yield
    dk_gram = d_low * gram
    d_gap = gap + beta * dk_gram
    kb_k = jnp.sum(d_kb * keys, axis=1, keepdims=True)
    d_beta = jnp.sum(dk_gram + d_vb * values, axis=1, keepdims=True) + gam * kb_k
    tail_part = tail * jnp.sum(d_kt * keys, axis=1, keepdims=True)
    d_cum = cum + gam * beta * kb_k - tail_part + jnp.sum(d_gap, axis=1, keepdims=True)
    d_last = jnp.sum(tail_part, axis=0, keepdims=True) + tt["glast"] * jnp.sum(
        jnp.sum(jnp.where(row == col, d_map, 0.0), axis=1, keepdims=True), axis=0, keepdims=True
    )
    lane = lax.broadcasted_iota(jnp.int32, (1, C), 1)
    d_cum_row = jnp.where(lane == C - 1, d_last, 0.0) - jnp.sum(d_gap, axis=0, keepdims=True)
    cols = jnp.where(col == 0, d_beta, 0.0) + jnp.where(col == 1, d_cum, 0.0)
    for i in range(NL):
        cols = cols + jnp.where(col == 2 + i, gate_grads[i], 0.0)
    rows = cols.T[:16, :]
    at = lax.broadcasted_iota(jnp.int32, (16, C), 0)
    rows = rows + jnp.where(at == 1, d_cum_row, 0.0)
    lower = jnp.where(row >= col, 1.0, 0.0).astype(F32)
    rows = jnp.where(at == 1, dot(rows, lower, precision=lax.Precision.HIGHEST), rows)
    return unit_back(d_key, keys, k_scale), rows


def chunk_chain(maps, adds):
    one = jnp.concatenate([maps[0], adds[0]], axis=1)
    two = mm(maps[1], one)
    run2 = two[:, C:] + adds[1]
    three = mm(maps[2], jnp.concatenate([two[:, :C], run2], axis=1))
    moved = three[:, C:]
    run3 = moved + adds[2]
    four = mm(maps[3], jnp.concatenate([three[:, :C], run3], axis=1))
    return [two[:, :C], three[:, :C], four[:, :C]], run2, moved, run3, four[:, C:] + adds[3]


def chain_back(d_total, d_run4, maps, add0, pre2, pre3, run2, run3, lift_grads, near):
    pair = jnp.concatenate([d_total, d_run4], axis=1)
    d_map3 = mm(pair, jnp.concatenate([pre3, run3], axis=1), 1, 1)
    d_add3 = d_run4
    down = mm(maps[3], pair, 0, 0)
    d_pre3 = down[:, :C] + lift_grads[2]
    d_run3 = down[:, C:]
    d_add2 = d_run3 + near["add2"]
    pair = jnp.concatenate([d_pre3, d_run3 + near["moved"]], axis=1)
    d_map2 = mm(pair, jnp.concatenate([pre2, run2], axis=1), 1, 1)
    down = mm(maps[2], pair, 0, 0)
    d_pre2 = down[:, :C] + lift_grads[1]
    d_run2 = down[:, C:] + near["run2"]
    pair = jnp.concatenate([d_pre2, d_run2], axis=1)
    d_map1 = mm(pair, jnp.concatenate([maps[0], add0], axis=1), 1, 1)
    down = mm(maps[1], pair, 0, 0)
    d_map0 = down[:, :C] + lift_grads[0]
    d_add0 = down[:, C:] + near["add0"]
    return [d_map0, d_map1, d_map2, d_map3], [d_add0, d_run2, d_add2, d_add3]


def kernel(
    k_ref, q_ref, v_ref, rate_ref, decay_ref, gate_ref, w_ref, cot_ref, fcot_ref,
    mixed_ref, dq_ref, dk_ref, dv_ref, dsmall_ref, gw_ref, fin_ref,
    kin, qin, vin, sin, spack, hgin, cot, hg, hl, hlout, gout, sout, wbuf, fcbuf,
    own, peer, mz, az, zst, dxo, dxp, dsc, dsz, lam,
    cotz, gpart, gpeer, gsum, zsend, zrecv, mown, mpart, mrecv,
    in_send, in_recv, out_send, out_recv, x_send, x_recv, loc, core_send, core_recv,
    zf_send, zf_recv, rel_send, rel_recv, zb_send, zb_recv, relb_send, relb_recv,
    gp_send, gp_recv, gz_send, gz_recv, f_send, f_recv,
):
    SPLITS.clear()
    me = lax.axis_index("ctx")
    x = lax.axis_index("head")
    z, y, c = me // 8, (me // 2) % 4, me % 2
    pending = []

    def flush(count):
        for finish in pending[:count]:
            finish()
        del pending[:count]


    def at(zz, yy, cc):
        return {"ctx": (zz * 4 + yy) * 2 + cc}

    def remote(src, dst, send, recv, target):
        return pltpu.make_async_remote_copy(
            src_ref=src, dst_ref=dst, send_sem=send, recv_sem=recv,
            device_id=target, device_id_type=MESH,
        )

    def put(src, dst, send, recv, target, here=None, when=None):
        copy = remote(src, dst, send, recv, target)
        cond = when
        if here is not None:
            cond = jnp.logical_not(here)

            @pl.when(here)
            def _():
                pltpu.make_async_copy(src, dst, recv).start()

        if cond is None:
            copy.start()
            pending.append(copy.wait_send)
        else:

            @pl.when(cond)
            def _():
                copy.start()

            def finish():
                @pl.when(cond)
                def _():
                    copy.wait_send()

            pending.append(finish)

    def got(dst, sem):
        pltpu.make_async_copy(dst, dst, sem).wait()

    def head_cols(i):
        return pl.ds(pl.multiple_of(i * C, C), C)

    local_w = pltpu.make_async_copy(w_ref, wbuf, loc.at[1])
    local_w.start()
    local_fc = pltpu.make_async_copy(fcot_ref.at[y], fcbuf, loc.at[2])
    local_fc.start()
    for h in range(NY):
        one = slice(h, h + 1)
        spack[h] = jnp.concatenate(
            [rate_ref[one], decay_ref[one]]
            + [gate_ref[i, one] for i in range(NL)]
            + [jnp.zeros((6, C), F32)],
            axis=0,
        )

    barrier = pltpu.get_barrier_semaphore()
    for dy in range(NY):
        for dc in range(2):
            if dy or dc:
                pl.semaphore_signal(
                    barrier, inc=1, device_id=at(z, (y + dy) % NY, (c + dc) % 2), device_id_type=MESH
                )
    for dz in range(1, NZ):
        pl.semaphore_signal(barrier, inc=1, device_id=at((z + dz) % NZ, y, c), device_id_type=MESH)
    for dx in range(1, 4):
        pl.semaphore_signal(barrier, inc=1, device_id={"head": (x + dx) % 4}, device_id_type=MESH)
    rows_from = at((z % 2) * 4 + y, z // 2, c)
    rows_to = at(2 * y + z // 4, z % 4, c)
    rows_stay = rows_to["ctx"] == me

    @pl.when(jnp.logical_not(rows_stay))
    def _():
        pl.semaphore_signal(barrier, inc=1, device_id=rows_from, device_id_type=MESH)

    pl.semaphore_wait(barrier, jnp.where(rows_stay, 17, 18))

    slot = (y % 2) * 2 + c
    half = y // 2

    def spread(idx, src_of, dst):
        for d in range(NY):
            h = (y + d) % NY
            put(
                src_of(h), dst(slot), in_send.at[idx, d], in_recv.at[idx, slot],
                at(z, h, half), here=(c == half) if d == 0 else None,
            )

    def spread_got(idx, dst):
        for b in range(NB):
            got(dst(b), in_recv.at[idx, b])

    cot_cols = pl.ds(pl.multiple_of(x * 512, 512), 512)
    kin_at, qin_at, vin_at = (lambda b: kin.at[b]), (lambda b: qin.at[b]), (lambda b: vin.at[b])
    sin_at, hgin_at = (lambda b: sin.at[b]), (lambda b: hgin.at[b])

    def cotz_at(b):
        return cotz.at[b, x, :, :256]

    def cotz_rest(b):
        return cotz.at[b, :, :, 256:]

    def gather_back(idx, src, dst_of):
        for b in range(NB):
            ty, tc = 2 * c + b // 2, b % 2
            put(
                src.at[b], dst_of(y), out_send.at[idx, b], out_recv.at[idx, y],
                at(z, ty, tc), here=(ty == y) & (tc == c),
            )

    def gather_got(idx, dst_of):
        for h in range(NY):
            got(dst_of(h), out_recv.at[idx, h])

    spread(1, lambda h: spack.at[h], sin_at)
    spread(0, lambda h: k_ref.at[:, head_cols(h)], kin_at)
    for d in range(1, 4):
        put(
            cot_ref, cot.at[x], x_send.at[0, d - 1], x_recv.at[0, d - 1], {"head": (x + d) % 4},
        )
    local_cot = pltpu.make_async_copy(cot_ref, cot.at[x], loc.at[0])
    local_cot.start()

    held = {}

    def load(name, b):
        return held[name, b]

    def store(name, b, value):
        held[name, b] = value

    row, col = iotas()
    blocks = range(NB)

    spread_got(1, sin_at)
    terms = [token_terms(sin[b]) for b in blocks]
    spread_got(0, kin_at)
    spread(3, lambda h: v_ref.at[:, head_cols(h)], vin_at)
    spread(2, lambda h: q_ref.at[:, head_cols(h)], qin_at)
    lows, k_scales = [], []
    for b in blocks:
        keys, scale = unit(kin[b])
        k_scales.append(scale)
        store("keys", b, keys)
        gram = mm(keys, keys, 1, 1)
        store("gram", b, gram)
        lows.append(jnp.where(row > col, terms[b]["beta"] * terms[b]["decay"] * gram, 0.0))
    for b, inv in enumerate(inverses(lows)):
        store("inv", b, inv)

    spread_got(3, vin_at)
    outs = lockstep([chunk_states(load("keys", b), vin[b], load("inv", b), terms[b]) for b in blocks])
    for b in blocks:
        for name in outs[b]:
            store(name, b, outs[b][name])
    maps = [load("map", b) for b in blocks]
    adds = [load("add", b) for b in blocks]
    pres, run2, moved, run3, run4 = chunk_chain(maps, adds)
    own[0] = pres[2]
    own[1] = run4
    other = at(z, y, 1 - c)
    put(own, peer, core_send.at[0], core_recv.at[0], other)

    local_cot.wait()
    for d in range(1, 4):
        got(cot.at[(x + 4 - d) % 4], x_recv.at[0, d - 1])
    local_w.wait()
    total = dot(cot[0], wbuf[:, :512], 1, 1)
    for i in range(1, 4):
        total = total + dot(cot[i], wbuf[:, 512 * i : 512 * i + 512], 1, 1)
    hg[...] = total
    spread(4, lambda h: hg.at[:, head_cols(h)], hgin_at)
    sent_early = len(pending)
    spread(5, lambda h: cot_ref.at[:, :256], cotz_at)
    spread(6, lambda h: cot.at[:, :, 256:], cotz_rest)

    got(peer, core_recv.at[0])
    first = c == 0
    lo_map = jnp.where(first, own[0], peer[0])
    lo_add = jnp.where(first, own[1], peer[1])
    hi_map = jnp.where(first, peer[0], own[0])
    hi_add = jnp.where(first, peer[1], own[1])
    both = mm(hi_map, jnp.concatenate([lo_map, lo_add], axis=1))
    chip_map, chip_add = both[:, :C], both[:, C:] + hi_add
    high = chip_map.astype(BF16)
    rest = jnp.sum(
        jnp.where(row == col, chip_map - high.astype(F32), 0.0), axis=0, keepdims=True
    )
    mz[z, :C] = high
    mz[z, C:] = jnp.broadcast_to(rest, (16, C)).astype(BF16)
    az[z] = chip_add.T.astype(BF16)
    second = c == 1
    for d in range(NZ - 1, 0, -1):
        tz = z + d
        up = tz < NZ
        put(mz.at[z], mz.at[z], zf_send.at[d], zf_recv.at[z], at(tz % NZ, y, c), when=up & first)
        put(az.at[z], az.at[z], zf_send.at[NZ + d], zf_recv.at[z], at(tz % NZ, y, c), when=up & second)
    for d in range(1, NZ):
        tz = z - d
        put(
            mz.at[z], mz.at[z], zf_send.at[2 * NZ + d], zf_recv.at[z], at((tz + NZ) % NZ, y, c),
            when=(tz >= 0) & first,
        )

    spread_got(5, cotz_at)
    for d in range(1, 4):
        put(
            cotz.at[:, x, :, :256], cotz.at[:, x, :, :256], x_send.at[2, d - 1],
            x_recv.at[2, d - 1], {"head": (x + d) % 4},
        )

    spread_got(2, qin_at)
    q_scales = []
    for b in blocks:
        queries, scale = unit(qin[b])
        q_scales.append(scale)
        store("queries", b, queries)
    outs = lockstep(
        [
            chunk_reads(load("keys", b), load("queries", b), vin[b], load("inv", b), terms[b])
            for b in blocks
        ]
    )
    for b in blocks:
        for name in outs[b]:
            store(name, b, outs[b][name])
    store("lift", 0, load("reader", 0))
    for b in (1, 2, 3):
        store("lift", b, mm(load("reader", b), maps[0] if b == 1 else pres[b - 2]))

    spread_got(4, hgin_at)
    d_states = jnp.zeros((4 * C, C), F32)
    for b in blocks:
        turned = hgin[b].T
        weighted = jnp.concatenate(
            [turned * sin[b, 6 + i : 7 + i] for i in range(4)], axis=0
        )
        d_states = d_states + mm(weighted, load("lift", b))
    dxo[...] = d_states
    put(dxo, dxp, core_send.at[1], core_recv.at[1], other)

    for b, state, gate in ((1, adds[0], 2), (2, run2, 3), (3, adds[2], 2), (3, moved, 3)):
        store(
            "near", b,
            load("near", b) + terms[b]["gates"][gate] * mm(load("reader", b), state),
        )

    bits = [(z // (1 << b)) % 2 == 1 for b in range(3)]
    starts = [(z // (2 << b)) * (2 << b) for b in range(3)]
    got(dxp, core_recv.at[1])
    lo_dx = jnp.where(first, dxo[...], dxp[...])
    hi_dx = jnp.where(first, dxp[...], dxo[...])
    d_chip = lo_dx[C:] + mm(hi_dx[C:], lo_map)
    for b in range(3):
        dsc[b] = d_chip[b * C : (b + 1) * C].astype(BF16)
    rows_mine = pl.ds(pl.multiple_of(c * 64, 64), 64)
    rows_other = pl.ds(pl.multiple_of((1 - c) * 64, 64), 64)
    for b in (2, 1, 0):
        for d in range((2 << b) - 1, 0, -1):
            tz = z - d
            put(
                dsc.at[b, rows_mine], dsz.at[z, b, rows_mine], zb_send.at[b, d],
                zb_recv.at[z, b], at((tz + NZ) % NZ, y, c), when=bits[b] & (tz >= starts[b]),
            )

    outs = lockstep([near_back(hgin[b], vin[b], load("mix", b), terms[b]) for b in blocks])
    gate_grads = []
    for b in blocks:
        store("dvb", b, outs[b]["dvb"])
        store("dmix", b, outs[b]["dmix"])
        gate_grads.append([outs[b]["d_g0"], outs[b]["d_g1"]] + [jnp.zeros((C, 1), F32)] * 6)
    near_reads = [jnp.zeros((C, C), F32)] * NB
    near_cots = {}
    for b, state, gate, name in (
        (1, adds[0], 2, "add0"), (2, run2, 3, "run2"), (3, adds[2], 2, "add2"), (3, moved, 3, "moved"),
    ):
        weight = terms[b]["gates"][gate]
        part = mm(hgin[b], state, 1, 1)
        reader = load("reader", b)
        gate_grads[b][gate] = jnp.sum(part * reader, axis=1, keepdims=True)
        near_reads[b] = near_reads[b] + weight * part
        near_cots[name] = mm(reader, weight * hgin[b], 0, 0)
    for b in blocks:
        store("dread", b, near_reads[b])
    flush(sent_early)

    for j in range(NZ - 1):

        @pl.when((j < z) & first)
        def _():
            got(mz.at[j], zf_recv.at[j])

        @pl.when((j < z) & second)
        def _():
            got(az.at[j], zf_recv.at[j])

        put(mz.at[j], mz.at[j], rel_send.at[j], rel_recv.at[j], other, when=(j < z) & first)
        put(az.at[j], az.at[j], rel_send.at[NZ + j], rel_recv.at[j], other, when=(j < z) & second)

    zst[...] = jnp.zeros_like(zst)

    def step(j, carry):
        @pl.when(first)
        def _():
            got(az.at[j], rel_recv.at[j])

        @pl.when(second)
        def _():
            got(mz.at[j], rel_recv.at[j])

        now = zst[...]
        high = mz[j, :C]
        new = dot(
            jnp.concatenate(split(now), axis=1), jnp.concatenate([high, high], axis=1), 1, 1
        ) + now * mz[j, C:].astype(F32)[:1]
        add = az[j].astype(F32)
        for b in range(3):
            inside = (j >= starts[b]) & (j < starts[b] + (1 << b))
            zst[b * C : (b + 1) * C] = new[b * C : (b + 1) * C] + jnp.where(inside, add, 0.0)
        return carry

    lax.fori_loop(0, z, step, 0)
    reads = [jnp.where(bits[b], zst[b * C : (b + 1) * C], 0.0) for b in range(3)]
    chip_states = jnp.concatenate(reads, axis=0)
    run_chip = reads[0] + reads[1] + reads[2]

    lower = mm(chip_states, lo_map, 1, 1)
    states = jnp.concatenate(
        [jnp.where(first, 0.0, lo_add.T), jnp.where(first, chip_states, lower)], axis=0
    )
    for b in blocks:
        reads_b = mm(load("lift", b), states, 1, 1)
        total = load("near", b)
        for i in range(4):
            total = total + terms[b]["gates"][4 + i] * reads_b[:, i * C : (i + 1) * C]
        hlout[b] = total.astype(BF16)
    gather_back(0, hlout, lambda h: hl.at[:, head_cols(h)])

    last = z == NZ - 1

    @pl.when(last)
    def _():
        fin_ref[y] = mm_split(split(run_chip), split(chip_map), 1, 1).T + chip_add

    for d in range(1, NZ):
        put(
            fin_ref.at[y], fin_ref.at[y], f_send.at[d], f_recv.at[0],
            at(NZ - 1 - d, y, c), when=last,
        )

    prefixes = [None, maps[0], pres[0], pres[1]]
    state_cols = jnp.concatenate([states[i * C : (i + 1) * C] for i in range(4)], axis=1)
    lift_grads = []
    backs = [mm(hgin[b], state_cols) for b in blocks]
    for b in blocks:
        lift = load("lift", b)
        d_lift = jnp.zeros((C, C), F32)
        for i in range(4):
            part = backs[b][:, i * C : (i + 1) * C]
            gate_grads[b][4 + i] = jnp.sum(part * lift, axis=1, keepdims=True)
            d_lift = d_lift + terms[b]["gates"][4 + i] * part
        if b:
            store("dread", b, load("dread", b) + mm(d_lift, prefixes[b], 1, 1))
            lift_grads.append(mm(load("reader", b), d_lift, 0, 0))
        else:
            store("dread", b, d_lift)

    for i in range(NZ - 1, 0, -1):
        for b in range(3):
            if not (i >> b) & 1:
                continue
            wanted = (z < i) & (z // (2 << b) == i // (2 << b))

            @pl.when(wanted)
            def _():
                got(dsz.at[i, b, rows_mine], zb_recv.at[i, b])

            put(
                dsz.at[i, b, rows_mine], dsz.at[i, b, rows_mine], relb_send.at[i, b],
                relb_recv.at[i, b], other, when=wanted,
            )

    for i in range(1, NZ):

        @pl.when((i > z) & first)
        def _():
            got(mz.at[i], zf_recv.at[i])

        put(mz.at[i], mz.at[i], rel_send.at[2 * NZ + i], rel_recv.at[i], other, when=(i > z) & first)

        @pl.when((i > z) & second)
        def _():
            got(mz.at[i], rel_recv.at[i])

    sent_early = len(pending)

    spread_got(6, cotz_rest)
    for d in range(1, 4):
        got(cotz.at[:, (x + 4 - d) % 4, :, :256], x_recv.at[2, d - 1])

    def weight_rows(i, carry):
        cols = pl.ds(pl.multiple_of(i * 512, 512), 512)
        part = dot(hlout[...].reshape(512, C), cotz[:, i].reshape(512, 512), 0, 0)
        gpart[:, :, :, cols] = part.reshape(NZ, 2, 8, 512)
        return carry

    lax.fori_loop(0, 4, weight_rows, 0)
    put(gpart.at[:, 1 - c], gpeer, core_send.at[2], core_recv.at[2], other)

    gather_got(0, lambda h: hl.at[:, head_cols(h)])
    for d in range(1, 4):
        tx = (x + d) % 4
        mpart[d - 1] = dot(
            hl[...], wbuf[:, pl.ds(pl.multiple_of(tx * 512, 512), 512)]
        ).astype(BF16)
        put(
            mpart.at[d - 1], mrecv.at[d - 1], x_send.at[1, d - 1], x_recv.at[1, d - 1],
            {"head": tx},
        )
    mown[...] = dot(hl[...], wbuf[:, cot_cols])

    got(gpeer, core_recv.at[2])

    def chip_rows(i, carry):
        part = gpart[i, c] + gpeer[i]
        zsend[i] = jnp.concatenate([part[:, :1024], part[:, 1024:]], axis=0).astype(BF16)
        return carry

    lax.fori_loop(0, NZ, chip_rows, 0)
    for d in range(NZ - 1, 0, -1):
        tz = (z + d) % NZ
        put(zsend.at[tz], zrecv.at[d - 1], gz_send.at[d - 1], gz_recv.at[d - 1], at(tz, y, c))

    outs = lockstep(
        [
            chunk_back_a(
                load("dmix", b), load("dread", b), load("keys", b), load("queries", b),
                load("inv", b), load("scores", b), load("mix", b), terms[b], q_scales[b],
            )
            for b in blocks
        ]
    )
    cums = [outs[b]["cum"] for b in blocks]
    for b in blocks:
        gout[0, b] = outs[b]["query"].astype(BF16)
        for name in ("dkb", "dlow", "dkey", "gap"):
            store(name, b, outs[b][name])
    targets = (dq_ref, dk_ref, dv_ref)

    def send_back(i):
        gather_back(1 + i, gout.at[i], lambda h: targets[i].at[:, head_cols(h)])

    send_back(0)

    lam[...] = jnp.zeros_like(lam)
    local_fc.wait()
    lam[3 * C :] = fcbuf[...].T
    for i in range(NZ - 1, 0, -1):

        @pl.when(i > z)
        def _():
            now = lam[...]
            high = mz[i, :C]
            lam[...] = dot(
                jnp.concatenate(split(now), axis=1), jnp.concatenate([high, high], axis=0)
            ) + now * mz[i, C:].astype(F32)[:1]

        for b in range(3):
            if not (i >> b) & 1:
                continue

            @pl.when((z < i) & (z // (2 << b) == i // (2 << b)))
            def _():
                got(dsz.at[i, b, rows_other], relb_recv.at[i, b])
                lam[b * C : (b + 1) * C] += dsz[i, b].astype(F32)

    d_chip_map = mm(lam[...], jnp.concatenate([zst[...], run_chip], axis=0), 0, 0)
    d_chip_add = lam[3 * C :]
    for b in range(3):
        d_chip_add = d_chip_add + jnp.where(bits[b], 0.0, lam[b * C : (b + 1) * C])
    d_chip_add = d_chip_add.T
    chip_pair = jnp.concatenate([d_chip_map, d_chip_add], axis=1)
    as_second = mm(chip_pair, jnp.concatenate([lo_map, lo_add], axis=1), 1, 1)
    through = mm(hi_map, chip_pair, 0, 0)
    as_first = through[:, :C] + mm(hi_dx[C:], chip_states, 0, 0)
    d_total = jnp.where(first, as_first, as_second)
    d_run4 = jnp.where(first, through[:, C:] + hi_dx[:C].T, d_chip_add)
    d_maps, d_adds = chain_back(
        d_total, d_run4, maps, adds[0], pres[0], pres[1], run2, run3, lift_grads, near_cots
    )

    @pl.when(jnp.logical_not(last))
    def _():
        got(fin_ref.at[y], f_recv.at[0])

    for d in range(1, NY):
        ty = (y + d) % NY
        put(fin_ref.at[y], fin_ref.at[y], f_send.at[NZ + d], f_recv.at[d], at(z, ty, c))

    flush(sent_early)
    pairs = lockstep(
        [
            chunk_back_b(
                d_maps[b], d_adds[b], load("keys", b), load("inv", b), load("weights", b),
                load("plain", b), load("dvb", b), load("dkb", b), terms[b],
            )
            for b in blocks
        ]
    )
    for b in blocks:
        gout[2, b] = pairs[b]["value"].astype(BF16)
    send_back(2)

    total = zsend[z].astype(F32)
    for d in range(1, NZ):
        got(zrecv.at[d - 1], gz_recv.at[d - 1])
        total = total + zrecv[d - 1].astype(F32)
    gsum[...] = jnp.concatenate([total[:8], total[8:]], axis=1)
    put(gsum, gw_ref, gp_send.at[0], gp_recv.at[0], rows_to, here=rows_stay)

    outs = lockstep(
        [
            chunk_back_c(
                d_maps[b], pairs[b]["dvb"], pairs[b]["dkb"], pairs[b]["dkt"], pairs[b]["back"],
                load("dlow", b), load("dkey", b), load("gap", b), cums[b], load("gram", b),
                load("keys", b), vin[b], load("weights", b), load("plain", b), terms[b],
                k_scales[b], gate_grads[b],
            )
            for b in blocks
        ]
    )
    for b in blocks:
        gout[1, b] = outs[b][0].astype(BF16)
        sout[b] = outs[b][1]
    send_back(1)
    gather_back(4, sout, lambda h: dsmall_ref.at[h])

    total = mown[...]
    for d in range(1, 4):
        got(mrecv.at[d - 1], x_recv.at[1, d - 1])
    for d in range(3):
        total = total + mrecv[d].astype(F32)
    mixed_ref[...] = total.astype(BF16)
    got(gw_ref, gp_recv.at[0])

    for d in range(1, NY):
        sy = (y + NY - d) % NY
        got(fin_ref.at[sy], f_recv.at[d])
    for i in range(3):
        gather_got(1 + i, lambda h, i=i: targets[i].at[:, head_cols(h)])
    gather_got(4, lambda h: dsmall_ref.at[h])
    flush(len(pending))


def finish_kernel(*refs):
    ins, small_ref = refs[:6], refs[6]
    outs, (rate_ref, decay_ref, gate_ref) = refs[7:13], refs[13:16]
    for i in range(6):
        outs[i][...] = ins[i][...].astype(outs[i].dtype)
    for h in range(NY):
        one = slice(h, h + 1)
        rate_ref[one] = small_ref[h, 0:1]
        decay_ref[one] = small_ref[h, 1:2]
        for i in range(NL):
            gate_ref[i, one] = small_ref[h, 2 + i : 3 + i]


def on_device(
    queries, key_vectors, values, write_rates, log_decay, level_gates, out_weight,
    out_cotangent, final_cotangent,
):
    vmem = pl.BlockSpec(memory_space=pltpu.VMEM)
    anywhere = pl.BlockSpec(memory_space=pl.ANY)
    sem = pltpu.SemaphoreType.DMA
    quad = pltpu.VMEM((NB, C, C), F32)
    mixed, dq, dk, dv, dsmall, gw, fin = pl.pallas_call(
        kernel,
        out_shape=[
            jax.ShapeDtypeStruct((C, 512), BF16),
            jax.ShapeDtypeStruct((C, 512), BF16),
            jax.ShapeDtypeStruct((C, 512), BF16),
            jax.ShapeDtypeStruct((C, 512), BF16),
            jax.ShapeDtypeStruct((4, 16, C), F32),
            jax.ShapeDtypeStruct((8, 2048), F32),
            jax.ShapeDtypeStruct((4, C, C), F32),
        ],
        in_specs=[anywhere] * 3 + [vmem] * 3 + [anywhere] * 3,
        out_specs=[vmem] + [anywhere] * 4 + [vmem] * 2,
        scratch_shapes=[
            quad, quad, quad, pltpu.VMEM((NB, 16, C), F32), pltpu.VMEM((NY, 16, C), F32), quad,
            pltpu.VMEM((4, C, 512), BF16),
            pltpu.VMEM((C, 512), F32),
            pltpu.VMEM((C, 512), BF16),
            pltpu.VMEM((NB, C, C), BF16),
            pltpu.VMEM((3, NB, C, C), BF16),
            pltpu.VMEM((NB, 16, C), F32),
            pltpu.VMEM((512, 2048), BF16),
            pltpu.VMEM((C, C), F32),
            pltpu.VMEM((2, C, C), F32),
            pltpu.VMEM((2, C, C), F32),
            pltpu.VMEM((NZ, C + 16, C), BF16),
            pltpu.VMEM((NZ, C, C), BF16),
            pltpu.VMEM((3 * C, C), F32),
            pltpu.VMEM((4 * C, C), F32),
            pltpu.VMEM((4 * C, C), F32),
            pltpu.VMEM((3, C, C), BF16),
            pltpu.VMEM((NZ, 3, C, C), BF16),
            pltpu.VMEM((4 * C, C), F32),
            pltpu.VMEM((NB, 4, C, 512), BF16),
            pltpu.VMEM((NZ, 2, 8, 2048), F32),
            pltpu.VMEM((NZ, 8, 2048), F32),
            pltpu.VMEM((8, 2048), F32),
            pltpu.VMEM((NZ, 16, 1024), BF16),
            pltpu.VMEM((NZ - 1, 16, 1024), BF16),
            pltpu.VMEM((C, 512), F32),
            pltpu.VMEM((3, C, 512), BF16),
            pltpu.VMEM((3, C, 512), BF16),
            sem((7, 4)), sem((7, 4)), sem((5, 4)), sem((5, 4)),
            sem((3, 3)), sem((3, 3)), sem((3,)), sem((3,)), sem((3,)),
            sem((3 * NZ,)), sem((NZ,)), sem((3 * NZ,)), sem((NZ,)),
            sem((3, NZ)), sem((NZ, 3)), sem((NZ, 3)), sem((NZ, 3)),
            sem((1,)), sem((1,)), sem((NZ - 1,)), sem((NZ - 1,)),
            sem((NZ + NY,)), sem((NY,)),
        ],
        compiler_params=pltpu.CompilerParams(
            collective_id=0, has_side_effects=True, vmem_limit_bytes=56 * 1024 * 1024
        ),
    )(
        key_vectors, queries, values, write_rates, log_decay, level_gates, out_weight,
        out_cotangent, final_cotangent,
    )
    whole = (mixed, dq, dk, dv, gw, fin)
    out = pl.pallas_call(
        finish_kernel,
        out_shape=[
            jax.ShapeDtypeStruct(part.shape, F32 if i else BF16) for i, part in enumerate(whole)
        ]
        + [
            jax.ShapeDtypeStruct((4, C), F32),
            jax.ShapeDtypeStruct((4, C), F32),
            jax.ShapeDtypeStruct((NL, 4, C), F32),
        ],
        in_specs=[vmem] * 7,
        out_specs=[vmem] * 9,
    )(*whole, dsmall)
    mixed, dq, dk, dv, gw, fin, d_rates, d_decay, d_gates = out
    return (mixed, dq, dk, dv, d_rates, d_decay, d_gates, gw, fin)


def solution(mesh):
    return jax.shard_map(
        on_device,
        mesh=mesh,
        in_specs=(
            P("ctx", "head"), P("ctx", "head"), P("ctx", "head"), P("head", "ctx"),
            P("head", "ctx"), P(None, "head", "ctx"), P("head", None), P("ctx", "head"),
            P("head", None, None),
        ),
        out_specs=(
            P("ctx", "head"), P("ctx", "head"), P("ctx", "head"), P("ctx", "head"),
            P("head", "ctx"), P("head", "ctx"), P(None, "head", "ctx"),
            P(("head", "ctx"), None), P("head", None, None),
        ),
        check_vma=False,
    )
```
